32 devices in a mesh: batch: 8 (over z, x), zero: 4 (over y, core).
Axes of the slice: x: 2, y: 2, z: 4, core: 2. Of those that a mesh axis runs over, the one named last changes fastest.
Arguments:
- inputs: bfloat16 [64, 512, 768], P(('batch', 'zero')), may hold values from -6 to 6
- lengths: int32 [64], P(('batch', 'zero')), may hold values from 8 to 512
- exits: int32 [64], P(('batch', 'zero')), may hold values from 1 to 12
- routes: int32 [64], P(('batch', 'zero')), may hold values from 0 to 63, as said below
- attn_weight: bfloat16 [768, 2304], P(('batch', 'zero')), may hold values from -0.21875 to 0.21875
- merge_weight: bfloat16 [768, 768], P(('batch', 'zero')), may hold values from -0.625 to 0.625
- up_weight: bfloat16 [768, 3072], P(('batch', 'zero')), may hold values from -0.21875 to 0.21875
- down_weight: bfloat16 [3072, 768], P(('batch', 'zero')), may hold values from -0.15625 to 0.15625
- layer_biases: bfloat16 [6, 768], P(None, ('batch', 'zero')), may hold values from -3 to 3
- norm_gains: bfloat16 [2, 768], P(None, ('batch', 'zero')), may hold values from 0.5 to 1.5
- unit_bias: bfloat16 [3072], P(('batch', 'zero')), may hold values from -3 to 3
- proj_weight: bfloat16 [768, 128], replicated, may hold values from -0.21875 to 0.21875
- pool_weight: float32 [3, 128, 128], replicated, may hold values from -0.5 to 0.5
- dense_weight: float32 [128, 128], replicated, may hold values from -0.5 to 0.5
- label_weight: float32 [128, 14], replicated, may hold values from -0.5 to 0.5
- student_biases: float32 [2, 128], replicated, may hold values from -3 to 3
- logit_bias: float32 [14], replicated, may hold values from -3 to 3
- grad_act: bfloat16 [64, 512, 768], P(('batch', 'zero')), may hold values from -6 to 6
- grad_logits: float32 [64, 14], P(('batch', 'zero')), may hold values from -6 to 6
Outputs:
- repacked: bfloat16 [64, 512, 768], P(('batch', 'zero'))
- logits: float32 [64, 14], P(('batch', 'zero'))
- grad_inputs: float32 [64, 512, 768], P(('batch', 'zero'))
- attn_grad: float32 [768, 2304], P(('batch', 'zero'))
- merge_grad: float32 [768, 768], P(('batch', 'zero'))
- up_grad: float32 [768, 3072], P(('batch', 'zero'))
- down_grad: float32 [3072, 768], P(('batch', 'zero'))
- biases_grad: float32 [6, 768], P(None, ('batch', 'zero'))
- gains_grad: float32 [2, 768], P(None, ('batch', 'zero'))
- unit_grad: float32 [3072], P(('batch', 'zero'))
- proj_grad: float32 [768, 128], replicated
- pool_grad: float32 [3, 128, 128], replicated
- dense_grad: float32 [128, 128], replicated
- label_grad: float32 [128, 14], replicated
- student_grad: float32 [2, 128], replicated
- logit_grad: float32 [14], replicated
The draws below stay inside these ranges and needn't reach their ends.
Inputs may be any that keep to these rules, and one draw needn't show every extreme that they name: `routes`: slots are numbered device by device, batch index slowest, then zero index, then the 2 local slots. A slot at batch index b, zero index z and local index k is routed to batch index (b + o[z, k]) mod 8, the same zero index z, and local index m[z, k]. For each z, m[z, :] is a permutation of the local indices and each o[z, k] lies in 1 to 7; one o[z, k] of each z equals 7.
All inputs are finite; a program needn't handle non-finite values.
Results may differ from the reference program's by a relative error of at most 0.014.
Values may be sent and summed in bfloat16 or wider, within the bound.
A program may use at most 192 MiB of HBM per device.

```python
import math
import jax
import jax.numpy as jnp
from jax import lax

D = 768
HEADS = 12
HD = 64
FF = 3072
L = 512
SD = 128
SH = 2
CLASSES = 14
DEPTH = 12
LAYER = 4
SLOT_DEV = 2
SLOTS = 64
N_BATCH = 8
N_ZERO = 4


def draw_routes(key, part):
    key = jax.random.fold_in(key, 7)
    offset_key, pick_key, local_key = jax.random.split(key, 3)
    offsets = jax.random.randint(offset_key, (N_ZERO, SLOT_DEV), 1, N_BATCH)
    picked = jax.random.randint(pick_key, (N_ZERO, 1), 0, SLOT_DEV)
    offsets = jnp.where(jnp.arange(SLOT_DEV)[None, :] == picked, N_BATCH - 1, offsets)
    local_order = jax.vmap(lambda subkey: jax.random.permutation(subkey, SLOT_DEV))(jax.random.split(local_key, N_ZERO))
    batch_index = jnp.arange(N_BATCH)[:, None, None]
    zero_index = jnp.arange(N_ZERO)[None, :, None]
    target_batch = (batch_index + offsets[None, :, :]) % N_BATCH
    target_local = local_order[None, :, :]
    target = (target_batch * N_ZERO + zero_index) * SLOT_DEV + target_local
    return target.reshape(-1).astype(jnp.int32)


def with_ends(array, key, smallest, top_value):
    longest = array.shape.index(max(array.shape))
    spots = []
    for shift in (0, 1):
        where = [jax.random.randint(jax.random.fold_in(key, axis), (), 0, length) for axis, length in enumerate(array.shape)]
        where[longest] = (where[longest] + shift) % array.shape[longest]
        spots.append(tuple(where))
    return array.at[spots[0]].set(smallest).at[spots[1]].set(top_value)


def steps_of(own_key, dims, cuts, low, largest):
    def one(position, shards_of):
        heights = jax.random.uniform(jax.random.fold_in(jax.random.fold_in(own_key, 6), position), (shards_of,), jnp.float32, low / len(cuts), largest / len(cuts))
        return jnp.repeat(jnp.exp(heights), dims[position] // shards_of).reshape((-1,) + (1,) * (len(dims) - position - 1))

    gain = one(*cuts[0])
    for cut in cuts[1:]:
        gain = gain * one(*cut)
    return gain


def gaussian(rng, shape, scale, reach, pieces=(), held_as=jnp.bfloat16):
    drawn = jax.random.normal(rng, shape, jnp.float32) * scale
    if len(pieces) > 0:
        drawn = steps_of(rng, shape, pieces, -0.22, 0.18) * drawn
    return jnp.clip(drawn, min=-reach, max=reach).astype(held_as)


def setup_inputs(seed: int = 0) -> dict:
    keys = jax.random.split(jax.random.key(seed), 20)
    inputs = gaussian(keys[0], (SLOTS, L, D), 1.0, 6.0, ((0, 32),))
    lengths = with_ends(jax.random.randint(keys[1], (SLOTS,), 8, L + 1), jax.random.fold_in(keys[1], 1), 8, L).astype(jnp.int32)
    exits = with_ends(jax.random.randint(keys[2], (SLOTS,), 1, DEPTH + 1), jax.random.fold_in(keys[2], 1), 1, DEPTH).astype(jnp.int32)
    routes = draw_routes(jax.random.fold_in(keys[19], 71), 0)
    attn_weight = gaussian(keys[4], (D, 3 * D), D ** -0.5, 0.21875, ((0, 32),))
    merge_weight = gaussian(keys[5], (D, D), (D // 8) ** -0.5, 0.625, ((0, 32),))
    up_weight = gaussian(keys[6], (D, FF), D ** -0.5, 0.21875, ((0, 32),))
    down_weight = gaussian(keys[7], (FF, D), (FF // 2) ** -0.5, 0.15625, ((0, 32),))
    layer_biases = gaussian(keys[8], (6, D), 0.5, 3.0, ((1, 32),))
    norm_gains = jnp.clip(1.0 + 0.1 * jax.random.normal(keys[9], (2, D), jnp.float32), 0.5, 1.5).astype(jnp.bfloat16)
    unit_bias = gaussian(keys[10], (FF,), 0.5, 3.0, ((0, 32),))
    proj_weight = gaussian(keys[11], (D, SD), D ** -0.5, 0.21875)
    pool_weight = gaussian(keys[12], (3, SD, SD), SD ** -0.5, 0.5, (), jnp.float32)
    dense_weight = gaussian(keys[13], (SD, SD), SD ** -0.5, 0.5, (), jnp.float32)
    label_weight = gaussian(keys[14], (SD, CLASSES), SD ** -0.5, 0.5, (), jnp.float32)
    student_biases = gaussian(keys[15], (2, SD), 0.5, 3.0, (), jnp.float32)
    logit_bias = gaussian(keys[16], (CLASSES,), 0.5, 3.0, (), jnp.float32)
    grad_act = gaussian(keys[17], (SLOTS, L, D), 1.0, 6.0, ((0, 32),))
    grad_logits = gaussian(keys[18], (SLOTS, CLASSES), 1.0, 6.0, ((0, 32),), jnp.float32)
    return {"inputs": inputs, "lengths": lengths, "exits": exits, "routes": routes, "attn_weight": attn_weight, "merge_weight": merge_weight, "up_weight": up_weight, "down_weight": down_weight, "layer_biases": layer_biases, "norm_gains": norm_gains, "unit_bias": unit_bias, "proj_weight": proj_weight, "pool_weight": pool_weight, "dense_weight": dense_weight, "label_weight": label_weight, "student_biases": student_biases, "logit_bias": logit_bias, "grad_act": grad_act, "grad_logits": grad_logits}


@jax.custom_vjp
def low(v):
    return lax.optimization_barrier(v.astype(jnp.bfloat16)).astype(jnp.float32)

@jax.custom_vjp
def low_back(v):
    return v

def low_keep(v):
    return (low(v), None)

def low_pass(kept, grad):
    return (grad,)

def back_keep(v):
    return (v, None)

def back_low(kept, grad):
    return (low(grad),)
low.defvjp(low_keep, low_pass)
low_back.defvjp(back_keep, back_low)
precise = lax.Precision.HIGHEST
eps_norm = 1e-12
neg_big = -1e+30

def gelu_erf(values):
    return 0.5 * values * (1.0 + jax.scipy.special.erf(values * 0.7071067811865476))

def norm_rows(hidden, norm_gain, norm_shift):
    centred = hidden - lax.optimization_barrier(jnp.mean(hidden, axis=-1, keepdims=True))
    spread = lax.optimization_barrier(jnp.mean(centred * centred, axis=-1, keepdims=True))
    return centred * lax.rsqrt(spread + eps_norm) * norm_gain + norm_shift

def student_head(hidden, valid_keys, pool_weight, dense_weight, label_weight, dense_bias, logit_bias):
    groups, length, features = hidden.shape
    head_size = features // SH
    queries = jnp.einsum('bd,de->be', hidden[:, 0], pool_weight[0], precision=precise).reshape(groups, SH, head_size)
    key_rows = jnp.einsum('bld,de->ble', hidden, pool_weight[1], precision=precise).reshape(groups, length, SH, head_size)
    value_rows = jnp.einsum('bld,de->ble', hidden, pool_weight[2], precision=precise).reshape(groups, length, SH, head_size)
    scores = jnp.einsum('bhe,blhe->bhl', queries, key_rows, precision=precise) / math.sqrt(head_size)
    scores = jnp.where(valid_keys[:, None, :], scores, neg_big)
    shares = jax.nn.softmax(scores, axis=-1)
    pooled = jnp.einsum('bhl,blhe->bhe', shares, value_rows, precision=precise).reshape(groups, features)
    dense_out = jnp.tanh(jnp.dot(pooled, dense_weight, precision=precise) + dense_bias)
    return jnp.dot(dense_out, label_weight, precision=precise) + logit_bias

def layer_slot(tokens, valid_keys, attn_weight, merge_weight, up_weight, down_weight, layer_biases, norm_gains, unit_bias, proj_weight, pool_weight, dense_weight, label_weight, student_biases, logit_bias):
    length, features = tokens.shape
    mixed_proj = low_back(jnp.dot(tokens, attn_weight, precision=precise))
    queries = low(mixed_proj[:, :features] + layer_biases[0]).reshape(length, HEADS, HD)
    key_rows = low(mixed_proj[:, features:2 * features]).reshape(length, HEADS, HD)
    value_rows = low(mixed_proj[:, 2 * features:] + layer_biases[1]).reshape(length, HEADS, HD)
    scores = low_back(jnp.einsum('qhe,khe->hqk', queries, key_rows, precision=precise) * HD ** (-0.5))
    scores = jnp.where(valid_keys[None, None, :], scores, neg_big)
    attn_probs = low(jax.nn.softmax(scores, axis=-1))
    context = low(low_back(jnp.einsum('hqk,khe->qhe', attn_probs, value_rows, precision=precise).reshape(length, features)))
    attended = low_back(jnp.dot(context, merge_weight, precision=precise)) + layer_biases[2]
    first_norm = norm_rows(tokens + attended, norm_gains[0], layer_biases[3])
    inner_pre = low_back(jnp.dot(low(first_norm), up_weight, precision=precise)) + unit_bias
    active = low(gelu_erf(inner_pre))
    branch_out = low_back(jnp.dot(active, down_weight, precision=precise)) + layer_biases[4]
    leaving = low(norm_rows(first_norm + branch_out, norm_gains[1], layer_biases[5]))
    projected = low_back(jnp.dot(leaving, proj_weight, precision=precise)) + student_biases[0]
    logits = student_head(projected[None], valid_keys[None], pool_weight, dense_weight, label_weight, student_biases[1], logit_bias)[0]
    return (leaving, logits)

def forward(tokens, lengths, exits, routes, *params):
    positions = jnp.arange(L)

    def one_slot(slot_pair):
        slot_tokens, slot_length = slot_pair
        return layer_slot(slot_tokens, positions < slot_length, *params)
    leaving, logits = lax.map(jax.checkpoint(one_slot), (tokens, lengths))
    target = jnp.where(exits > LAYER, routes, SLOTS).astype(jnp.int32)
    moved = jnp.zeros_like(leaving).at[target].set(leaving, mode='drop')
    return (moved, logits)

def reference(inputs, lengths, exits, routes, attn_weight, merge_weight, up_weight, down_weight, layer_biases, norm_gains, unit_bias, proj_weight, pool_weight, dense_weight, label_weight, student_biases, logit_bias, grad_act, grad_logits):
    floats = [array_in.astype(jnp.float32) for array_in in (inputs, attn_weight, merge_weight, up_weight, down_weight, layer_biases, norm_gains, unit_bias, proj_weight, pool_weight, dense_weight, label_weight, student_biases, logit_bias)]

    def apply_layer(tokens, *params):
        return forward(tokens, lengths, exits, routes, *params)
    (moved, logits), pull_back = jax.vjp(apply_layer, *floats)
    grads = pull_back((grad_act.astype(jnp.float32), grad_logits))
    return (moved.astype(jnp.bfloat16), logits, grads[0], grads[1], grads[2], grads[3], grads[4], grads[5], grads[6], grads[7], grads[8], grads[9], grads[10], grads[11], grads[12], grads[13])
```

```python
import functools
import math

import jax
import jax.numpy as jnp
from jax import lax
from jax.experimental import pallas as pl
from jax.experimental.pallas import tpu as pltpu
from jax.sharding import PartitionSpec as P

HD = 64
SH = 2
LAYER = 4

precise = lax.Precision.HIGHEST
eps_norm = 1e-12
neg_big = -1e30


MESH = pl.DeviceIdType.MESH
f32 = jnp.float32
bf16 = jnp.bfloat16
SMALL = 128


class Place:
    def __init__(self):
        batch, zero = lax.axis_index("batch"), lax.axis_index("zero")
        self.z, self.x = lax.div(batch, 2), lax.rem(batch, 2)
        self.y, self.c = lax.div(zero, 2), lax.rem(zero, 2)

    def device(self, z=None, x=None, y=None, c=None):
        z = self.z if z is None else z
        x = self.x if x is None else x
        y = self.y if y is None else y
        c = self.c if c is None else c
        return (z * 2 + x, y * 2 + c)

    def sibling(self):
        return self.device(c=1 - self.c)

    def greet(self):
        barrier = pltpu.get_barrier_semaphore()

        def call(device):
            pl.semaphore_signal(barrier, inc=1, device_id=device, device_id_type=MESH)

        call(self.sibling())
        call(self.device(x=1 - self.x))
        call(self.device(y=1 - self.y))

        @pl.when(self.z > 0)
        def _():
            call(self.device(z=self.z - 1))

        @pl.when(self.z < 3)
        def _():
            call(self.device(z=self.z + 1))

        inner = lax.rem(lax.div(self.z + 1, 2), 2)
        pl.semaphore_wait(barrier, 4 + inner)

    def order(self, j):
        low = lax.div(3 - self.z, 2)
        near = self.z * low + (3 - self.z) * (1 - low)
        if j < 2:
            turned = near * (1 - j) + (1 - near) * j
        else:
            turned = j
        return turned * low + (3 - turned) * (1 - low)

    def first_way(self, zb):
        odd = lax.rem(zb, 2)
        return (
            self.x * odd + (1 - self.x) * (1 - odd),
            self.y * (1 - odd) + (1 - self.y) * odd,
        )

    def second_way(self, zb):
        odd = lax.rem(zb, 2)
        return (
            self.x * (1 - odd) + (1 - self.x) * odd,
            self.y * odd + (1 - self.y) * (1 - odd),
        )


def remote(src, dst, send_sem, recv_sem, device):
    return pltpu.make_async_remote_copy(
        src_ref=src,
        dst_ref=dst,
        send_sem=send_sem,
        recv_sem=recv_sem,
        device_id=device,
        device_id_type=MESH,
    )


class Gather:
    SEMS = 24

    def __init__(self, at, block, line, send, recv):
        self.at, self.block, self.line, self.send, self.recv = at, block, line, send, recv

    def move(self, view, k, device, recv_k=None):
        recv_k = k if recv_k is None else recv_k
        return remote(view, view, self.send.at[k], self.recv.at[recv_k], device)

    def hop(self, zb, step):
        at = self.at
        return self.move(
            self.block(zb, at.x, at.y, at.c),
            zb if step > 0 else zb + 20,
            at.device(z=at.z + step),
            recv_k=zb,
        )

    def first(self, zb, coming=False):
        at = self.at
        x, y = at.first_way(zb)
        view = self.block(zb, x, y, at.c) if coming else self.block(zb, at.x, at.y, at.c)
        return self.move(view, zb + 4, at.device(x=x, y=y))

    def second(self, zb, coming=False):
        at = self.at
        x, y = at.second_way(zb)
        view = self.block(zb, x, y, at.c) if coming else self.block(zb, at.x, at.y, at.c)
        return self.move(view, zb + 8, at.device(x=x, y=y))

    def corner(self, zb, coming=False):
        at = self.at
        x, y = at.second_way(zb)
        if coming:
            view = self.block(zb, 1 - at.x, 1 - at.y, at.c)
        else:
            view = self.block(zb, *at.first_way(zb), at.c)
        return self.move(view, zb + 12, at.device(x=x, y=y))

    def across(self, zb, coming=False):
        at = self.at
        return self.move(self.line(zb, 1 - at.c if coming else at.c), zb + 16, at.sibling())

    def arrive(self, j):
        at = self.at
        zb = at.order(j)
        if j > 0:
            self.hop(zb, 1).wait_recv()

        @pl.when(jnp.logical_and(zb <= at.z, at.z < 3))
        def _():
            self.hop(zb, 1).start()

        @pl.when(jnp.logical_and(zb >= at.z, at.z > 0))
        def _():
            self.hop(zb, -1).start()

        self.first(zb).start()
        self.second(zb).start()

    def turn(self, j):
        zb = self.at.order(j)
        self.first(zb, coming=True).wait_recv()
        self.corner(zb).start()

    def share(self, j):
        zb = self.at.order(j)
        self.second(zb, coming=True).wait_recv()
        self.corner(zb, coming=True).wait_recv()
        self.across(zb).start()

    def settle(self, j):
        self.across(self.at.order(j), coming=True).wait_recv()

    def finish(self):
        at = self.at
        for j in range(4):
            zb = at.order(j)

            @pl.when(jnp.logical_and(zb <= at.z, at.z < 3))
            def _():
                self.hop(zb, 1).wait_send()

            @pl.when(jnp.logical_and(zb >= at.z, at.z > 0))
            def _():
                self.hop(zb, -1).wait_send()

            self.first(zb).wait_send()
            self.second(zb).wait_send()
            self.corner(zb).wait_send()
            self.across(zb).wait_send()


def add_into(total, term):
    total[...] = (total[...].astype(f32) + term[...].astype(f32)).astype(bf16)


class Scatter:
    SEMS = 24

    def __init__(self, at, block, line, from_core, from_second, from_first, from_line, send, recv):
        self.at, self.block, self.line = at, block, line
        self.from_core, self.from_second = from_core, from_second
        self.from_first, self.from_line = from_first, from_line
        self.send, self.recv = send, recv

    def move(self, src, dst, k, device):
        return remote(src, dst, self.send.at[k], self.recv.at[k], device)

    def across(self, zb):
        at = self.at
        return self.move(self.line(zb, 1 - at.c), self.from_core.at[zb], zb, at.sibling())

    def second(self, zb):
        at = self.at
        x, y = at.second_way(zb)
        return self.move(
            self.block(zb, x, y, at.c), self.from_second.at[zb, 0], zb + 4, at.device(x=x, y=y)
        )

    def corner(self, zb):
        at = self.at
        x, y = at.second_way(zb)
        return self.move(
            self.block(zb, 1 - at.x, 1 - at.y, at.c),
            self.from_second.at[zb, 1],
            zb + 8,
            at.device(x=x, y=y),
        )

    def first(self, zb):
        at = self.at
        x, y = at.first_way(zb)
        return self.move(
            self.block(zb, x, y, at.c), self.from_first.at[zb], zb + 12, at.device(x=x, y=y)
        )

    def hop(self, zb, step):
        at = self.at
        side = 0 if step > 0 else 1
        return self.move(
            self.block(zb, at.x, at.y, at.c),
            self.from_line.at[zb, side],
            zb + 16 + 4 * side,
            at.device(z=at.z + step),
        )

    def give(self, j):
        self.across(self.at.order(j)).start()

    def join(self, j):
        at = self.at
        zb = at.order(j)
        self.across(zb).wait_recv()

        def one(k, carry):
            x, y = lax.div(k, 2), lax.rem(k, 2)
            add_into(self.block(zb, x, y, at.c), self.from_core.at[zb, x, y])
            return carry

        lax.fori_loop(0, 4, one, 0)
        self.second(zb).start()
        self.corner(zb).start()

    def halve(self, j):
        at = self.at
        zb = at.order(j)
        self.second(zb).wait_recv()
        self.corner(zb).wait_recv()
        x, y = at.first_way(zb)
        add_into(self.block(zb, x, y, at.c), self.from_second.at[zb, 1])
        self.first(zb).start()
        add_into(self.block(zb, at.x, at.y, at.c), self.from_second.at[zb, 0])

    def leave(self, j):
        at = self.at
        zb = at.order(j)
        mine = self.block(zb, at.x, at.y, at.c)
        self.first(zb).wait_recv()
        add_into(mine, self.from_first.at[zb])

        @pl.when(jnp.logical_and(zb >= at.z, at.z > 0))
        def _():
            self.hop(zb, 1).wait_recv()
            add_into(mine, self.from_line.at[zb, 0])

        @pl.when(jnp.logical_and(zb <= at.z, at.z < 3))
        def _():
            self.hop(zb, -1).wait_recv()
            add_into(mine, self.from_line.at[zb, 1])

        @pl.when(zb > at.z)
        def _():
            self.hop(zb, 1).start()

        @pl.when(zb < at.z)
        def _():
            self.hop(zb, -1).start()

    def finish(self):
        at = self.at
        for j in range(4):
            zb = at.order(j)
            self.across(zb).wait_send()
            self.second(zb).wait_send()
            self.corner(zb).wait_send()
            self.first(zb).wait_send()

            @pl.when(zb > at.z)
            def _():
                self.hop(zb, 1).wait_send()

            @pl.when(zb < at.z)
            def _():
                self.hop(zb, -1).wait_send()


def wide_block(ref):
    return (lambda z, x, y, c: ref.at[c, z, x, y]), (lambda z, c: ref.at[c, z])


def tall_block(ref):
    return (lambda z, x, y, c: ref.at[z, x, y, c]), (lambda z, c: ref.at[z, :, :, c])


def take_half(ref, c):
    width = ref.shape[1] // 2
    return ref[:, pl.ds(pl.multiple_of(c * width, 128), width)].astype(f32)


def gather_kernel(
    attn, merge, up, down, biases, gains, unit,
    attn_all, merge_all, up_all, down_all,
    attn_mine, merge_mine, up_mine, attn_pair, merge_pair, up_pair,
    send, recv, swap_send, swap_recv,
):
    at = Place()
    rows = attn.shape[0]
    own = pl.ds(pl.multiple_of(at.c * rows, 8), rows)
    lanes = attn.shape[1] // 2
    mine_small = jnp.concatenate([biases[...].astype(f32), gains[...].astype(f32)], axis=0)
    for ref, to_send, pair in (
        (attn, attn_mine, attn_pair),
        (merge, merge_mine, merge_pair),
        (up, up_mine, up_pair),
    ):
        width = ref.shape[1] // 2
        to_send[:, :width] = take_half(ref, 1 - at.c)
        pair[own, :width] = take_half(ref, at.c)
    small = jnp.zeros((rows, SMALL), f32)
    attn_mine[:, lanes:] = small
    attn_mine[0:8, lanes : lanes + rows] = mine_small
    attn_mine[8:9, lanes : lanes + unit.shape[1]] = unit[...].astype(f32)
    attn_pair[own, lanes:] = attn_mine[:, lanes:]
    down_all[at.z, at.x, at.y, at.c] = down[...]
    at.greet()
    swaps = []
    for k, (to_send, pair) in enumerate(
        ((attn_mine, attn_pair), (merge_mine, merge_pair), (up_mine, up_pair))
    ):
        swaps.append(
            remote(to_send, pair.at[own], swap_send.at[k], swap_recv.at[k], at.sibling())
        )
        swaps[-1].start()
    chunks = []
    for k, (ref, views) in enumerate(
        (
            (attn_all, wide_block),
            (merge_all, wide_block),
            (up_all, wide_block),
            (down_all, tall_block),
        )
    ):
        chunks.append(Gather(at, *views(ref), send.at[k], recv.at[k]))
    for k, (ref, pair) in enumerate(
        ((attn_all, attn_pair), (merge_all, merge_pair), (up_all, up_pair))
    ):
        swaps[k].wait_recv()
        ref[at.c, at.z, at.x, at.y] = pair[...].astype(bf16)
        chunks[k].arrive(0)
    chunks[3].arrive(0)
    for j in range(1, 4):
        for chunk in chunks:
            chunk.arrive(j)
            chunk.turn(j - 1)
    for chunk in chunks:
        chunk.turn(3)
    for j in range(4):
        for chunk in chunks:
            chunk.share(j)
    for j in range(4):
        for chunk in chunks:
            chunk.settle(j)
    for chunk in chunks:
        chunk.finish()
    for swap in swaps:
        swap.wait_send()


def gather_weights(attn, merge, up, down, biases, gains, unit):
    rows = attn.shape[0]
    widths = (attn.shape[1] // 2 + SMALL, merge.shape[1] // 2, up.shape[1] // 2)
    shapes = [(2, 4, 2, 2, 2 * rows, width) for width in widths]
    shapes.append((4, 2, 2, 2) + down.shape)
    vmem = pl.BlockSpec(memory_space=pltpu.VMEM)
    return pl.pallas_call(
        gather_kernel,
        out_shape=[jax.ShapeDtypeStruct(shape, bf16) for shape in shapes],
        in_specs=[vmem] * 7,
        out_specs=[vmem] * 4,
        scratch_shapes=[pltpu.VMEM((rows, width), f32) for width in widths]
        + [pltpu.VMEM((2 * rows, width), f32) for width in widths]
        + [
            pltpu.SemaphoreType.DMA((4, Gather.SEMS)),
            pltpu.SemaphoreType.DMA((4, Gather.SEMS)),
            pltpu.SemaphoreType.DMA((3,)),
            pltpu.SemaphoreType.DMA((3,)),
        ],
        compiler_params=pltpu.CompilerParams(
            collective_id=0, has_side_effects=True, vmem_limit_bytes=48 << 20
        ),
    )(attn, merge, up, down, biases, gains, unit.reshape(1, -1))


def scatter_kernel(
    attn_in, merge_in, up_in, down_in, attn_out, merge_out, up_out, down_out, *scratch
):
    at = Place()
    local, swap_send, swap_recv, send, recv = scratch[-5:]
    ins = (attn_in, merge_in, up_in, down_in)
    outs = (attn_out, merge_out, up_out, down_out)
    chunks, loads, totals, swaps = [], [], [], []
    for k in range(4):
        grad, from_core, from_second, from_first, from_line, total = scratch[6 * k : 6 * k + 6]
        loads.append(pltpu.make_async_copy(ins[k], grad, local.at[k]))
        loads[-1].start()
        block, line = (tall_block if k == 3 else wide_block)(grad)
        chunks.append(
            Scatter(
                at, block, line, from_core, from_second, from_first, from_line,
                send.at[k], recv.at[k],
            )
        )
        totals.append(total)
    at.greet()
    for k in (3, 2, 1, 0):
        loads[k].wait()
        for j in (3, 2, 1, 0):
            chunks[k].give(j)
    for stage in ("join", "halve", "leave"):
        for k in (3, 2, 1, 0):
            for j in (3, 2, 1, 0):
                getattr(chunks[k], stage)(j)
    for k in range(4):
        finish_scatter(at, chunks[k], totals[k], outs[k], swap_send.at[k], swap_recv.at[k], k == 3)
    for chunk in chunks:
        chunk.finish()


def finish_scatter(at, chunk, total, out, swap_send, swap_recv, tall):
    mine = chunk.block(at.z, at.x, at.y, at.c)
    if tall:
        out[...] = mine[...].astype(f32)
        return
    total[...] = mine[...].astype(f32)
    rows, width = out.shape[0], out.shape[1] // 2
    here = pl.ds(pl.multiple_of(at.c * width, 128), width)
    there = pl.ds(pl.multiple_of((1 - at.c) * width, 128), width)
    swap = remote(
        total.at[pl.ds(pl.multiple_of((1 - at.c) * rows, 8), rows)],
        out.at[:, here],
        swap_send,
        swap_recv,
        at.sibling(),
    )
    swap.start()
    out[:, here] = total[pl.ds(pl.multiple_of(at.c * rows, 8), rows), :]
    remote(
        total.at[pl.ds(pl.multiple_of((1 - at.c) * rows, 8), rows)],
        out.at[:, there],
        swap_send,
        swap_recv,
        at.sibling(),
    ).wait_recv()
    swap.wait_send()


def scatter_grads(attn, merge, up, down, shards):
    scratch = []
    for k, grad in enumerate((attn, merge, up, down)):
        rows, width = grad.shape[-2:]
        scratch += [
            pltpu.VMEM(grad.shape, bf16),
            pltpu.VMEM((4, 2, 2, rows, width), bf16),
            pltpu.VMEM((4, 2, rows, width), bf16),
            pltpu.VMEM((4, rows, width), bf16),
            pltpu.VMEM((4, 2, rows, width), bf16),
            pltpu.VMEM((rows, width) if k < 3 else (8, 128), f32),
        ]
    vmem = pl.BlockSpec(memory_space=pltpu.VMEM)
    return pl.pallas_call(
        scatter_kernel,
        out_shape=[jax.ShapeDtypeStruct(shape, f32) for shape in shards],
        in_specs=[pl.BlockSpec(memory_space=pl.ANY)] * 4,
        out_specs=[vmem] * 4,
        scratch_shapes=scratch
        + [
            pltpu.SemaphoreType.DMA((4,)),
            pltpu.SemaphoreType.DMA((4,)),
            pltpu.SemaphoreType.DMA((4,)),
            pltpu.SemaphoreType.DMA((4, Scatter.SEMS)),
            pltpu.SemaphoreType.DMA((4, Scatter.SEMS)),
        ],
        compiler_params=pltpu.CompilerParams(
            collective_id=1, has_side_effects=True, vmem_limit_bytes=56 << 20
        ),
    )(attn, merge, up, down)


def passed_along(block, axis, distance):
    devices = range(lax.axis_size(axis))
    route = [((i - distance) % len(devices), i) for i in devices]
    return lax.ppermute(block, axis, route)


def product(pattern, left, right):
    return jnp.einsum(pattern, left, right, preferred_element_type=jnp.float32)


def gelu_erf(values):
    return 0.5 * values * (1.0 + jax.scipy.special.erf(values * 0.7071067811865476))


def gelu_slope(values):
    return (
        0.5 * (1.0 + jax.scipy.special.erf(values * 0.7071067811865476))
        + values * jnp.exp(-0.5 * values * values) * 0.3989422804014327
    )


def norm_forward(hidden, norm_gain, norm_shift):
    centred = hidden - jnp.mean(hidden, axis=-1, keepdims=True)
    inverse = lax.rsqrt(jnp.mean(centred * centred, axis=-1, keepdims=True) + eps_norm)
    normed = centred * inverse
    return (normed * norm_gain + norm_shift, normed, inverse)


def norm_backward(grad_out, normed, inverse, norm_gain):
    scaled = grad_out * norm_gain
    return inverse * (
        scaled
        - jnp.mean(scaled, axis=-1, keepdims=True)
        - normed * jnp.mean(scaled * normed, axis=-1, keepdims=True)
    )


def student_head(
    hidden, valid_keys, pool_weight, dense_weight, label_weight, dense_bias, logit_bias
):
    groups, length, features = hidden.shape
    head_size = features // SH
    queries = jnp.einsum("bd,de->be", hidden[:, 0], pool_weight[0], precision=precise).reshape(
        groups, SH, head_size
    )
    key_rows = jnp.einsum("bld,de->ble", hidden, pool_weight[1], precision=precise).reshape(
        groups, length, SH, head_size
    )
    value_rows = jnp.einsum("bld,de->ble", hidden, pool_weight[2], precision=precise).reshape(
        groups, length, SH, head_size
    )
    scores = jnp.einsum("bhe,blhe->bhl", queries, key_rows, precision=precise) / math.sqrt(
        head_size
    )
    scores = jnp.where(valid_keys[:, None, :], scores, neg_big)
    shares = jax.nn.softmax(scores, axis=-1)
    pooled = jnp.einsum("bhl,blhe->bhe", shares, value_rows, precision=precise).reshape(
        groups, features
    )
    dense_out = jnp.tanh(jnp.dot(pooled, dense_weight, precision=precise) + dense_bias)
    return jnp.dot(dense_out, label_weight, precision=precise) + logit_bias


def layer_forward(tokens, valid_keys, weights, student):
    attn_weight, merge_weight, up_weight, down_weight, biases, norm_gains, unit_bias = weights
    proj_weight, pool_weight, dense_weight, label_weight, student_biases, logit_bias = student
    groups, length, features = tokens.shape
    mixed_proj = product("bld,de->ble", tokens, attn_weight)
    queries = (
        (mixed_proj[..., :features] + biases[0])
        .astype(jnp.bfloat16)
        .reshape(groups, length, -1, HD)
    )
    key_rows = (
        mixed_proj[..., features : 2 * features]
        .astype(jnp.bfloat16)
        .reshape(groups, length, -1, HD)
    )
    value_rows = (
        (mixed_proj[..., 2 * features :] + biases[1])
        .astype(jnp.bfloat16)
        .reshape(groups, length, -1, HD)
    )
    scores = product("bqhe,bkhe->bhqk", queries, key_rows) * HD ** (-0.5)
    scores = jnp.where(valid_keys[:, None, None, :], scores, neg_big)
    row_top = jnp.max(scores, axis=-1, keepdims=True)
    exponent = jnp.exp(scores - row_top)
    row_total = jnp.sum(exponent, axis=-1, keepdims=True)
    attn_probs = (exponent / row_total).astype(jnp.bfloat16)
    log_total = row_top + jnp.log(row_total)
    context = (
        product("bhqk,bkhe->bqhe", attn_probs, value_rows)
        .astype(jnp.bfloat16)
        .reshape(groups, length, features)
    )
    attended = product("bld,de->ble", context, merge_weight) + biases[2]
    first_norm, normed_one, inverse_one = norm_forward(
        tokens.astype(jnp.float32) + attended, norm_gains[0], biases[3]
    )
    first_low = first_norm.astype(jnp.bfloat16)
    inner_pre = product("bld,df->blf", first_low, up_weight) + unit_bias
    active = gelu_erf(inner_pre).astype(jnp.bfloat16)
    branch_out = product("blf,fd->bld", active, down_weight) + biases[4]
    second, normed_two, inverse_two = norm_forward(
        first_norm + branch_out, norm_gains[1], biases[5]
    )
    leaving = second.astype(jnp.bfloat16)
    projected = product("bld,de->ble", leaving, proj_weight) + student_biases[0]

    def classify(hidden, attn_part, dense_part, label_part, dense_bias, class_bias):
        return student_head(
            hidden, valid_keys, attn_part, dense_part, label_part, dense_bias, class_bias
        )

    logits, pull_back = jax.vjp(
        classify, projected, pool_weight, dense_weight, label_weight, student_biases[1], logit_bias
    )
    saved_state = (
        tokens,
        valid_keys,
        queries,
        key_rows,
        value_rows,
        log_total,
        context,
        normed_one,
        inverse_one,
        first_low,
        inner_pre,
        active,
        normed_two,
        inverse_two,
        leaving,
        pull_back,
    )
    return (leaving, logits, saved_state)


def layer_backward(saved_state, grad_leaving, grad_logits, weights, proj_weight):
    (
        tokens,
        valid_keys,
        queries,
        key_rows,
        value_rows,
        log_total,
        context,
        normed_one,
        inverse_one,
        first_low,
        inner_pre,
        active,
        normed_two,
        inverse_two,
        leaving,
        pull_back,
    ) = saved_state
    attn_weight, merge_weight, up_weight, down_weight, biases, norm_gains, unit_bias = weights
    groups, length, features = tokens.shape
    grad_proj, grad_pool, grad_dense, grad_label, grad_dense_bias, grad_logit_bias = pull_back(
        grad_logits
    )
    proj_low = grad_proj.astype(jnp.bfloat16)
    grad_proj_weight = product("bld,ble->de", leaving, proj_low)
    grad_second = grad_leaving + product("ble,de->bld", proj_low, proj_weight)
    grad_mid = norm_backward(grad_second, normed_two, inverse_two, norm_gains[1])
    down_low = grad_mid.astype(jnp.bfloat16)
    grad_down = product("blf,bld->fd", active, down_low)
    grad_inner = product("bld,fd->blf", down_low, down_weight) * gelu_slope(inner_pre)
    inner_low = grad_inner.astype(jnp.bfloat16)
    grad_up = product("bld,blf->df", first_low, inner_low)
    grad_first = grad_mid + product("blf,df->bld", inner_low, up_weight)
    grad_res = norm_backward(grad_first, normed_one, inverse_one, norm_gains[0])
    res_low = grad_res.astype(jnp.bfloat16)
    grad_merge = product("blc,bld->cd", context, res_low)
    grad_context = (
        product("bld,cd->blc", res_low, merge_weight)
        .astype(jnp.bfloat16)
        .reshape(groups, length, -1, HD)
    )
    scores = product("bqhe,bkhe->bhqk", queries, key_rows) * HD ** (-0.5)
    scores = jnp.where(valid_keys[:, None, None, :], scores, neg_big)
    attn_probs = jnp.exp(scores - log_total)
    grad_values = product("bhqk,bqhe->bkhe", attn_probs.astype(jnp.bfloat16), grad_context)
    grad_probs = product("bqhe,bkhe->bhqk", grad_context, value_rows)
    grad_scores = (
        attn_probs * (grad_probs - jnp.sum(grad_probs * attn_probs, axis=-1, keepdims=True))
    ).astype(jnp.bfloat16)
    grad_queries = product("bhqk,bkhe->bqhe", grad_scores, key_rows) * HD ** (-0.5)
    grad_keys = product("bhqk,bqhe->bkhe", grad_scores, queries) * HD ** (-0.5)
    grad_queries = grad_queries.reshape(groups, length, features)
    grad_values = grad_values.reshape(groups, length, features)
    grad_mixed = jnp.concatenate(
        [grad_queries, grad_keys.reshape(groups, length, features), grad_values], axis=-1
    )
    mixed_low = grad_mixed.astype(jnp.bfloat16)
    grad_attn = product("bld,ble->de", tokens, mixed_low)
    grad_tokens = grad_res + product("ble,de->bld", mixed_low, attn_weight)
    grad_biases = jnp.stack(
        [
            jnp.sum(grad_queries, axis=(0, 1)),
            jnp.sum(grad_values, axis=(0, 1)),
            jnp.sum(grad_res, axis=(0, 1)),
            jnp.sum(grad_first, axis=(0, 1)),
            jnp.sum(grad_mid, axis=(0, 1)),
            jnp.sum(grad_second, axis=(0, 1)),
        ]
    )
    grad_gains = jnp.stack(
        [
            jnp.sum(grad_first * normed_one, axis=(0, 1)),
            jnp.sum(grad_second * normed_two, axis=(0, 1)),
        ]
    )
    grad_unit = jnp.sum(grad_inner, axis=(0, 1))
    grad_student_biases = jnp.stack([jnp.sum(grad_proj, axis=(0, 1)), grad_dense_bias])
    layer_terms = (grad_attn, grad_merge, grad_up, grad_down, grad_biases, grad_gains, grad_unit)
    student_terms = (
        grad_proj_weight,
        grad_pool,
        grad_dense,
        grad_label,
        grad_student_biases,
        grad_logit_bias,
    )
    return (grad_tokens, layer_terms, student_terms)


BOTH = ("batch", "zero")


def whole_gather(attn, merge, up, down, biases, gains, unit):
    return (
        lax.all_gather(attn, BOTH, axis=0, tiled=True),
        lax.all_gather(merge, BOTH, axis=0, tiled=True),
        lax.all_gather(up, BOTH, axis=0, tiled=True),
        lax.all_gather(down, BOTH, axis=0, tiled=True),
        lax.all_gather(biases, BOTH, axis=1, tiled=True).astype(f32),
        lax.all_gather(gains, BOTH, axis=1, tiled=True).astype(f32),
        lax.all_gather(unit, BOTH, axis=0, tiled=True).astype(f32),
    )


def linked_gather(attn, merge, up, down, biases, gains, unit):
    attn_all, merge_all, up_all, down_all = gather_weights(
        attn, merge, up, down, biases, gains, unit
    )

    def joined(halves, width):
        halves = halves.reshape(2, -1, halves.shape[-1])[:, :, :width]
        return jnp.concatenate([halves[0], halves[1]], axis=1)

    width = attn.shape[1] // 2
    small = attn_all[0].reshape(-1, attn.shape[0], attn_all.shape[-1])[:, :, width:].astype(f32)
    lanes = small[:, :8, : biases.shape[1]].transpose(1, 0, 2).reshape(8, -1)
    return (
        joined(attn_all, width),
        joined(merge_all, merge.shape[1] // 2),
        joined(up_all, up.shape[1] // 2),
        down_all.reshape(-1, down.shape[1]),
        lanes[:6],
        lanes[6:],
        small[:, 8, : unit.shape[0]].reshape(-1),
    )


def halves_of(grad, parts):
    width = grad.shape[1] // 2
    low = grad.astype(bf16)
    return jnp.stack([low[:, :width], low[:, width:]]).reshape(2, 4, 2, 2, -1, width)


def on_device(linked, *arguments):
    (
        inputs, lengths, exits, routes, attn_weight, merge_weight, up_weight, down_weight,
        layer_biases, norm_gains, unit_bias, proj_weight, pool_weight, dense_weight,
        label_weight, student_biases, logit_bias, grad_act, grad_logits,
    ) = arguments
    slot_count, length, features = inputs.shape
    batch_count = lax.axis_size("batch")
    zero_count = lax.axis_size("zero")
    section_count = (batch_count - 1).bit_length()
    student = (proj_weight, pool_weight, dense_weight, label_weight, student_biases, logit_bias)
    my_batch = lax.axis_index("batch")
    sent = exits > LAYER
    offsets = (routes // (slot_count * zero_count) - my_batch + batch_count) % batch_count
    dest_local = routes % slot_count
    one_back = offsets[0] == batch_count - 1
    lands_first = dest_local[0] == 0
    other = jnp.where(one_back, offsets[1], offsets[0])

    def swapped(pair, straight):
        return jnp.where(straight, pair[0], pair[1]), jnp.where(straight, pair[1], pair[0])

    def carried(near, far, sign):
        near = passed_along(near, "batch", -sign)
        for level in range(section_count):
            moved = passed_along(far, "batch", sign * (1 << level))
            far = jnp.where(other // (1 << level) % 2 == 1, moved, far)
        return near, far

    here = swapped(grad_act, lands_first)
    near, far = carried(*swapped(here, one_back), -1)
    back = swapped((near, far), one_back)
    grad_leaving = jnp.stack(back).astype(f32) * sent[:, None, None].astype(f32)
    weights = (linked_gather if linked else whole_gather)(
        attn_weight, merge_weight, up_weight, down_weight, layer_biases, norm_gains, unit_bias
    )
    valid_all = jnp.arange(length)[None, :] < lengths[:, None]
    leaving, logits, saved_state = layer_forward(inputs, valid_all, weights, student)
    pieces = jnp.where(sent[:, None, None], leaving, jnp.zeros_like(leaving))
    near, far = carried(*swapped(pieces, one_back), 1)
    landed = swapped((near, far), one_back)
    arrived = jnp.stack(swapped(landed, lands_first))
    grad_tokens, layer_sum, student_sum = layer_backward(
        saved_state, grad_leaving, grad_logits, weights, proj_weight
    )
    if linked:
        shards = [
            w.shape for w in (attn_weight, merge_weight, up_weight, down_weight)
        ]
        layer_grads = scatter_grads(
            halves_of(layer_sum[0], linked),
            halves_of(layer_sum[1], linked),
            halves_of(layer_sum[2], linked),
            layer_sum[3].astype(bf16).reshape(4, 2, 2, 2, -1, features),
            shards,
        )
    else:
        layer_grads = [
            lax.psum_scatter(layer_sum[k], BOTH, scatter_dimension=0, tiled=True) for k in range(4)
        ]
    small_grads = (
        lax.psum_scatter(layer_sum[4], BOTH, scatter_dimension=1, tiled=True),
        lax.psum_scatter(layer_sum[5], BOTH, scatter_dimension=1, tiled=True),
        lax.psum_scatter(layer_sum[6], BOTH, scatter_dimension=0, tiled=True),
    )
    student_grads = lax.psum(student_sum, BOTH)
    return (arrived, logits, grad_tokens, *layer_grads, *small_grads, *student_grads)


def solution(mesh):
    in_specs = (
        P(("batch", "zero"), None, None),
        P(("batch", "zero")),
        P(("batch", "zero")),
        P(("batch", "zero")),
        P(("batch", "zero"), None),
        P(("batch", "zero"), None),
        P(("batch", "zero"), None),
        P(("batch", "zero"), None),
        P(None, ("batch", "zero")),
        P(None, ("batch", "zero")),
        P(("batch", "zero")),
        P(),
        P(),
        P(),
        P(),
        P(),
        P(),
        P(("batch", "zero"), None, None),
        P(("batch", "zero"), None),
    )
    out_specs = (
        P(("batch", "zero"), None, None),
        P(("batch", "zero"), None),
        P(("batch", "zero"), None, None),
        P(("batch", "zero"), None),
        P(("batch", "zero"), None),
        P(("batch", "zero"), None),
        P(("batch", "zero"), None),
        P(None, ("batch", "zero")),
        P(None, ("batch", "zero")),
        P(("batch", "zero")),
        P(),
        P(),
        P(),
        P(),
        P(),
        P(),
    )
    linked = (mesh.shape["batch"], mesh.shape["zero"]) == (8, 4)
    return jax.shard_map(
        functools.partial(on_device, linked), mesh=mesh, in_specs=in_specs, out_specs=out_specs, check_vma=False
    )
```

```python
import functools
import math

import jax
import jax.numpy as jnp
from jax import lax
from jax.experimental import pallas as pl
from jax.experimental.pallas import tpu as pltpu
from jax.sharding import PartitionSpec as P

HD = 64
SH = 2
LAYER = 4

precise = lax.Precision.HIGHEST
eps_norm = 1e-12
neg_big = -1e30


MESH = pl.DeviceIdType.MESH
f32 = jnp.float32
bf16 = jnp.bfloat16
SMALL = 128


class Place:
    def __init__(self):
        batch, zero = lax.axis_index("batch"), lax.axis_index("zero")
        self.z, self.x = lax.div(batch, 2), lax.rem(batch, 2)
        self.y, self.c = lax.div(zero, 2), lax.rem(zero, 2)

    def device(self, z=None, x=None, y=None, c=None):
        z = self.z if z is None else z
        x = self.x if x is None else x
        y = self.y if y is None else y
        c = self.c if c is None else c
        return (z * 2 + x, y * 2 + c)

    def sibling(self):
        return self.device(c=1 - self.c)

    def greet(self, far=False):
        barrier = pltpu.get_barrier_semaphore()

        def call(device):
            pl.semaphore_signal(barrier, inc=1, device_id=device, device_id_type=MESH)

        call(self.sibling())
        call(self.device(x=1 - self.x))
        call(self.device(y=1 - self.y))

        @pl.when(self.z > 0)
        def _():
            call(self.device(z=self.z - 1))

        @pl.when(self.z < 3)
        def _():
            call(self.device(z=self.z + 1))

        if far:
            call(self.device(z=lax.rem(self.z + 2, 4)))
        inner = lax.rem(lax.div(self.z + 1, 2), 2)
        pl.semaphore_wait(barrier, 4 + inner + (1 if far else 0))

    def order(self, j):
        low = lax.div(3 - self.z, 2)
        near = self.z * low + (3 - self.z) * (1 - low)
        if j < 2:
            turned = near * (1 - j) + (1 - near) * j
        else:
            turned = j
        return turned * low + (3 - turned) * (1 - low)

    def first_way(self, zb):
        odd = lax.rem(zb, 2)
        return (
            self.x * odd + (1 - self.x) * (1 - odd),
            self.y * (1 - odd) + (1 - self.y) * odd,
        )

    def second_way(self, zb):
        odd = lax.rem(zb, 2)
        return (
            self.x * (1 - odd) + (1 - self.x) * odd,
            self.y * odd + (1 - self.y) * (1 - odd),
        )


def remote(src, dst, send_sem, recv_sem, device):
    return pltpu.make_async_remote_copy(
        src_ref=src,
        dst_ref=dst,
        send_sem=send_sem,
        recv_sem=recv_sem,
        device_id=device,
        device_id_type=MESH,
    )


class Gather:
    SEMS = 24

    def __init__(self, at, block, line, send, recv):
        self.at, self.block, self.line, self.send, self.recv = at, block, line, send, recv

    def move(self, view, k, device, recv_k=None):
        recv_k = k if recv_k is None else recv_k
        return remote(view, view, self.send.at[k], self.recv.at[recv_k], device)

    def hop(self, zb, step):
        at = self.at
        return self.move(
            self.block(zb, at.x, at.y, at.c),
            zb if step > 0 else zb + 20,
            at.device(z=at.z + step),
            recv_k=zb,
        )

    def first(self, zb, coming=False):
        at = self.at
        x, y = at.first_way(zb)
        view = self.block(zb, x, y, at.c) if coming else self.block(zb, at.x, at.y, at.c)
        return self.move(view, zb + 4, at.device(x=x, y=y))

    def second(self, zb, coming=False):
        at = self.at
        x, y = at.second_way(zb)
        view = self.block(zb, x, y, at.c) if coming else self.block(zb, at.x, at.y, at.c)
        return self.move(view, zb + 8, at.device(x=x, y=y))

    def corner(self, zb, coming=False):
        at = self.at
        x, y = at.second_way(zb)
        if coming:
            view = self.block(zb, 1 - at.x, 1 - at.y, at.c)
        else:
            view = self.block(zb, *at.first_way(zb), at.c)
        return self.move(view, zb + 12, at.device(x=x, y=y))

    def across(self, zb, coming=False):
        at = self.at
        return self.move(self.line(zb, 1 - at.c if coming else at.c), zb + 16, at.sibling())

    def arrive(self, j):
        at = self.at
        zb = at.order(j)
        if j > 0:
            self.hop(zb, 1).wait_recv()

        @pl.when(jnp.logical_and(zb <= at.z, at.z < 3))
        def _():
            self.hop(zb, 1).start()

        @pl.when(jnp.logical_and(zb >= at.z, at.z > 0))
        def _():
            self.hop(zb, -1).start()

        self.first(zb).start()
        self.second(zb).start()

    def turn(self, j):
        zb = self.at.order(j)
        self.first(zb, coming=True).wait_recv()
        self.corner(zb).start()

    def share(self, j):
        zb = self.at.order(j)
        self.second(zb, coming=True).wait_recv()
        self.corner(zb, coming=True).wait_recv()
        self.across(zb).start()

    def settle(self, j):
        self.across(self.at.order(j), coming=True).wait_recv()

    def finish(self):
        at = self.at
        for j in range(4):
            zb = at.order(j)

            @pl.when(jnp.logical_and(zb <= at.z, at.z < 3))
            def _():
                self.hop(zb, 1).wait_send()

            @pl.when(jnp.logical_and(zb >= at.z, at.z > 0))
            def _():
                self.hop(zb, -1).wait_send()

            self.first(zb).wait_send()
            self.second(zb).wait_send()
            self.corner(zb).wait_send()
            self.across(zb).wait_send()


def add_into(total, term):
    total[...] = (total[...].astype(f32) + term[...].astype(f32)).astype(bf16)


class Scatter:
    SEMS = 24

    def __init__(self, at, block, line, from_core, from_second, from_first, from_line, send, recv):
        self.at, self.block, self.line = at, block, line
        self.from_core, self.from_second = from_core, from_second
        self.from_first, self.from_line = from_first, from_line
        self.send, self.recv = send, recv

    def move(self, src, dst, k, device):
        return remote(src, dst, self.send.at[k], self.recv.at[k], device)

    def across(self, zb):
        at = self.at
        return self.move(self.line(zb, 1 - at.c), self.from_core.at[zb], zb, at.sibling())

    def second(self, zb):
        at = self.at
        x, y = at.second_way(zb)
        return self.move(
            self.block(zb, x, y, at.c), self.from_second.at[zb, 0], zb + 4, at.device(x=x, y=y)
        )

    def corner(self, zb):
        at = self.at
        x, y = at.second_way(zb)
        return self.move(
            self.block(zb, 1 - at.x, 1 - at.y, at.c),
            self.from_second.at[zb, 1],
            zb + 8,
            at.device(x=x, y=y),
        )

    def first(self, zb):
        at = self.at
        x, y = at.first_way(zb)
        return self.move(
            self.block(zb, x, y, at.c), self.from_first.at[zb], zb + 12, at.device(x=x, y=y)
        )

    def hop(self, zb, step):
        at = self.at
        side = 0 if step > 0 else 1
        return self.move(
            self.block(zb, at.x, at.y, at.c),
            self.from_line.at[zb, side],
            zb + 16 + 4 * side,
            at.device(z=at.z + step),
        )

    def give(self, j):
        self.across(self.at.order(j)).start()

    def join(self, j):
        at = self.at
        zb = at.order(j)
        self.across(zb).wait_recv()

        def one(k, carry):
            x, y = lax.div(k, 2), lax.rem(k, 2)
            add_into(self.block(zb, x, y, at.c), self.from_core.at[zb, x, y])
            return carry

        lax.fori_loop(0, 4, one, 0)
        self.second(zb).start()
        self.corner(zb).start()

    def halve(self, j):
        at = self.at
        zb = at.order(j)
        self.second(zb).wait_recv()
        self.corner(zb).wait_recv()
        x, y = at.first_way(zb)
        add_into(self.block(zb, x, y, at.c), self.from_second.at[zb, 1])
        self.first(zb).start()
        add_into(self.block(zb, at.x, at.y, at.c), self.from_second.at[zb, 0])

    def leave(self, j):
        at = self.at
        zb = at.order(j)
        mine = self.block(zb, at.x, at.y, at.c)
        self.first(zb).wait_recv()
        add_into(mine, self.from_first.at[zb])

        @pl.when(jnp.logical_and(zb >= at.z, at.z > 0))
        def _():
            self.hop(zb, 1).wait_recv()
            add_into(mine, self.from_line.at[zb, 0])

        @pl.when(jnp.logical_and(zb <= at.z, at.z < 3))
        def _():
            self.hop(zb, -1).wait_recv()
            add_into(mine, self.from_line.at[zb, 1])

        @pl.when(zb > at.z)
        def _():
            self.hop(zb, 1).start()

        @pl.when(zb < at.z)
        def _():
            self.hop(zb, -1).start()

    def finish(self):
        at = self.at
        for j in range(4):
            zb = at.order(j)
            self.across(zb).wait_send()
            self.second(zb).wait_send()
            self.corner(zb).wait_send()
            self.first(zb).wait_send()

            @pl.when(zb > at.z)
            def _():
                self.hop(zb, 1).wait_send()

            @pl.when(zb < at.z)
            def _():
                self.hop(zb, -1).wait_send()


def wide_block(ref):
    return (lambda z, x, y, c: ref.at[c, z, x, y]), (lambda z, c: ref.at[c, z])


def tall_block(ref):
    return (lambda z, x, y, c: ref.at[z, x, y, c]), (lambda z, c: ref.at[z, :, :, c])


def take_half(ref, c):
    width = ref.shape[1] // 2
    return ref[:, pl.ds(pl.multiple_of(c * width, 128), width)].astype(f32)


def finish_scatter(at, chunk, total, out, swap_send, swap_recv, tall):
    mine = chunk.block(at.z, at.x, at.y, at.c)
    if tall:
        out[...] = mine[...].astype(f32)
        return
    total[...] = mine[...].astype(f32)
    rows, width = out.shape[0], out.shape[1] // 2
    here = pl.ds(pl.multiple_of(at.c * width, 128), width)
    there = pl.ds(pl.multiple_of((1 - at.c) * width, 128), width)
    swap = remote(
        total.at[pl.ds(pl.multiple_of((1 - at.c) * rows, 8), rows)],
        out.at[:, here],
        swap_send,
        swap_recv,
        at.sibling(),
    )
    swap.start()
    out[:, here] = total[pl.ds(pl.multiple_of(at.c * rows, 8), rows), :]
    remote(
        total.at[pl.ds(pl.multiple_of((1 - at.c) * rows, 8), rows)],
        out.at[:, there],
        swap_send,
        swap_recv,
        at.sibling(),
    ).wait_recv()
    swap.wait_send()


def dots(left, right, over_left, over_right):
    return lax.dot_general(
        left, right, (((over_left,), (over_right,)), ((), ())), preferred_element_type=f32
    )


def rows_of(i, size):
    return pl.ds(pl.multiple_of(i * size, size), size)


def lanes_of(i, size=128):
    return pl.ds(pl.multiple_of(i * size, size), size)


def unpack_small(attn_all, vectors, units, shard):
    halves, width = attn_all.shape[-2:]
    lanes = pl.ds(width - SMALL, SMALL)
    lane = lax.broadcasted_iota(jnp.int32, (8, SMALL), 1)
    for ref, rows, size in ((vectors, 0, shard), (units, 8, 4 * shard)):
        tiles = [jnp.zeros((8, SMALL), f32) for _ in range(ref.shape[1] // SMALL)]
        for n in range(32):
            chip, core = n // 2, n % 2
            piece = attn_all[0, chip // 4, chip // 2 % 2, chip % 2, :, lanes].astype(f32)
            piece = piece[core * shard + rows : core * shard + rows + 8]
            tile, shift = n * size // SMALL, n * size % SMALL
            if shift:
                piece = pltpu.roll(piece, shift, 1)
            tiles[tile] = tiles[tile] + jnp.where(lane >= shift, piece, 0.0)
            if shift + size > SMALL:
                tiles[tile + 1] = tiles[tile + 1] + jnp.where(lane < shift, piece, 0.0)
        for t, tile in enumerate(tiles):
            ref[:, t * SMALL : (t + 1) * SMALL] = tile[: ref.shape[0]]


def project_slot(tokens, weights, vectors, mixed, slot, length):
    features = tokens.shape[1]
    width = 3 * features // 2
    here = pl.ds(slot * length, length)
    for half in range(2):
        for part in range(2):
            size = features if (part == half) else width - features
            start = 0 if part == 0 else width - size
            out = jnp.dot(
                tokens[here, :],
                weights(half, start, size),
                preferred_element_type=f32,
            )
            if part == half:
                out = out + vectors[half : half + 1, :]
            mixed[here, half * width + start : half * width + start + size] = out.astype(bf16)


def attend_pair(mixed, context, totals, slot, pair, length, used):
    features = context.shape[1]
    here = pl.ds(slot * length, length) if isinstance(slot, int) else rows_of(slot, length)
    base = pl.multiple_of(pair * 128, 128)
    two_q = mixed[here, pl.ds(base, 128)]
    two_k = mixed[here, pl.ds(pl.multiple_of(base + features, 128), 128)]
    two_v = mixed[here, pl.ds(pl.multiple_of(base + 2 * features, 128), 128)]
    low = lax.broadcasted_iota(jnp.int32, two_k.shape, 1) < HD
    valid = lax.broadcasted_iota(jnp.int32, (length, 1), 0) < used
    none = jnp.zeros_like(two_k)
    two_q = two_q * jnp.asarray(HD ** (-0.5), bf16)
    outs = []
    for head in range(2):
        keys = jnp.where(low if head == 0 else ~low, two_k, none)
        scores = jnp.where(valid, dots(keys, two_q, 1, 1), neg_big)
        top = jnp.max(scores, axis=0, keepdims=True)
        powers = jnp.exp(scores - top)
        total = jnp.sum(powers, axis=0, keepdims=True)
        shares = (powers * (1.0 / total)).astype(bf16)
        outs.append(dots(shares, two_v, 0, 0))
        totals[slot, pl.ds(2 * pair + head, 1), :] = top + jnp.log(total)
    context[here, pl.ds(base, 128)] = jnp.where(low, outs[0], outs[1]).astype(bf16)


def norm_rows(hidden, gain, shift):
    centred = hidden - jnp.mean(hidden, axis=-1, keepdims=True)
    inverse = lax.rsqrt(jnp.mean(centred * centred, axis=-1, keepdims=True) + eps_norm)
    normed = centred * inverse
    return normed * gain + shift, normed, inverse


def gelu_both(v):
    size = jnp.abs(v) * 0.7071067811865476
    t = 1.0 / (1.0 + 0.3275911 * size)
    bell = jnp.exp(-0.5 * v * v)
    poly = t * (
        0.254829592
        + t * (-0.284496736 + t * (1.421413741 + t * (-1.453152027 + t * 1.061405429)))
    )
    tail = 0.5 * poly * bell
    share = jnp.where(v < 0.0, tail, 1.0 - tail)
    return v * share, share + v * bell * 0.3989422804014327


def first_rows(tokens, context, merge, up, vectors, units, first, near, outs, r, size):
    normed_out, inverse_out, low_out, active_out, slope_out = outs
    here = rows_of(r, size)
    attended = jnp.concatenate(
        [jnp.dot(context[here, :], merge(h), preferred_element_type=f32) for h in range(2)], axis=1
    )
    hidden = tokens[here, :].astype(f32) + (attended + vectors[2:3, :])
    full, normed, inverse = norm_rows(hidden, vectors[6:7, :], vectors[3:4, :])
    first[here, :] = full
    low = full.astype(bf16)
    normed_out[here, :] = normed.astype(bf16)
    inverse_out[here, :] = inverse
    low_out[here, :] = low
    width = units.shape[1] // 2
    step = width // 2
    for part in range(4):
        cols = pl.ds(part * step, step)
        inner = jnp.dot(low, up(part // 2, part % 2 * step, step), preferred_element_type=f32)
        active, slope = gelu_both(inner + units[0:1, cols])
        active_out[here, cols] = active.astype(bf16)
        slope_out[here, cols] = slope.astype(bf16)


def second_rows(active, down, vectors, first, outs, r, size):
    normed_out, inverse_out, leaving_out = outs
    here = rows_of(r, size)
    branch = jnp.dot(active[here, :], down[...], preferred_element_type=f32)
    hidden = first[here, :] + (branch + vectors[4:5, :])
    full, normed, inverse = norm_rows(hidden, vectors[7:8, :], vectors[5:6, :])
    normed_out[here, :] = normed.astype(bf16)
    inverse_out[here, :] = inverse
    leaving_out[here, :] = full.astype(bf16)


def attend_kernel(
    lengths, tokens, attn, merge, up, biases, gains, unit,
    mixed_out, context_out, totals, attn_out, merge_out, up_out, vectors, units,
    attn_all, merge_all, up_all, mixed, context,
    attn_mine, merge_mine, up_mine, attn_pair, merge_pair, up_pair,
    send, recv, swap_send, swap_recv, local,
):
    at = Place()
    rows = attn.shape[0]
    own = pl.ds(pl.multiple_of(at.c * rows, 8), rows)
    lanes = attn.shape[1] // 2
    sources = (attn, merge, up)
    mine = (attn_mine, merge_mine, up_mine)
    pairs = (attn_pair, merge_pair, up_pair)
    gathered = (attn_all, merge_all, up_all)
    for ref, to_send, pair in zip(sources, mine, pairs):
        width = ref.shape[1] // 2
        to_send[:, :width] = take_half(ref, 1 - at.c)
        pair[own, :width] = take_half(ref, at.c)
    attn_mine[:, lanes:] = jnp.zeros((rows, SMALL), f32)
    attn_mine[0:8, lanes : lanes + rows] = jnp.concatenate(
        [biases[...].astype(f32), gains[...].astype(f32)], axis=0
    )
    attn_mine[8:9, lanes : lanes + unit.shape[1]] = unit[...].astype(f32)
    attn_pair[own, lanes:] = attn_mine[:, lanes:]
    at.greet()
    swaps = []
    for k in range(3):
        swaps.append(
            remote(mine[k], pairs[k].at[own], swap_send.at[k], swap_recv.at[k], at.sibling())
        )
        swaps[-1].start()
    chunks = []
    for k in range(3):
        chunks.append(Gather(at, *wide_block(gathered[k]), send.at[k], recv.at[k]))

    def begin(k):
        swaps[k].wait_recv()
        gathered[k][at.c, at.z, at.x, at.y] = pairs[k][...].astype(bf16)
        chunks[k].arrive(0)

    begin(0)
    for j in range(1, 4):
        chunks[0].arrive(j)
        chunks[0].turn(j - 1)
    chunks[0].turn(3)
    begin(1)
    begin(2)
    for j in range(4):
        chunks[0].share(j)
    for j in range(4):
        chunks[0].settle(j)
    unpack_small(attn_all, vectors, units, rows)
    slots = lengths.shape[0]
    length = tokens.shape[0] // slots
    features = tokens.shape[1]
    full = attn_all.shape[-1]

    def columns(half, start, size):
        return attn_all[half, :, :, :, :, start : start + size].reshape(features, size)

    for slot in range(slots):
        project_slot(tokens, columns, vectors, mixed, slot, length)
    saves = [
        pltpu.make_async_copy(src, dst, local.at[k])
        for k, (src, dst) in enumerate(
            ((attn_all, attn_out), (mixed, mixed_out), (context, context_out), (merge_all, merge_out), (up_all, up_out))
        )
    ]
    saves[0].start()
    saves[1].start()
    plan = {
        0: (("arrive", 1),),
        1: (("turn", 0),),
        2: (("arrive", 2),),
        3: (("turn", 1),),
        4: (("arrive", 3), ("turn", 2)),
        6: (("turn", 3), ("share", 0)),
        8: (("share", 1),),
        10: (("share", 2),),
    }

    def one(i, carry):
        for when, events in plan.items():

            @pl.when(i == when)
            def _():
                for event, j in events:
                    for chunk in chunks[1:]:
                        getattr(chunk, event)(j)

        slot, pair = lax.div(i, 6), lax.rem(i, 6)
        used = jnp.where(slot == 0, lengths[0], lengths[1])
        attend_pair(mixed, context, totals, slot, pair, length, used)
        return carry

    lax.fori_loop(0, 6 * slots, one, 0)
    saves[2].start()
    for chunk in chunks[1:]:
        chunk.share(3)
    for k, chunk in enumerate(chunks[1:]):
        for j in range(4):
            chunk.settle(j)
        saves[3 + k].start()
    for chunk in chunks:
        chunk.finish()
    for swap in swaps:
        swap.wait_send()
    for save in saves:
        save.wait()


def attend_forward(lengths, tokens, attn, merge, up, biases, gains, unit):
    rows, features = tokens.shape
    shard = attn.shape[0]
    slots = lengths.shape[0]
    widths = (attn.shape[1] // 2 + SMALL, merge.shape[1] // 2, up.shape[1] // 2)
    blocks = [(2, 4, 2, 2, 2 * shard, width) for width in widths]
    vmem = pl.BlockSpec(memory_space=pltpu.VMEM)
    anywhere = pl.BlockSpec(memory_space=pl.ANY)

    def shape(*dims, kind=bf16):
        return jax.ShapeDtypeStruct(dims, kind)

    return pl.pallas_call(
        attend_kernel,
        out_shape=[
            shape(rows, 3 * features),
            shape(rows, features),
            shape(slots, features // HD, rows // slots, kind=f32),
            *[shape(*block) for block in blocks],
            shape(8, features, kind=f32),
            shape(8, up.shape[1], kind=f32),
        ],
        in_specs=[pl.BlockSpec(memory_space=pltpu.SMEM)] + [vmem] * 7,
        out_specs=[anywhere, anywhere, vmem, anywhere, anywhere, anywhere, vmem, vmem],
        scratch_shapes=[pltpu.VMEM(block, bf16) for block in blocks]
        + [pltpu.VMEM((rows, 3 * features), bf16), pltpu.VMEM((rows, features), bf16)]
        + [pltpu.VMEM((shard, width), f32) for width in widths]
        + [pltpu.VMEM((2 * shard, width), f32) for width in widths]
        + [
            pltpu.SemaphoreType.DMA((3, Gather.SEMS)),
            pltpu.SemaphoreType.DMA((3, Gather.SEMS)),
            pltpu.SemaphoreType.DMA((3,)),
            pltpu.SemaphoreType.DMA((3,)),
            pltpu.SemaphoreType.DMA((5,)),
        ],
        compiler_params=pltpu.CompilerParams(
            collective_id=0, has_side_effects=True, vmem_limit_bytes=48 << 20
        ),
        cost_estimate=pl.CostEstimate(
            flops=2 * rows * features * 3 * features * 4, bytes_accessed=100 << 20, transcendentals=0
        ),
    )(lengths, tokens, attn, merge, up, biases, gains, unit.reshape(1, -1))


def feed_kernel(
    tokens, context, merge, up_in, vectors, units, down,
    normed_one, inverse_one, low, active_out, slope_out, normed_two, inverse_two, leaving, down_out,
    up, active, slope, first, down_all, send, recv, local,
):
    at = Place()
    fetch = pltpu.make_async_copy(up_in, up, local.at[0])
    fetch.start()
    chunk = Gather(at, *tall_block(down_all), send, recv)
    down_all[at.z, at.x, at.y, at.c] = down[...]
    at.greet()
    chunk.arrive(0)
    rows, features = tokens.shape
    size = rows // 4

    def merge_half(half):
        return merge[half].reshape(features, merge.shape[-1])

    def up_part(half, start, width):
        return up[half, :, :, :, :, start : start + width].reshape(features, width)

    fetch.wait()

    def one(r, carry):
        for when in range(4):

            @pl.when(r == when)
            def _():
                if when > 0:
                    chunk.arrive(when)
                    chunk.turn(when - 1)

        first_rows(
            tokens, context, merge_half, up_part, vectors, units, first, None,
            (normed_one, inverse_one, low, active, slope), r, size,
        )
        return carry

    lax.fori_loop(0, 4, one, 0)
    saves = [
        pltpu.make_async_copy(src, dst, local.at[k + 1])
        for k, (src, dst) in enumerate(((active, active_out), (slope, slope_out), (down_all, down_out)))
    ]
    saves[0].start()
    saves[1].start()
    chunk.turn(3)
    for j in range(4):
        chunk.share(j)
    for j in range(4):
        chunk.settle(j)
    saves[2].start()

    def two(r, carry):
        here = rows_of(r, size)
        branch = jnp.dot(
            active[here, :], down_all[...].reshape(-1, features), preferred_element_type=f32
        )
        hidden = first[here, :] + (branch + vectors[4:5, :])
        full, normed, inverse = norm_rows(hidden, vectors[7:8, :], vectors[5:6, :])
        normed_two[here, :] = normed.astype(bf16)
        inverse_two[here, :] = inverse
        leaving[here, :] = full.astype(bf16)
        return carry

    lax.fori_loop(0, 4, two, 0)
    chunk.finish()
    for save in saves:
        save.wait()


def feed_forward(tokens, context, merge, up, vectors, units, down):
    rows, features = tokens.shape
    hidden = units.shape[1]
    vmem = pl.BlockSpec(memory_space=pltpu.VMEM)
    anywhere = pl.BlockSpec(memory_space=pl.ANY)
    block = (4, 2, 2, 2) + down.shape

    def shape(*dims, kind=bf16):
        return jax.ShapeDtypeStruct(dims, kind)

    return pl.pallas_call(
        feed_kernel,
        out_shape=[
            shape(rows, features),
            shape(rows, 1, kind=f32),
            shape(rows, features),
            shape(rows, hidden),
            shape(rows, hidden),
            shape(rows, features),
            shape(rows, 1, kind=f32),
            shape(rows, features),
            shape(*block),
        ],
        in_specs=[vmem, vmem, vmem, anywhere, vmem, vmem, vmem],
        out_specs=[vmem, vmem, vmem, anywhere, anywhere, vmem, vmem, vmem, anywhere],
        scratch_shapes=[
            pltpu.VMEM(up.shape, bf16),
            pltpu.VMEM((rows, hidden), bf16),
            pltpu.VMEM((rows, hidden), bf16),
            pltpu.VMEM((rows, features), f32),
            pltpu.VMEM(block, bf16),
            pltpu.SemaphoreType.DMA((Gather.SEMS,)),
            pltpu.SemaphoreType.DMA((Gather.SEMS,)),
            pltpu.SemaphoreType.DMA((4,)),
        ],
        compiler_params=pltpu.CompilerParams(
            collective_id=1, has_side_effects=True, vmem_limit_bytes=56 << 20
        ),
        cost_estimate=pl.CostEstimate(
            flops=2 * rows * features * (2 * hidden + features),
            bytes_accessed=40 << 20,
            transcendentals=0,
        ),
    )(tokens, context, merge, up, vectors, units, down)


def exact(left, right, over_left=1, over_right=0):
    return lax.dot_general(
        left,
        right,
        (((over_left,), (over_right,)), ((), ())),
        precision=precise,
        preferred_element_type=f32,
    )


def rows_sum(values):
    return jnp.sum(values, axis=0, keepdims=True)


def pile(rows):
    width = rows[0].shape[1]
    count = sum(r.shape[0] for r in rows)
    return jnp.concatenate(rows + [jnp.zeros((8 - count, width), f32)], axis=0)


def student_slots(
    leaving, proj, pool, dense, label, student_bias, logit_bias, grad_logits, lengths,
    logits, low_grad, pack,
):
    slots = lengths.shape[0]
    length = leaving.shape[0] // slots
    half = proj.shape[1] // SH
    low = lax.broadcasted_iota(jnp.int32, (1, proj.shape[1]), 1) < half
    scale = 1.0 / math.sqrt(half)
    left, right = [[] for _ in range(5)], [[] for _ in range(5)]
    sums, outs = [], []

    def by_head(row):
        return jnp.concatenate([jnp.where(low, row, 0.0), jnp.where(low, 0.0, row)], axis=0)

    def one_row(two):
        return jnp.where(low, two[0:1], two[1:2])

    for slot in range(slots):
        here = pl.ds(slot * length, length)
        projected = jnp.dot(leaving[here, :], proj[...], preferred_element_type=f32)
        projected = projected + student_bias[0:1, :]
        valid = lax.broadcasted_iota(jnp.int32, (length, 1), 0) < lengths[slot]
        start = projected[0:1]
        query = exact(start, pool[0])
        queries = by_head(query)
        asks = exact(queries, pool[1], 1, 1)
        shares, means = [], []
        for h in range(SH):
            scores = jnp.sum(projected * asks[h : h + 1], axis=1, keepdims=True) * scale
            scores = jnp.where(valid, scores, neg_big)
            powers = jnp.exp(scores - jnp.max(scores, axis=0, keepdims=True))
            shares.append(powers / rows_sum(powers))
            means.append(rows_sum(shares[h] * projected))
        mean_rows = jnp.concatenate(means, axis=0)
        pooled = one_row(exact(mean_rows, pool[2]))
        active = jnp.tanh(exact(pooled, dense[...]) + student_bias[1:2, :])
        outs.append(exact(active, label[...]) + logit_bias[...])
        g_logits = grad_logits[slot : slot + 1, :]
        g_pre = exact(g_logits, label[...], 1, 1) * (1.0 - active * active)
        g_pooled = by_head(exact(g_pre, dense[...], 1, 1))
        g_means = exact(g_pooled, pool[2], 1, 1)
        g_projected = jnp.zeros_like(projected)
        g_asks = []
        for h in range(SH):
            g_share = jnp.sum(projected * g_means[h : h + 1], axis=1, keepdims=True)
            g_score = shares[h] * (g_share - rows_sum(g_share * shares[h])) * scale
            g_projected = g_projected + shares[h] * g_means[h : h + 1] + g_score * asks[h : h + 1]
            g_asks.append(rows_sum(g_score * projected))
        g_ask_rows = jnp.concatenate(g_asks, axis=0)
        g_query = one_row(exact(g_ask_rows, pool[1]))
        first = lax.broadcasted_iota(jnp.int32, (length, 1), 0) == 0
        g_projected = g_projected + jnp.where(first, exact(g_query, pool[0], 1, 1), 0.0)
        low_grad[here, :] = g_projected.astype(bf16)
        sums.append((rows_sum(g_projected), g_pre, g_logits))
        for k, (a, b) in enumerate(
            (
                (start, g_query),
                (g_ask_rows, queries),
                (mean_rows, g_pooled),
                (pooled, g_pre),
                (g_logits, active),
            )
        ):
            left[k].append(a)
            right[k].append(b)
    features, lanes = proj.shape
    pack[0:features, :] = dots(leaving[...], low_grad[...], 0, 0)
    for k in range(5):
        grad = exact(pile(left[k]), pile(right[k]), 0, 0)
        row = features + k * lanes
        size = lanes if k < 4 else 16
        pack[row : row + size, :] = grad[:size]
    row = features + 4 * lanes + 16
    pack[row : row + 8, :] = pile([sum(s[k] for s in sums) for k in range(3)])
    logits[...] = pile(outs)


def norm_back(grad, normed, inverse, gain):
    scaled = grad * gain
    return inverse * (
        scaled
        - jnp.mean(scaled, axis=-1, keepdims=True)
        - normed * jnp.mean(scaled * normed, axis=-1, keepdims=True)
    )


def rows_kernel(
    lengths, leaving, proj, pool, dense, label, student_bias, logit_bias, grad_logits,
    merge, up, down, vectors, grad_leaving, normed_one, inverse_one, normed_two, inverse_two,
    slope,
    logits, pack, mid_low, inner_low, res, res_low, grad_context,
    proj_low, sums, unit_sum,
):
    step = pl.program_id(0)
    size = grad_leaving.shape[0]

    @pl.when(step == 0)
    def _():
        student_slots(
            leaving, proj, pool, dense, label, student_bias, logit_bias, grad_logits, lengths,
            logits, proj_low, pack,
        )
        sums[...] = jnp.zeros_like(sums)
        unit_sum[...] = jnp.zeros_like(unit_sum)

    grad_second = grad_leaving[...].astype(f32) + dots(proj_low[rows_of(step, size), :], proj[...], 1, 1)
    two = normed_two[...].astype(f32)
    grad_mid = norm_back(grad_second, two, inverse_two[...], vectors[7:8, :])
    mid = grad_mid.astype(bf16)
    mid_low[...] = mid
    width = up.shape[2]
    grad_first = grad_mid
    for half in range(2):
        for part in range(2):
            cols = pl.ds(half * width + part * (width // 2), width // 2)
            inside = pl.ds(part * (width // 2), width // 2)
            inner = dots(mid, down[cols, :], 1, 1) * slope[:, cols].astype(f32)
            unit_sum[0:1, cols] += rows_sum(inner)
            inner = inner.astype(bf16)
            inner_low[:, cols] = inner
            grad_first = grad_first + dots(inner, up[half, :, inside], 1, 1)
    one = normed_one[...].astype(f32)
    grad_res = norm_back(grad_first, one, inverse_one[...], vectors[6:7, :])
    res[...] = grad_res
    low = grad_res.astype(bf16)
    res_low[...] = low
    narrow = merge.shape[2]
    grad_context[...] = (
        dots(low[:, :narrow], merge[0], 1, 1) + dots(low[:, narrow:], merge[1], 1, 1)
    ).astype(bf16)
    sums[...] += jnp.concatenate(
        [
            jnp.zeros((2, grad_res.shape[1]), f32),
            rows_sum(grad_res),
            rows_sum(grad_first),
            rows_sum(grad_mid),
            rows_sum(grad_second),
            rows_sum(grad_first * one),
            rows_sum(grad_second * two),
        ],
        axis=0,
    )

    @pl.when(step == pl.num_programs(0) - 1)
    def _():
        row = pack.shape[0] - 72
        for t in range(6):
            pack[row + 8 * t : row + 8 * t + 8, :] = sums[:, 128 * t : 128 * t + 128]
        pack[row + 48 : row + 72, :] = unit_sum[0:1, :].reshape(24, 128)


def rows_backward(lengths, leaving, student, grad_logits, weights, vectors, grad_leaving, saved):
    proj, pool, dense, label, student_bias, logit_bias = student
    merge, up, down = weights
    normed_one, inverse_one, normed_two, inverse_two, slope = saved
    rows, features = leaving.shape
    hidden = down.shape[0]
    size = rows // 4
    lanes = proj.shape[1]
    label_lanes = jnp.pad(label, ((0, 0), (0, lanes - label.shape[1])))
    logit_lanes = jnp.pad(logit_bias, (0, lanes - label.shape[1])).reshape(1, lanes)
    grad_lanes = jnp.pad(grad_logits, ((0, 0), (0, lanes - label.shape[1])))

    def fixed(array):
        return pl.BlockSpec(array.shape, lambda i, n=array.ndim: (0,) * n, pipeline_mode=pl.Buffered(1))

    def by_rows(array):
        return pl.BlockSpec((size, array.shape[1]), lambda i: (i, 0))

    def shape(*dims, kind=f32):
        return jax.ShapeDtypeStruct(dims, kind)

    whole_in = (leaving, proj, pool, dense, label_lanes, student_bias, logit_lanes, grad_lanes, merge, up, down, vectors)
    row_in = (grad_leaving, normed_one, inverse_one, normed_two, inverse_two, slope)
    whole_out = (
        shape(8, lanes), shape(features + 4 * lanes + 24 + 72, lanes),
    )
    row_out = (
        shape(rows, features, kind=bf16), shape(rows, hidden, kind=bf16), shape(rows, features),
        shape(rows, features, kind=bf16), shape(rows, features, kind=bf16),
    )
    return pl.pallas_call(
        rows_kernel,
        grid=(4,),
        out_shape=whole_out + row_out,
        in_specs=[pl.BlockSpec(memory_space=pltpu.SMEM)]
        + [fixed(a) for a in whole_in]
        + [by_rows(a) for a in row_in],
        out_specs=[fixed(a) for a in whole_out] + [by_rows(a) for a in row_out],
        scratch_shapes=[
            pltpu.VMEM((rows, lanes), bf16),
            pltpu.VMEM((8, features), f32),
            pltpu.VMEM((8, hidden), f32),
        ],
        compiler_params=pltpu.CompilerParams(
            dimension_semantics=("arbitrary",), vmem_limit_bytes=56 << 20
        ),
        cost_estimate=pl.CostEstimate(
            flops=2 * rows * features * (2 * hidden + features),
            bytes_accessed=40 << 20,
            transcendentals=0,
        ),
    )(lengths, *whole_in, *row_in)


def attend_back_pair(mixed, grad_context, totals, sums, slot, pair, length, used, features):
    here = rows_of(slot, length)
    base = pl.multiple_of(pair * 128, 128)
    spots = [pl.ds(pl.multiple_of(base + k * features, 128), 128) for k in range(3)]
    two_q, two_k, two_v = (mixed[here, spot] for spot in spots)
    two_g = grad_context[here, pl.ds(base, 128)]
    low = lax.broadcasted_iota(jnp.int32, two_k.shape, 1) < HD
    valid = lax.broadcasted_iota(jnp.int32, (length, 1), 0) < used
    none = jnp.zeros_like(two_k)
    scale = jnp.asarray(HD ** (-0.5), bf16)
    two_q = two_q * scale
    small_k = two_k * scale
    outs = [[], [], []]
    for head in range(2):
        side = low if head == 0 else ~low
        scores = dots(jnp.where(side, two_k, none), two_q, 1, 1)
        probs = jnp.where(valid, jnp.exp(scores - totals[slot, pl.ds(2 * pair + head, 1), :]), 0.0)
        grad_probs = dots(jnp.where(side, two_v, none), two_g, 1, 1)
        shared = jnp.sum(grad_probs * probs, axis=0, keepdims=True)
        grad_scores = (probs * (grad_probs - shared)).astype(bf16)
        outs[0].append(dots(grad_scores, small_k, 0, 0))
        outs[1].append(jnp.dot(grad_scores, two_q, preferred_element_type=f32))
        outs[2].append(jnp.dot(probs.astype(bf16), two_g, preferred_element_type=f32))
    for k in range(3):
        grad = jnp.where(low, outs[k][0], outs[k][1])
        mixed[here, spots[k]] = grad.astype(bf16)
        if k != 1:
            sums[k // 2 : k // 2 + 1, pl.ds(base, 128)] += rows_sum(grad)


def close_kernel(
    lengths, totals, pack, mixed_in, grad_context_in, tokens_in, attn_in, res_in,
    active_in, inner_in, mid_in, low_in, context_in, res_low_in,
    grad_inputs, attn_out, merge_out, up_out, down_out, small_out,
    *scratch,
):
    at = Place()
    (
        mixed, attn, tiles, mid, low, context, res_low, bias_sums,
        small_low, small_got, small_sum, attn_total, merge_total, up_total,
        local, tile_sems, small_send, small_recv, swap_send, swap_recv, send, recv,
    ) = scratch[-22:]
    chunks = []
    for k in range(4):
        grad, from_core, from_second, from_first, from_line = scratch[5 * k : 5 * k + 5]
        block, line = (tall_block if k == 3 else wide_block)(grad)
        chunks.append(
            Scatter(
                at, block, line, from_core, from_second, from_first, from_line,
                send.at[k], recv.at[k],
            )
        )
    grads = [scratch[5 * k] for k in range(4)]
    on_attn, on_merge, on_up, on_down = chunks
    features = mid.shape[1]
    slots = lengths.shape[0]
    length = mixed.shape[0] // slots
    tile_lanes = tiles.shape[2]
    steps = inner_in.shape[1] // tile_lanes

    def load(k, src, dst):
        copy = pltpu.make_async_copy(src, dst, local.at[k])
        copy.start()
        return copy

    def tile(src, t):
        return pltpu.make_async_copy(
            src.at[:, lanes_of(t, tile_lanes)], tiles.at[lax.rem(t, 2)], tile_sems.at[lax.rem(t, 2)]
        )

    mid_load = load(0, mid_in, mid)
    tile(active_in, 0).start()
    low_load = load(1, low_in, low)
    context_load = load(2, context_in, context)
    res_low_load = load(3, res_low_in, res_low)
    mixed_load = load(4, mixed_in, mixed)
    res_load = load(5, res_in, grad_inputs)
    attn_load = load(6, attn_in, attn)
    at.greet(far=True)

    mid_load.wait()

    def down_tile(t, carry):
        tile(active_in, t).wait()

        @pl.when(t + 1 < steps)
        def _():
            tile(active_in, t + 1).start()

        part = dots(tiles[lax.rem(t, 2)], mid[...], 0, 0).astype(bf16)
        grads[3][lax.div(t, 2), lax.rem(t, 2)] = part.reshape(2, 2, part.shape[0] // 4, features)

        @pl.when(lax.rem(t, 2) == 1)
        def _():
            on_down.across(lax.div(t, 2)).start()

        return carry

    lax.fori_loop(0, steps, down_tile, 0)
    tokens_load = load(7, tokens_in, mid)
    low_load.wait()
    half_steps = steps // 2

    def up_source(t):
        half = (1 - at.c) * (1 - lax.div(t, half_steps)) + at.c * lax.div(t, half_steps)
        return half, half * half_steps + lax.rem(t, half_steps)

    def up_fetch(t):
        return pltpu.make_async_copy(
            inner_in.at[:, lanes_of(up_source(t)[1], tile_lanes)],
            tiles.at[lax.rem(t, 2)],
            tile_sems.at[lax.rem(t, 2)],
        )

    up_fetch(0).start()

    def up_tile(t, carry):
        up_fetch(t).wait()

        @pl.when(t + 1 < steps)
        def _():
            up_fetch(t + 1).start()

        part = dots(low[...], tiles[lax.rem(t, 2)], 0, 0).astype(bf16)
        half = up_source(t)[0]
        grads[2][half, :, :, :, :, lanes_of(lax.rem(t, half_steps), tile_lanes)] = part.reshape(
            4, 2, 2, -1, tile_lanes
        )
        for when in range(4):

            @pl.when(t == when + 1)
            def _():
                on_down.join(3 - when)

        @pl.when(t == half_steps - 1)
        def _():
            for j in (3, 2, 1, 0):
                on_up.give(j)

        return carry

    lax.fori_loop(0, steps, up_tile, 0)
    context_load.wait()
    res_low_load.wait()
    narrow = res_low.shape[1] // 2
    for half in range(2):
        part = dots(context[...], res_low[:, half * narrow : (half + 1) * narrow], 0, 0)
        grads[1][half] = part.astype(bf16).reshape(4, 2, 2, -1, narrow)
    for j in (3, 2, 1, 0):
        on_merge.give(j)
    context_again = load(8, grad_context_in, low)
    bias_sums[...] = jnp.zeros_like(bias_sums)
    mixed_load.wait()
    context_again.wait()
    plan = {
        0: ((on_up, "join", 3),),
        1: ((on_up, "join", 2),),
        2: ((on_up, "join", 1), (on_up, "join", 0)),
        3: ((on_down, "halve", 3), (on_down, "halve", 2)),
        4: ((on_down, "halve", 1), (on_down, "halve", 0)),
        5: tuple((on_merge, "join", j) for j in (3, 2, 1, 0)),
        6: ((on_down, "leave", 3),),
        7: ((on_down, "leave", 2),),
        8: ((on_down, "leave", 1), (on_up, "halve", 3)),
        9: ((on_up, "halve", 2), (on_down, "leave", 0)),
        10: ((on_up, "halve", 1), (on_up, "halve", 0)),
        11: tuple((on_merge, "halve", j) for j in (3, 2, 1, 0)),
    }

    def one(i, carry):
        for when, events in plan.items():

            @pl.when(i == when)
            def _():
                for chunk, event, j in events:
                    getattr(chunk, event)(j)

        slot, pair = lax.div(i, 6), lax.rem(i, 6)
        used = jnp.where(slot == 0, lengths[0], lengths[1])
        attend_back_pair(mixed, low, totals, bias_sums, slot, pair, length, used, features)
        return carry

    lax.fori_loop(0, 6 * slots, one, 0)
    tokens_load.wait()
    wide = mixed.shape[1] // 2
    third = wide // 3

    def attn_part(p, carry):
        half = (1 - at.c) * (1 - lax.div(p, 3)) + at.c * lax.div(p, 3)
        cols = lanes_of(half * 3 + lax.rem(p, 3), third)
        part = dots(mid[...], mixed[:, cols], 0, 0).astype(bf16)
        grads[0][half, :, :, :, :, lanes_of(lax.rem(p, 3), third)] = part.reshape(
            4, 2, 2, -1, third
        )

        @pl.when(p == 2)
        def _():
            for j in (3, 2, 1, 0):
                on_attn.give(j)

        @pl.when(p == 3)
        def _():
            on_up.leave(3)

        @pl.when(p == 4)
        def _():
            on_up.leave(2)

        return carry

    lax.fori_loop(0, 6, attn_part, 0)
    small_rows = small_low.shape[1]
    middle = pack.shape[0] - 72

    def small_step(k, device):
        return remote(small_low.at[k], small_got.at[k], small_send.at[k], small_recv.at[k], device)

    partners = (
        at.sibling(),
        at.device(y=1 - at.y),
        at.device(x=1 - at.x),
        at.device(z=at.z + 1 - 2 * lax.rem(at.z, 2)),
        at.device(z=lax.rem(at.z + 2, 4)),
    )
    for half in range(2):
        from_row = half * small_rows
        part = pack[from_row : from_row + small_rows, :]
        if half == 1:
            inside = middle - from_row
            gained = [part[:inside]]
            for t in range(6):
                tile_rows = part[inside + 8 * t : inside + 8 * t + 8]
                gained.append(tile_rows + bias_sums[:, 128 * t : 128 * t + 128])
            gained.append(part[inside + 48 :])
            part = jnp.concatenate(gained, axis=0)
        part = part.astype(bf16)
        here = half == at.c

        @pl.when(here)
        def _():
            small_sum[...] = part.astype(f32)

        @pl.when(jnp.logical_not(here))
        def _():
            small_low[0] = part

    small_step(0, partners[0]).start()

    def small_next(k):
        small_step(k, partners[k]).wait_recv()
        small_sum[...] = small_sum[...] + small_got[k].astype(f32)
        if k < 4:
            small_low[k + 1] = small_sum[...].astype(bf16)
            small_sum[...] = small_low[k + 1].astype(f32)
            small_step(k + 1, partners[k + 1]).start()

    for j in (3, 2, 1, 0):
        on_attn.join(j)
    attn_load.wait()
    res_load.wait()
    small_next(0)

    def inputs_part(r, carry):
        here = rows_of(r, length // 2)
        total = grad_inputs[here, :]
        for half in range(2):
            weight = attn[half, :, :, :, :, :wide].reshape(features, wide)
            total = total + dots(mixed[here, half * wide : (half + 1) * wide], weight, 1, 1)
        grad_inputs[here, :] = total

        @pl.when(r == 1)
        def _():
            on_up.leave(1)
            on_up.leave(0)
            small_next(1)

        @pl.when(r == 2)
        def _():
            for j in (3, 2, 1, 0):
                on_merge.leave(j)
            small_next(2)

        return carry

    lax.fori_loop(0, 2 * slots, inputs_part, 0)
    for j in (3, 2, 1, 0):
        on_attn.halve(j)
    small_next(3)
    finish_scatter(at, on_down, None, down_out, None, None, True)
    finish_scatter(at, on_up, up_total, up_out, swap_send.at[2], swap_recv.at[2], False)
    finish_scatter(at, on_merge, merge_total, merge_out, swap_send.at[1], swap_recv.at[1], False)
    for j in (3, 2, 1, 0):
        on_attn.leave(j)
    small_next(4)
    own = pl.ds(pl.multiple_of(at.c * small_rows, 8), small_rows)
    small_out[own, :] = small_sum[...]
    last = remote(small_sum, small_out.at[own], swap_send.at[3], swap_recv.at[3], at.sibling())
    last.start()
    finish_scatter(at, on_attn, attn_total, attn_out, swap_send.at[0], swap_recv.at[0], False)
    last.wait()
    for k in range(5):
        small_step(k, partners[k]).wait_send()
    for chunk in chunks:
        chunk.finish()


def close_backward(lengths, totals, pack, mixed, grad_context, tokens, attn, res, active, inner, mid, low, context, res_low, shards):
    rows, features = tokens.shape
    hidden = active.shape[1]
    vmem = pl.BlockSpec(memory_space=pltpu.VMEM)
    anywhere = pl.BlockSpec(memory_space=pl.ANY)
    scratch = []
    for k, (shard_rows, columns) in enumerate(shards):
        if k < 3:
            tall, width = 2 * shard_rows, columns // 2
            scratch.append(pltpu.VMEM((2, 4, 2, 2, tall, width), bf16))
        else:
            tall, width = shard_rows, columns
            scratch.append(pltpu.VMEM((4, 2, 2, 2, tall, width), bf16))
        scratch += [
            pltpu.VMEM((4, 2, 2, tall, width), bf16),
            pltpu.VMEM((4, 2, tall, width), bf16),
            pltpu.VMEM((4, tall, width), bf16),
            pltpu.VMEM((4, 2, tall, width), bf16),
        ]
    small_rows = pack.shape[0] // 2
    wide = [(2 * r, c // 2) for r, c in shards[:3]]
    scratch += [
        pltpu.VMEM(mixed.shape, bf16),
        pltpu.VMEM(attn.shape, bf16),
        pltpu.VMEM((2, rows, hidden // 8), bf16),
        pltpu.VMEM((rows, features), bf16),
        pltpu.VMEM((rows, features), bf16),
        pltpu.VMEM((rows, features), bf16),
        pltpu.VMEM((rows, features), bf16),
        pltpu.VMEM((8, features), f32),
        pltpu.VMEM((5, small_rows, 128), bf16),
        pltpu.VMEM((5, small_rows, 128), bf16),
        pltpu.VMEM((small_rows, 128), f32),
        *[pltpu.VMEM(w, f32) for w in wide],
        pltpu.SemaphoreType.DMA((9,)),
        pltpu.SemaphoreType.DMA((2,)),
        pltpu.SemaphoreType.DMA((5,)),
        pltpu.SemaphoreType.DMA((5,)),
        pltpu.SemaphoreType.DMA((4,)),
        pltpu.SemaphoreType.DMA((4,)),
        pltpu.SemaphoreType.DMA((4, Scatter.SEMS)),
        pltpu.SemaphoreType.DMA((4, Scatter.SEMS)),
    ]
    return pl.pallas_call(
        close_kernel,
        out_shape=[jax.ShapeDtypeStruct((rows, features), f32)]
        + [jax.ShapeDtypeStruct(shape, f32) for shape in shards]
        + [jax.ShapeDtypeStruct(pack.shape, f32)],
        in_specs=[pl.BlockSpec(memory_space=pltpu.SMEM), vmem, vmem] + [anywhere] * 11,
        out_specs=[vmem] * 6,
        scratch_shapes=scratch,
        compiler_params=pltpu.CompilerParams(
            collective_id=2, has_side_effects=True, vmem_limit_bytes=62 << 20
        ),
        cost_estimate=pl.CostEstimate(
            flops=2 * rows * features * 12 * features, bytes_accessed=60 << 20, transcendentals=0
        ),
    )(lengths, totals, pack, mixed, grad_context, tokens, attn, res, active, inner, mid, low, context, res_low)


def passed_along(block, axis, distance):
    devices = range(lax.axis_size(axis))
    route = [((i - distance) % len(devices), i) for i in devices]
    return lax.ppermute(block, axis, route)


def product(pattern, left, right):
    return jnp.einsum(pattern, left, right, preferred_element_type=jnp.float32)


def gelu_erf(values):
    return 0.5 * values * (1.0 + jax.scipy.special.erf(values * 0.7071067811865476))


def gelu_slope(values):
    return (
        0.5 * (1.0 + jax.scipy.special.erf(values * 0.7071067811865476))
        + values * jnp.exp(-0.5 * values * values) * 0.3989422804014327
    )


def norm_forward(hidden, norm_gain, norm_shift):
    centred = hidden - jnp.mean(hidden, axis=-1, keepdims=True)
    inverse = lax.rsqrt(jnp.mean(centred * centred, axis=-1, keepdims=True) + eps_norm)
    normed = centred * inverse
    return (normed * norm_gain + norm_shift, normed, inverse)


def norm_backward(grad_out, normed, inverse, norm_gain):
    scaled = grad_out * norm_gain
    return inverse * (
        scaled
        - jnp.mean(scaled, axis=-1, keepdims=True)
        - normed * jnp.mean(scaled * normed, axis=-1, keepdims=True)
    )


def student_head(
    hidden, valid_keys, pool_weight, dense_weight, label_weight, dense_bias, logit_bias
):
    groups, length, features = hidden.shape
    head_size = features // SH
    queries = jnp.einsum("bd,de->be", hidden[:, 0], pool_weight[0], precision=precise).reshape(
        groups, SH, head_size
    )
    key_rows = jnp.einsum("bld,de->ble", hidden, pool_weight[1], precision=precise).reshape(
        groups, length, SH, head_size
    )
    value_rows = jnp.einsum("bld,de->ble", hidden, pool_weight[2], precision=precise).reshape(
        groups, length, SH, head_size
    )
    scores = jnp.einsum("bhe,blhe->bhl", queries, key_rows, precision=precise) / math.sqrt(
        head_size
    )
    scores = jnp.where(valid_keys[:, None, :], scores, neg_big)
    shares = jax.nn.softmax(scores, axis=-1)
    pooled = jnp.einsum("bhl,blhe->bhe", shares, value_rows, precision=precise).reshape(
        groups, features
    )
    dense_out = jnp.tanh(jnp.dot(pooled, dense_weight, precision=precise) + dense_bias)
    return jnp.dot(dense_out, label_weight, precision=precise) + logit_bias


def layer_forward(tokens, valid_keys, weights, student):
    attn_weight, merge_weight, up_weight, down_weight, biases, norm_gains, unit_bias = weights
    proj_weight, pool_weight, dense_weight, label_weight, student_biases, logit_bias = student
    groups, length, features = tokens.shape
    mixed_proj = product("bld,de->ble", tokens, attn_weight)
    queries = (
        (mixed_proj[..., :features] + biases[0])
        .astype(jnp.bfloat16)
        .reshape(groups, length, -1, HD)
    )
    key_rows = (
        mixed_proj[..., features : 2 * features]
        .astype(jnp.bfloat16)
        .reshape(groups, length, -1, HD)
    )
    value_rows = (
        (mixed_proj[..., 2 * features :] + biases[1])
        .astype(jnp.bfloat16)
        .reshape(groups, length, -1, HD)
    )
    scores = product("bqhe,bkhe->bhqk", queries, key_rows) * HD ** (-0.5)
    scores = jnp.where(valid_keys[:, None, None, :], scores, neg_big)
    row_top = jnp.max(scores, axis=-1, keepdims=True)
    exponent = jnp.exp(scores - row_top)
    row_total = jnp.sum(exponent, axis=-1, keepdims=True)
    attn_probs = (exponent / row_total).astype(jnp.bfloat16)
    log_total = row_top + jnp.log(row_total)
    context = (
        product("bhqk,bkhe->bqhe", attn_probs, value_rows)
        .astype(jnp.bfloat16)
        .reshape(groups, length, features)
    )
    attended = product("bld,de->ble", context, merge_weight) + biases[2]
    first_norm, normed_one, inverse_one = norm_forward(
        tokens.astype(jnp.float32) + attended, norm_gains[0], biases[3]
    )
    first_low = first_norm.astype(jnp.bfloat16)
    inner_pre = product("bld,df->blf", first_low, up_weight) + unit_bias
    active = gelu_erf(inner_pre).astype(jnp.bfloat16)
    branch_out = product("blf,fd->bld", active, down_weight) + biases[4]
    second, normed_two, inverse_two = norm_forward(
        first_norm + branch_out, norm_gains[1], biases[5]
    )
    leaving = second.astype(jnp.bfloat16)
    projected = product("bld,de->ble", leaving, proj_weight) + student_biases[0]

    def classify(hidden, attn_part, dense_part, label_part, dense_bias, class_bias):
        return student_head(
            hidden, valid_keys, attn_part, dense_part, label_part, dense_bias, class_bias
        )

    logits, pull_back = jax.vjp(
        classify, projected, pool_weight, dense_weight, label_weight, student_biases[1], logit_bias
    )
    saved_state = (
        tokens,
        valid_keys,
        queries,
        key_rows,
        value_rows,
        log_total,
        context,
        normed_one,
        inverse_one,
        first_low,
        inner_pre,
        active,
        normed_two,
        inverse_two,
        leaving,
        pull_back,
    )
    return (leaving, logits, saved_state)


def layer_backward(saved_state, grad_leaving, grad_logits, weights, proj_weight):
    (
        tokens,
        valid_keys,
        queries,
        key_rows,
        value_rows,
        log_total,
        context,
        normed_one,
        inverse_one,
        first_low,
        inner_pre,
        active,
        normed_two,
        inverse_two,
        leaving,
        pull_back,
    ) = saved_state
    attn_weight, merge_weight, up_weight, down_weight, biases, norm_gains, unit_bias = weights
    groups, length, features = tokens.shape
    grad_proj, grad_pool, grad_dense, grad_label, grad_dense_bias, grad_logit_bias = pull_back(
        grad_logits
    )
    proj_low = grad_proj.astype(jnp.bfloat16)
    grad_proj_weight = product("bld,ble->de", leaving, proj_low)
    grad_second = grad_leaving + product("ble,de->bld", proj_low, proj_weight)
    grad_mid = norm_backward(grad_second, normed_two, inverse_two, norm_gains[1])
    down_low = grad_mid.astype(jnp.bfloat16)
    grad_down = product("blf,bld->fd", active, down_low)
    grad_inner = product("bld,fd->blf", down_low, down_weight) * gelu_slope(inner_pre)
    inner_low = grad_inner.astype(jnp.bfloat16)
    grad_up = product("bld,blf->df", first_low, inner_low)
    grad_first = grad_mid + product("blf,df->bld", inner_low, up_weight)
    grad_res = norm_backward(grad_first, normed_one, inverse_one, norm_gains[0])
    res_low = grad_res.astype(jnp.bfloat16)
    grad_merge = product("blc,bld->cd", context, res_low)
    grad_context = (
        product("bld,cd->blc", res_low, merge_weight)
        .astype(jnp.bfloat16)
        .reshape(groups, length, -1, HD)
    )
    scores = product("bqhe,bkhe->bhqk", queries, key_rows) * HD ** (-0.5)
    scores = jnp.where(valid_keys[:, None, None, :], scores, neg_big)
    attn_probs = jnp.exp(scores - log_total)
    grad_values = product("bhqk,bqhe->bkhe", attn_probs.astype(jnp.bfloat16), grad_context)
    grad_probs = product("bqhe,bkhe->bhqk", grad_context, value_rows)
    grad_scores = (
        attn_probs * (grad_probs - jnp.sum(grad_probs * attn_probs, axis=-1, keepdims=True))
    ).astype(jnp.bfloat16)
    grad_queries = product("bhqk,bkhe->bqhe", grad_scores, key_rows) * HD ** (-0.5)
    grad_keys = product("bhqk,bqhe->bkhe", grad_scores, queries) * HD ** (-0.5)
    grad_queries = grad_queries.reshape(groups, length, features)
    grad_values = grad_values.reshape(groups, length, features)
    grad_mixed = jnp.concatenate(
        [grad_queries, grad_keys.reshape(groups, length, features), grad_values], axis=-1
    )
    mixed_low = grad_mixed.astype(jnp.bfloat16)
    grad_attn = product("bld,ble->de", tokens, mixed_low)
    grad_tokens = grad_res + product("ble,de->bld", mixed_low, attn_weight)
    grad_biases = jnp.stack(
        [
            jnp.sum(grad_queries, axis=(0, 1)),
            jnp.sum(grad_values, axis=(0, 1)),
            jnp.sum(grad_res, axis=(0, 1)),
            jnp.sum(grad_first, axis=(0, 1)),
            jnp.sum(grad_mid, axis=(0, 1)),
            jnp.sum(grad_second, axis=(0, 1)),
        ]
    )
    grad_gains = jnp.stack(
        [
            jnp.sum(grad_first * normed_one, axis=(0, 1)),
            jnp.sum(grad_second * normed_two, axis=(0, 1)),
        ]
    )
    grad_unit = jnp.sum(grad_inner, axis=(0, 1))
    grad_student_biases = jnp.stack([jnp.sum(grad_proj, axis=(0, 1)), grad_dense_bias])
    layer_terms = (grad_attn, grad_merge, grad_up, grad_down, grad_biases, grad_gains, grad_unit)
    student_terms = (
        grad_proj_weight,
        grad_pool,
        grad_dense,
        grad_label,
        grad_student_biases,
        grad_logit_bias,
    )
    return (grad_tokens, layer_terms, student_terms)


BOTH = ("batch", "zero")


def swapped(pair, straight):
    return jnp.where(straight, pair[0], pair[1]), jnp.where(straight, pair[1], pair[0])


def shifted(block, distance):
    return passed_along(block, "batch", distance)


def by_steps(far, other, steps, sign):
    for step in steps:
        moved = shifted(far, sign * step)
        far = jnp.where(other // step % 2 == 1, moved, far)
    return far


def by_choice(far, other, sign):
    moved = [far] + [shifted(far, sign * step) for step in (2, 4, 6)]
    even = other // 2 % 4
    low = jnp.where(even == 1, moved[1], moved[0])
    return jnp.where(even >= 2, jnp.where(even == 2, moved[2], moved[3]), low)


def routing(routes, slot_count):
    batch_count, zero_count = lax.axis_size("batch"), lax.axis_size("zero")
    offsets = routes // (slot_count * zero_count) - lax.axis_index("batch")
    offsets = (offsets + batch_count) % batch_count
    one_back = offsets[0] == batch_count - 1
    lands_first = routes[0] % slot_count == 0
    return one_back, lands_first, jnp.where(one_back, offsets[1], offsets[0])


def on_device_linked(
    inputs, lengths, exits, routes, attn_weight, merge_weight, up_weight, down_weight,
    layer_biases, norm_gains, unit_bias, proj_weight, pool_weight, dense_weight,
    label_weight, student_biases, logit_bias, grad_act, grad_logits,
):
    slot_count, length, features = inputs.shape
    rows = slot_count * length
    sent = exits > LAYER
    one_back, lands_first, other = routing(routes, slot_count)
    near, far = swapped(swapped(grad_act, lands_first), one_back)
    near = shifted(near, 1)
    far = by_choice(far, other, -1)
    tokens = inputs.reshape(rows, features)
    mixed, context, totals, attn_all, merge_all, up_all, vectors, units = attend_forward(
        lengths, tokens, attn_weight, merge_weight, up_weight, layer_biases, norm_gains, unit_bias
    )
    far = by_steps(far, other, (1,), -1)
    (
        normed_one, inverse_one, first_low, active, slope, normed_two, inverse_two, leaving, down_all
    ) = feed_forward(tokens, context, merge_all, up_all, vectors, units, down_weight)
    grad_leaving = jnp.stack(swapped((near, far), one_back))
    grad_leaving = jnp.where(sent[:, None, None], grad_leaving, 0).reshape(rows, features)
    pieces = leaving.reshape(slot_count, length, features)
    pieces = jnp.where(sent[:, None, None], pieces, 0)
    near, far = swapped(pieces, one_back)
    near = shifted(near, -1)
    far = by_steps(far, other, (1,), 1)
    logits, pack, mid_low, inner_low, res, res_low, grad_context = rows_backward(
        lengths,
        leaving,
        (proj_weight, pool_weight, dense_weight, label_weight, student_biases, logit_bias),
        grad_logits,
        (
            merge_all.reshape(2, features, -1),
            up_all.reshape(2, features, -1),
            down_all.reshape(-1, features),
        ),
        vectors,
        grad_leaving,
        (normed_one, inverse_one, normed_two, inverse_two, slope),
    )
    far = by_choice(far, other, 1)
    landed = swapped((near, far), one_back)
    arrived = jnp.stack(swapped(landed, lands_first))
    shards = [w.shape for w in (attn_weight, merge_weight, up_weight, down_weight)]
    grad_tokens, attn_grad, merge_grad, up_grad, down_grad, small = close_backward(
        lengths, totals, pack, mixed, grad_context, tokens, attn_all, res, active, inner_low,
        mid_low, first_low, context, res_low, shards,
    )
    lanes = proj_weight.shape[1]
    classes = label_weight.shape[1]
    row = features + 4 * lanes
    tail = row + 24
    mine = lax.axis_index("batch") * lax.axis_size("zero") + lax.axis_index("zero")
    vector_grads = small[tail : tail + 48].reshape(6, 8, 128).transpose(1, 0, 2).reshape(8, features)
    shard = features // (lax.axis_size("batch") * lax.axis_size("zero"))
    vector_grads = lax.dynamic_slice_in_dim(vector_grads, mine * shard, shard, 1)
    unit_grads = small[tail + 48 :].reshape(-1)
    return (
        arrived,
        logits[:slot_count, :classes],
        grad_tokens.reshape(inputs.shape),
        attn_grad,
        merge_grad,
        up_grad,
        down_grad,
        vector_grads[:6],
        vector_grads[6:],
        lax.dynamic_slice_in_dim(unit_grads, mine * unit_bias.shape[0], unit_bias.shape[0]),
        small[:features],
        small[features : features + 3 * lanes].reshape(3, lanes, lanes),
        small[features + 3 * lanes : row],
        small[row : row + classes].T,
        jnp.stack([small[row + 16], small[row + 17]]),
        small[row + 18, :classes],
    )


def whole_gather(attn, merge, up, down, biases, gains, unit):
    return (
        lax.all_gather(attn, BOTH, axis=0, tiled=True),
        lax.all_gather(merge, BOTH, axis=0, tiled=True),
        lax.all_gather(up, BOTH, axis=0, tiled=True),
        lax.all_gather(down, BOTH, axis=0, tiled=True),
        lax.all_gather(biases, BOTH, axis=1, tiled=True).astype(f32),
        lax.all_gather(gains, BOTH, axis=1, tiled=True).astype(f32),
        lax.all_gather(unit, BOTH, axis=0, tiled=True).astype(f32),
    )


def on_device(
    inputs, lengths, exits, routes, attn_weight, merge_weight, up_weight, down_weight,
    layer_biases, norm_gains, unit_bias, proj_weight, pool_weight, dense_weight,
    label_weight, student_biases, logit_bias, grad_act, grad_logits,
):
    slot_count, length, features = inputs.shape
    section_count = (lax.axis_size("batch") - 1).bit_length()
    steps = [1 << level for level in range(section_count)]
    student = (proj_weight, pool_weight, dense_weight, label_weight, student_biases, logit_bias)
    sent = exits > LAYER
    one_back, lands_first, other = routing(routes, slot_count)
    near, far = swapped(swapped(grad_act, lands_first), one_back)
    near, far = shifted(near, 1), by_steps(far, other, steps, -1)
    grad_leaving = jnp.stack(swapped((near, far), one_back)).astype(f32)
    grad_leaving = jnp.where(sent[:, None, None], grad_leaving, 0.0)
    weights = whole_gather(
        attn_weight, merge_weight, up_weight, down_weight, layer_biases, norm_gains, unit_bias
    )
    valid_all = jnp.arange(length)[None, :] < lengths[:, None]
    leaving, logits, saved_state = layer_forward(inputs, valid_all, weights, student)
    pieces = jnp.where(sent[:, None, None], leaving, jnp.zeros_like(leaving))
    near, far = swapped(pieces, one_back)
    near, far = shifted(near, -1), by_steps(far, other, steps, 1)
    arrived = jnp.stack(swapped(swapped((near, far), one_back), lands_first))
    grad_tokens, layer_sum, student_sum = layer_backward(
        saved_state, grad_leaving, grad_logits, weights, proj_weight
    )
    layer_grads = [
        lax.psum_scatter(term, BOTH, scatter_dimension=int(k in (4, 5)), tiled=True)
        for k, term in enumerate(layer_sum)
    ]
    student_grads = lax.psum(student_sum, BOTH)
    return (arrived, logits, grad_tokens, *layer_grads, *student_grads)


def solution(mesh):
    in_specs = (
        P(("batch", "zero"), None, None),
        P(("batch", "zero")),
        P(("batch", "zero")),
        P(("batch", "zero")),
        P(("batch", "zero"), None),
        P(("batch", "zero"), None),
        P(("batch", "zero"), None),
        P(("batch", "zero"), None),
        P(None, ("batch", "zero")),
        P(None, ("batch", "zero")),
        P(("batch", "zero")),
        P(),
        P(),
        P(),
        P(),
        P(),
        P(),
        P(("batch", "zero"), None, None),
        P(("batch", "zero"), None),
    )
    out_specs = (
        P(("batch", "zero"), None, None),
        P(("batch", "zero"), None),
        P(("batch", "zero"), None, None),
        P(("batch", "zero"), None),
        P(("batch", "zero"), None),
        P(("batch", "zero"), None),
        P(("batch", "zero"), None),
        P(None, ("batch", "zero")),
        P(None, ("batch", "zero")),
        P(("batch", "zero")),
        P(),
        P(),
        P(),
        P(),
        P(),
        P(),
    )
    linked = (mesh.shape["batch"], mesh.shape["zero"]) == (8, 4)
    return jax.shard_map(
        on_device_linked if linked else on_device, mesh=mesh, in_specs=in_specs, out_specs=out_specs, check_vma=False
    )
```

```python
import functools
import math

import jax
import jax.numpy as jnp
from jax import lax
from jax.experimental import pallas as pl
from jax.experimental.pallas import tpu as pltpu
from jax.sharding import PartitionSpec as P

HD = 64
SH = 2
LAYER = 4

precise = lax.Precision.HIGHEST
eps_norm = 1e-12
neg_big = -1e30


MESH = pl.DeviceIdType.MESH
f32 = jnp.float32
bf16 = jnp.bfloat16
SMALL = 128


class Place:
    def __init__(self):
        batch, zero = lax.axis_index("batch"), lax.axis_index("zero")
        self.z, self.x = lax.div(batch, 2), lax.rem(batch, 2)
        self.y, self.c = lax.div(zero, 2), lax.rem(zero, 2)

    def device(self, z=None, x=None, y=None, c=None):
        z = self.z if z is None else z
        x = self.x if x is None else x
        y = self.y if y is None else y
        c = self.c if c is None else c
        return (z * 2 + x, y * 2 + c)

    def sibling(self):
        return self.device(c=1 - self.c)

    def greet(self, far=False, routes=False):
        barrier = pltpu.get_barrier_semaphore()

        def call(device):
            pl.semaphore_signal(barrier, inc=1, device_id=device, device_id_type=MESH)

        call(self.sibling())
        call(self.device(x=1 - self.x))
        call(self.device(y=1 - self.y))

        @pl.when(self.z > 0)
        def _():
            call(self.device(z=self.z - 1))

        @pl.when(self.z < 3)
        def _():
            call(self.device(z=self.z + 1))

        if far:
            call(self.device(z=lax.rem(self.z + 2, 4)))
        if routes:
            call(self.ring(1))
            call(self.ring(7))
        inner = lax.rem(lax.div(self.z + 1, 2), 2)
        pl.semaphore_wait(barrier, 4 + inner + (1 if far else 0) + (2 if routes else 0))

    def ring(self, step):
        batch = lax.rem(2 * self.z + self.x + step, 8)
        return (batch, 2 * self.y + self.c)

    def order(self, j):
        low = lax.div(3 - self.z, 2)
        near = self.z * low + (3 - self.z) * (1 - low)
        if j < 2:
            turned = near * (1 - j) + (1 - near) * j
        else:
            turned = j
        return turned * low + (3 - turned) * (1 - low)

    def first_way(self, zb, mixed=True):
        odd = lax.rem(zb, 2) if mixed else 0
        return (
            self.x * odd + (1 - self.x) * (1 - odd),
            self.y * (1 - odd) + (1 - self.y) * odd,
        )

    def second_way(self, zb, mixed=True):
        odd = lax.rem(zb, 2) if mixed else 0
        return (
            self.x * (1 - odd) + (1 - self.x) * odd,
            self.y * odd + (1 - self.y) * (1 - odd),
        )


def remote(src, dst, send_sem, recv_sem, device):
    return pltpu.make_async_remote_copy(
        src_ref=src,
        dst_ref=dst,
        send_sem=send_sem,
        recv_sem=recv_sem,
        device_id=device,
        device_id_type=MESH,
    )


class Gather:
    SEMS = 24

    def __init__(self, at, block, line, send, recv, mixed=True):
        self.mixed = mixed
        self.at, self.block, self.line, self.send, self.recv = at, block, line, send, recv

    def move(self, view, k, device, recv_k=None):
        recv_k = k if recv_k is None else recv_k
        return remote(view, view, self.send.at[k], self.recv.at[recv_k], device)

    def hop(self, zb, step):
        at = self.at
        return self.move(
            self.block(zb, at.x, at.y, at.c),
            zb if step > 0 else zb + 20,
            at.device(z=at.z + step),
            recv_k=zb,
        )

    def first(self, zb, coming=False):
        at = self.at
        x, y = at.first_way(zb, self.mixed)
        view = self.block(zb, x, y, at.c) if coming else self.block(zb, at.x, at.y, at.c)
        return self.move(view, zb + 4, at.device(x=x, y=y))

    def second(self, zb, coming=False):
        at = self.at
        x, y = at.second_way(zb, self.mixed)
        view = self.block(zb, x, y, at.c) if coming else self.block(zb, at.x, at.y, at.c)
        return self.move(view, zb + 8, at.device(x=x, y=y))

    def corner(self, zb, coming=False):
        at = self.at
        x, y = at.second_way(zb, self.mixed)
        if coming:
            view = self.block(zb, 1 - at.x, 1 - at.y, at.c)
        else:
            view = self.block(zb, *at.first_way(zb, self.mixed), at.c)
        return self.move(view, zb + 12, at.device(x=x, y=y))

    def across(self, zb, coming=False):
        at = self.at
        return self.move(self.line(zb, 1 - at.c if coming else at.c), zb + 16, at.sibling())

    def arrive(self, j):
        at = self.at
        zb = at.order(j)
        if j > 0:
            self.hop(zb, 1).wait_recv()

        @pl.when(jnp.logical_and(zb <= at.z, at.z < 3))
        def _():
            self.hop(zb, 1).start()

        @pl.when(jnp.logical_and(zb >= at.z, at.z > 0))
        def _():
            self.hop(zb, -1).start()

        self.first(zb).start()
        self.second(zb).start()

    def turn(self, j):
        zb = self.at.order(j)
        self.first(zb, coming=True).wait_recv()
        self.corner(zb).start()

    def share(self, j):
        zb = self.at.order(j)
        self.second(zb, coming=True).wait_recv()
        self.corner(zb, coming=True).wait_recv()
        self.across(zb).start()

    def settle(self, j):
        self.across(self.at.order(j), coming=True).wait_recv()

    def finish(self):
        at = self.at
        for j in range(4):
            zb = at.order(j)

            @pl.when(jnp.logical_and(zb <= at.z, at.z < 3))
            def _():
                self.hop(zb, 1).wait_send()

            @pl.when(jnp.logical_and(zb >= at.z, at.z > 0))
            def _():
                self.hop(zb, -1).wait_send()

            self.first(zb).wait_send()
            self.second(zb).wait_send()
            self.corner(zb).wait_send()
            self.across(zb).wait_send()


def add_into(total, term):
    total[...] = (total[...].astype(f32) + term[...].astype(f32)).astype(bf16)


class Scatter:
    SEMS = 24

    def __init__(
        self, at, block, line, from_core, from_second, from_first, from_line, send, recv, mixed=True
    ):
        self.mixed = mixed
        self.at, self.block, self.line = at, block, line
        self.from_core, self.from_second = from_core, from_second
        self.from_first, self.from_line = from_first, from_line
        self.send, self.recv = send, recv

    def move(self, src, dst, k, device):
        return remote(src, dst, self.send.at[k], self.recv.at[k], device)

    def across(self, zb):
        at = self.at
        return self.move(self.line(zb, 1 - at.c), self.from_core.at[zb], zb, at.sibling())

    def second(self, zb):
        at = self.at
        x, y = at.second_way(zb, self.mixed)
        return self.move(
            self.block(zb, x, y, at.c), self.from_second.at[zb, 0], zb + 4, at.device(x=x, y=y)
        )

    def corner(self, zb):
        at = self.at
        x, y = at.second_way(zb, self.mixed)
        return self.move(
            self.block(zb, 1 - at.x, 1 - at.y, at.c),
            self.from_second.at[zb, 1],
            zb + 8,
            at.device(x=x, y=y),
        )

    def first(self, zb):
        at = self.at
        x, y = at.first_way(zb, self.mixed)
        return self.move(
            self.block(zb, x, y, at.c), self.from_first.at[zb], zb + 12, at.device(x=x, y=y)
        )

    def hop(self, zb, step):
        at = self.at
        side = 0 if step > 0 else 1
        return self.move(
            self.block(zb, at.x, at.y, at.c),
            self.from_line.at[zb, side],
            zb + 16 + 4 * side,
            at.device(z=at.z + step),
        )

    def give(self, j):
        self.across(self.at.order(j)).start()

    def join(self, j):
        at = self.at
        zb = at.order(j)
        self.across(zb).wait_recv()

        def one(k, carry):
            x, y = lax.div(k, 2), lax.rem(k, 2)
            add_into(self.block(zb, x, y, at.c), self.from_core.at[zb, x, y])
            return carry

        lax.fori_loop(0, 4, one, 0)
        self.second(zb).start()
        self.corner(zb).start()

    def halve(self, j):
        at = self.at
        zb = at.order(j)
        self.second(zb).wait_recv()
        self.corner(zb).wait_recv()
        x, y = at.first_way(zb, self.mixed)
        add_into(self.block(zb, x, y, at.c), self.from_second.at[zb, 1])
        self.first(zb).start()
        add_into(self.block(zb, at.x, at.y, at.c), self.from_second.at[zb, 0])

    def leave(self, j):
        at = self.at
        zb = at.order(j)
        mine = self.block(zb, at.x, at.y, at.c)
        self.first(zb).wait_recv()
        add_into(mine, self.from_first.at[zb])

        @pl.when(jnp.logical_and(zb >= at.z, at.z > 0))
        def _():
            self.hop(zb, 1).wait_recv()
            add_into(mine, self.from_line.at[zb, 0])

        @pl.when(jnp.logical_and(zb <= at.z, at.z < 3))
        def _():
            self.hop(zb, -1).wait_recv()
            add_into(mine, self.from_line.at[zb, 1])

        @pl.when(zb > at.z)
        def _():
            self.hop(zb, 1).start()

        @pl.when(zb < at.z)
        def _():
            self.hop(zb, -1).start()

    def finish(self):
        at = self.at
        for j in range(4):
            zb = at.order(j)
            self.across(zb).wait_send()
            self.second(zb).wait_send()
            self.corner(zb).wait_send()
            self.first(zb).wait_send()

            @pl.when(zb > at.z)
            def _():
                self.hop(zb, 1).wait_send()

            @pl.when(zb < at.z)
            def _():
                self.hop(zb, -1).wait_send()


class Route:
    PARTS = 4
    BUFFERS = 10
    SEMS = 7 * PARTS + 1

    def __init__(self, at, buffers, send, recv, near_step, shift):
        self.at, self.send, self.recv, self.near_step = at, send, recv, near_step
        (
            self.near, self.near_got, self.far, self.other, self.mine, self.end,
            self.a, self.b, self.a_got, self.b_got,
        ) = buffers
        self.size = self.far.shape[0] // self.PARTS
        low = lax.div(3 - at.z, 2)
        self.outer = lax.rem(lax.div(at.z + 1, 2), 2) == 0
        inward = 2 * low - 1
        self.inward = at.device(z=at.z + inward)
        side = lax.rem(lax.div(at.z + 1, 2), 2)
        self.outward = at.device(z=at.z + inward * (1 - 2 * side))
        self.odd = lax.rem(shift, 2) == 1
        up = lax.rem(lax.div(shift + lax.rem(shift + at.x, 2), 2), 4)
        self.up = up * low + lax.rem(4 - up, 4) * (1 - low)

    def part(self, ref, k):
        return ref.at[pl.ds(k * self.size, self.size), :]

    def move(self, src, dst, k, sem, device):
        sem = sem * self.PARTS + k + 1
        return remote(
            self.part(src, k), self.part(dst, k), self.send.at[sem], self.recv.at[sem], device
        )

    def near_move(self):
        return remote(
            self.near, self.near_got, self.send.at[0], self.recv.at[0], self.at.ring(self.near_step)
        )

    def x_move(self, k):
        return self.move(self.far, self.other, k, 0, self.at.device(x=1 - self.at.x))

    def in_move(self, k):
        return self.move(self.mine, self.end, k, 1, self.inward)

    def a_move(self, k):
        return self.move(self.a, self.a_got, k, 2, self.inward)

    def b_move(self, k):
        return self.move(self.b, self.b_got, k, 3, self.inward)

    def out_move(self, k):
        return self.move(self.other, self.end, k, 4, self.outward)

    def start(self):
        for k in range(self.PARTS):
            self.x_move(k).start()

    def step(self):
        self.near_move().start()

    def turn(self, k):
        self.x_move(k).wait_recv()
        mine, other = self.part(self.mine, k), self.part(self.other, k)
        mine[...] = jnp.where(self.odd, other[...], self.part(self.far, k)[...])

        @pl.when(self.outer)
        def _():
            self.in_move(k).start()

    def cross(self, k):
        @pl.when(jnp.logical_not(self.outer))
        def _():
            self.in_move(k).wait_recv()
            mine, end = self.part(self.mine, k)[...], self.part(self.end, k)[...]
            self.part(self.b, k)[...] = jnp.where(self.up == 2, mine, end)
            self.b_move(k).start()
            self.part(self.a, k)[...] = jnp.where(self.up == 1, mine, end)
            self.a_move(k).start()

    def hand(self, k):
        @pl.when(jnp.logical_not(self.outer))
        def _():
            self.b_move(k).wait_recv()
            self.part(self.other, k)[...] = jnp.where(
                self.up == 3, self.part(self.mine, k)[...], self.part(self.b_got, k)[...]
            )
            self.out_move(k).start()

    def land(self, k):
        self.x_move(k).wait_send()
        far, mine, end = self.part(self.far, k), self.part(self.mine, k), self.part(self.end, k)

        @pl.when(self.outer)
        def _():
            self.out_move(k).wait_recv()
            far[...] = jnp.where(self.up == 0, mine[...], end[...])

        @pl.when(jnp.logical_not(self.outer))
        def _():
            self.a_move(k).wait_recv()
            moved = jnp.where(self.up == 1, end[...], self.part(self.a_got, k)[...])
            far[...] = jnp.where(self.up == 0, mine[...], moved)

    def finish(self):
        self.near_move().wait_send()
        for k in range(self.PARTS):

            @pl.when(self.outer)
            def _():
                self.in_move(k).wait_send()

            @pl.when(jnp.logical_not(self.outer))
            def _():
                self.a_move(k).wait_send()
                self.b_move(k).wait_send()
                self.out_move(k).wait_send()


class RouteStart(Route):
    def settle(self, k, a_out, b_out, mine_out, landed):
        rows = pl.ds(k * self.size, self.size)
        mine = self.part(self.mine, k)
        mine_out[rows, :] = mine[...]

        @pl.when(self.outer)
        def _():
            landed[rows, :] = mine[...]

        @pl.when(jnp.logical_not(self.outer))
        def _():
            self.in_move(k).wait_recv()
            end = self.part(self.end, k)
            a_out[rows, :] = jnp.where(self.up == 1, mine[...], end[...])
            b_out[rows, :] = jnp.where(self.up == 2, mine[...], end[...])
            landed[rows, :] = jnp.where(self.up == 0, mine[...], end[...])

    def finish(self):
        for k in range(self.PARTS):
            self.x_move(k).wait_send()

            @pl.when(self.outer)
            def _():
                self.in_move(k).wait_send()


class RouteEnd(Route):
    def __init__(self, at, near, near_got, a, b, mine, a_got, b_got, send, recv, shift):
        super().__init__(
            at, (near, near_got, a, b_got, mine, a_got, a, b, a_got, b_got), send, recv, 7, shift
        )

    def cross(self, k):
        @pl.when(jnp.logical_not(self.outer))
        def _():
            self.b_move(k).start()
            self.a_move(k).start()

    def hand(self, k):
        @pl.when(jnp.logical_not(self.outer))
        def _():
            self.b_move(k).wait_recv()
            onward = self.part(self.b_got, k)
            onward[...] = jnp.where(self.up == 3, self.part(self.mine, k)[...], onward[...])
            self.out_move(k).start()

    def take(self, k):
        @pl.when(self.outer)
        def _():
            self.out_move(k).wait_recv()

        @pl.when(jnp.logical_not(self.outer))
        def _():
            self.a_move(k).wait_recv()

    def join(self):
        self.near_move().wait_recv()

    def stays(self):
        return jnp.logical_or(self.up == 0, jnp.logical_and(self.up == 1, jnp.logical_not(self.outer)))

    def finish(self):
        self.near_move().wait_send()
        for k in range(self.PARTS):

            @pl.when(jnp.logical_not(self.outer))
            def _():
                self.a_move(k).wait_send()
                self.b_move(k).wait_send()
                self.out_move(k).wait_send()


class Butterfly:
    def __init__(self, at, total, low, got, send, recv, halves):
        self.at, self.total, self.low, self.got = at, total, low, got
        self.send, self.recv, self.halves = send, recv, halves
        self.partners = (
            at.sibling(),
            at.device(y=1 - at.y),
            at.device(x=1 - at.x),
            at.device(z=at.z + 1 - 2 * lax.rem(at.z, 2)),
            at.device(z=lax.rem(at.z + 2, 4)),
        )

    def move(self, k):
        return remote(
            self.low.at[k], self.got.at[k], self.send.at[k], self.recv.at[k], self.partners[k]
        )

    def begin(self):
        self.move(0).start()

    def step(self, k):
        self.move(k).wait_recv()
        total = self.total[...] + self.got[k].astype(f32)
        if k < 4:
            kept = total.astype(self.low.dtype)
            self.low[k + 1] = kept
            total = kept.astype(f32)
        self.total[...] = total
        if k < 4:
            self.move(k + 1).start()

    def finish(self):
        for k in range(5):
            self.move(k).wait_send()


def in_turn(count, body, run, plan):
    def one(i, carry):
        for when, events in plan.items():

            @pl.when(i == when)
            def _():
                run(events)

        body(i)
        return carry

    lax.fori_loop(0, count, one, 0)


def wide_block(ref):
    return (lambda z, x, y, c: ref.at[c, z, x, y]), (lambda z, c: ref.at[c, z])


def tall_block(ref):
    return (lambda z, x, y, c: ref.at[z, x, y, c]), (lambda z, c: ref.at[z, :, :, c])


def take_half(ref, c):
    width = ref.shape[1] // 2
    return ref[:, pl.ds(pl.multiple_of(c * width, 128), width)].astype(f32)


def finish_scatter(at, chunk, total, out, swap_send, swap_recv, tall):
    mine = chunk.block(at.z, at.x, at.y, at.c)
    if tall:
        out[...] = mine[...].astype(f32)
        return
    total[...] = mine[...].astype(f32)
    rows, width = out.shape[0], out.shape[1] // 2
    here = pl.ds(pl.multiple_of(at.c * width, 128), width)
    there = pl.ds(pl.multiple_of((1 - at.c) * width, 128), width)
    swap = remote(
        total.at[pl.ds(pl.multiple_of((1 - at.c) * rows, 8), rows)],
        out.at[:, here],
        swap_send,
        swap_recv,
        at.sibling(),
    )
    swap.start()
    out[:, here] = total[pl.ds(pl.multiple_of(at.c * rows, 8), rows), :]
    remote(
        total.at[pl.ds(pl.multiple_of((1 - at.c) * rows, 8), rows)],
        out.at[:, there],
        swap_send,
        swap_recv,
        at.sibling(),
    ).wait_recv()
    swap.wait_send()


def dots(left, right, over_left, over_right):
    return lax.dot_general(
        left, right, (((over_left,), (over_right,)), ((), ())), preferred_element_type=f32
    )


def rows_of(i, size):
    return pl.ds(pl.multiple_of(i * size, size), size)


def lanes_of(i, size=128):
    return pl.ds(pl.multiple_of(i * size, size), size)


def unpack_small(attn_all, vectors, units, shard):
    halves, width = attn_all.shape[-2:]
    lanes = pl.ds(width - SMALL, SMALL)
    lane = lax.broadcasted_iota(jnp.int32, (8, SMALL), 1)
    for ref, rows, size in ((vectors, 0, shard), (units, 8, 4 * shard)):
        tiles = [jnp.zeros((8, SMALL), f32) for _ in range(ref.shape[1] // SMALL)]
        for n in range(32):
            chip, core = n // 2, n % 2
            piece = attn_all[0, chip // 4, chip // 2 % 2, chip % 2, :, lanes].astype(f32)
            piece = piece[core * shard + rows : core * shard + rows + 8]
            tile, shift = n * size // SMALL, n * size % SMALL
            if shift:
                piece = pltpu.roll(piece, shift, 1)
            tiles[tile] = tiles[tile] + jnp.where(lane >= shift, piece, 0.0)
            if shift + size > SMALL:
                tiles[tile + 1] = tiles[tile + 1] + jnp.where(lane < shift, piece, 0.0)
        for t, tile in enumerate(tiles):
            ref[:, t * SMALL : (t + 1) * SMALL] = tile[: ref.shape[0]]


def project_half(tokens, weights, vectors, mixed, slot, length, half):
    features = tokens.shape[1]
    width = 3 * features // 2
    here = pl.ds(slot * length, length)
    for part in range(2):
        size = features if (part == half) else width - features
        start = 0 if part == 0 else width - size
        out = jnp.dot(tokens[here, :], weights(half, start, size), preferred_element_type=f32)
        if part == half:
            out = out + vectors[half : half + 1, :]
        mixed[here, half * width + start : half * width + start + size] = out.astype(bf16)


def attend_pair(mixed, context, totals, slot, pair, length, used):
    features = context.shape[1]
    here = pl.ds(slot * length, length) if isinstance(slot, int) else rows_of(slot, length)
    base = pl.multiple_of(pair * 128, 128)
    two_q = mixed[here, pl.ds(base, 128)]
    two_k = mixed[here, pl.ds(pl.multiple_of(base + features, 128), 128)]
    two_v = mixed[here, pl.ds(pl.multiple_of(base + 2 * features, 128), 128)]
    low = lax.broadcasted_iota(jnp.int32, two_k.shape, 1) < HD
    valid = lax.broadcasted_iota(jnp.int32, (length, 1), 0) < used
    none = jnp.zeros_like(two_k)
    two_q = two_q * jnp.asarray(HD ** (-0.5), bf16)
    outs = []
    for head in range(2):
        keys = jnp.where(low if head == 0 else ~low, two_k, none)
        scores = jnp.where(valid, dots(keys, two_q, 1, 1), neg_big)
        top = jnp.max(scores, axis=0, keepdims=True)
        powers = jnp.exp(scores - top)
        total = jnp.sum(powers, axis=0, keepdims=True)
        shares = (powers * (1.0 / total)).astype(bf16)
        outs.append(dots(shares, two_v, 0, 0))
        totals[slot, pl.ds(2 * pair + head, 1), :] = top + jnp.log(total)
    context[here, pl.ds(base, 128)] = jnp.where(low, outs[0], outs[1]).astype(bf16)


def norm_rows(hidden, gain, shift):
    centred = hidden - jnp.mean(hidden, axis=-1, keepdims=True)
    inverse = lax.rsqrt(jnp.mean(centred * centred, axis=-1, keepdims=True) + eps_norm)
    normed = centred * inverse
    return normed * gain + shift, normed, inverse


def gelu_both(v):
    size = jnp.abs(v) * 0.7071067811865476
    t = 1.0 / (1.0 + 0.3275911 * size)
    bell = jnp.exp(-0.5 * v * v)
    poly = t * (
        0.254829592
        + t * (-0.284496736 + t * (1.421413741 + t * (-1.453152027 + t * 1.061405429)))
    )
    tail = 0.5 * poly * bell
    share = jnp.where(v < 0.0, tail, 1.0 - tail)
    return v * share, share + v * bell * 0.3989422804014327


def first_rows(tokens, context, merge, up, vectors, units, first, outs, r, size):
    normed_out, inverse_out, low_out, active_out, slope_out = outs
    here = rows_of(r, size)
    attended = jnp.concatenate(
        [jnp.dot(context[here, :], merge(h), preferred_element_type=f32) for h in range(2)], axis=1
    )
    hidden = tokens[here, :].astype(f32) + (attended + vectors[2:3, :])
    full, normed, inverse = norm_rows(hidden, vectors[6:7, :], vectors[3:4, :])
    first[here, :] = full
    low = full.astype(bf16)
    normed_out[here, :] = normed.astype(bf16)
    inverse_out[here, :] = inverse
    low_out[here, :] = low
    width = units.shape[1] // 2
    step = width // 2
    for part in range(4):
        cols = pl.ds(part * step, step)
        inner = jnp.dot(low, up(part // 2, part % 2 * step, step), preferred_element_type=f32)
        active, slope = gelu_both(inner + units[0:1, cols])
        active_out[here, cols] = active.astype(bf16)
        slope_out[here, cols] = slope.astype(bf16)


def second_rows(active, down, vectors, first, outs, r, size, features):
    normed_out, inverse_out, leaving_out = outs
    here = rows_of(r, size)
    branch = jnp.dot(
        active[here, :], down[...].reshape(-1, features), preferred_element_type=f32
    )
    hidden = first[here, :] + (branch + vectors[4:5, :])
    full, normed, inverse = norm_rows(hidden, vectors[7:8, :], vectors[5:6, :])
    normed_out[here, :] = normed.astype(bf16)
    inverse_out[here, :] = inverse
    leaving_out[here, :] = full.astype(bf16)


FORWARD_PLAN = {
    "open": ("m.begin", "a.begin", "d.arrive.0", "u.begin",),
    "gather": (
        "a.arrive.1", "m.turn.0", "m.arrive.1", "a.arrive.2", "a.turn.0", "a.turn.1",
        "a.arrive.3", "u.arrive.1", "a.turn.2", "a.turn.3", "m.turn.1", "u.arrive.2", "u.turn.1",
        "a.share.1", "a.share.0", "m.arrive.2", "a.share.2", "r.start", "u.arrive.3",
        "d.arrive.1", "a.settle.2", "a.share.3", "a.settle.3", "a.settle.0", "a.settle.1",
    ),
    "project": (
        (),
        ("r.turn.0", "m.arrive.3",),
        (),
        ("u.turn.2", "u.turn.0",),
    ),
    "attend": {
        0: ("d.arrive.2",),
        1: ("u.share.1", "m.share.1", "m.turn.2", "m.share.0",),
        3: ("r.turn.2", "r.cross.0", "r.turn.1", "m.settle.1", "d.arrive.3", "u.share.0",),
        4: ("r.step",),
        5: ("u.share.2", "u.settle.1",),
        6: ("r.cross.2", "u.turn.3",),
        7: ("u.settle.2",),
        8: ("m.share.2", "m.turn.3", "m.settle.0",),
        9: ("m.settle.2", "d.turn.1",),
        10: ("u.share.3", "d.turn.2", "m.share.3", "r.turn.3", "u.settle.0",),
        11: ("d.turn.3",),
    },
    "before_first": ("m.settle.3", "u.settle.3",),
    "first": {
        0: ("d.share.1",),
        1: ("d.turn.0", "r.cross.1", "r.hand.0",),
        2: ("d.share.2", "r.hand.2", "r.cross.3",),
        3: ("d.settle.2", "d.share.3", "r.hand.1", "d.share.0",),
    },
    "before_second": ("d.settle.1", "d.settle.3", "d.settle.0",),
    "second": {
        1: ("r.hand.3",),
        2: ("r.land.0", "r.land.2",),
    },
    "close": ("r.land.3", "r.land.1",),
}


def forward_kernel(
    lengths, picks, tokens, attn, merge, up, down, biases, gains, unit, grad_act,
    mixed_out, context_out, totals, attn_out, merge_out, up_out, down_out, vectors, units,
    normed_one, inverse_one, low, active_out, slope_out, normed_two, inverse_two, leaving,
    grad_leaving,
    attn_all, merge_all, up_all, down_all, mixed, context, active, slope, first,
    attn_mine, merge_mine, up_mine, attn_pair, merge_pair, up_pair, *scratch,
):
    at = Place()
    route_buffers = scratch[: Route.BUFFERS]
    send, recv, swap_send, swap_recv, local, route_send, route_recv = scratch[Route.BUFFERS :]
    shard = attn.shape[0]
    own = pl.ds(pl.multiple_of(at.c * shard, 8), shard)
    lanes = attn.shape[1] // 2
    slots = lengths.shape[0]
    rows, features = tokens.shape
    length = rows // slots
    sources = (attn, merge, up)
    mine = (attn_mine, merge_mine, up_mine)
    pairs = (attn_pair, merge_pair, up_pair)
    gathered = (attn_all, merge_all, up_all)
    route = Route(at, route_buffers, route_send, route_recv, 1, picks[1])
    near, near_got, far = route.near, route.near_got, route.far
    here = [
        pltpu.make_async_copy(grad_act.at[k], ref, local.at[k])
        for k, ref in enumerate((route.a, route.b))
    ]
    for copy in here:
        copy.start()
    for k in range(3):
        width = sources[k].shape[1] // 2
        mine[k][:, :width] = take_half(sources[k], 1 - at.c)
        pairs[k][own, :width] = take_half(sources[k], at.c)
    attn_mine[:, lanes:] = jnp.zeros((shard, SMALL), f32)
    attn_mine[0:8, lanes : lanes + shard] = jnp.concatenate(
        [biases[...].astype(f32), gains[...].astype(f32)], axis=0
    )
    attn_mine[8:9, lanes : lanes + unit.shape[1]] = unit[...].astype(f32)
    attn_pair[own, lanes:] = attn_mine[:, lanes:]
    down_all[at.z, at.x, at.y, at.c] = down[...]
    at.greet(routes=True)
    swaps = []
    for k in range(3):
        swaps.append(
            remote(mine[k], pairs[k].at[own], swap_send.at[k], swap_recv.at[k], at.sibling())
        )
        swaps[-1].start()
    chunks = [
        Gather(at, *wide_block(gathered[k]), send.at[k], recv.at[k], mixed=k == 0)
        for k in range(3)
    ]
    chunks.append(Gather(at, *tall_block(down_all), send.at[3], recv.at[3], mixed=False))
    on_attn, on_merge, on_up, on_down = chunks

    actors = {"a": on_attn, "m": on_merge, "u": on_up, "d": on_down, "r": route}
    wide = {"a": 0, "m": 1, "u": 2}

    def run(events):
        for event in events:
            who, what, *rest = event.split(".")
            if what == "begin":
                k = wide[who]
                swaps[k].wait_recv()
                gathered[k][at.c, at.z, at.x, at.y] = pairs[k][...].astype(bf16)
                chunks[k].arrive(0)
            else:
                getattr(actors[who], what)(*(int(j) for j in rest))

    plan = FORWARD_PLAN
    run(plan["open"])
    for copy in here:
        copy.wait()
    near_first = picks[0] == 0
    near[...] = jnp.where(near_first, route.a[...], route.b[...])
    far[...] = jnp.where(near_first, route.b[...], route.a[...])
    run(plan["gather"])
    unpack_small(attn_all, vectors, units, shard)

    def columns(half, start, size):
        return attn_all[half, :, :, :, :, start : start + size].reshape(features, size)

    def up_part(half, start, width):
        return up_all[half, :, :, :, :, start : start + width].reshape(features, width)

    def merge_half(half):
        return merge_all[half].reshape(features, merge_all.shape[-1])

    for slot in range(slots):
        for half in range(2):
            project_half(tokens, columns, vectors, mixed, slot, length, half)
            run(plan["project"][2 * slot + half])
    saves = [
        pltpu.make_async_copy(src, dst, local.at[k + 2])
        for k, (src, dst) in enumerate(
            (
                (attn_all, attn_out),
                (mixed, mixed_out),
                (context, context_out),
                (merge_all, merge_out),
                (up_all, up_out),
                (down_all, down_out),
                (active, active_out),
                (slope, slope_out),
                (route.a, grad_leaving.at[0]),
                (route.b, grad_leaving.at[1]),
            )
        )
    ]
    saves[0].start()
    saves[1].start()

    def pair_step(i):
        slot, pair = lax.div(i, 6), lax.rem(i, 6)
        used = jnp.where(slot == 0, lengths[0], lengths[1])
        attend_pair(mixed, context, totals, slot, pair, length, used)

    in_turn(6 * slots, pair_step, run, plan["attend"])
    saves[2].start()
    run(plan["before_first"])
    saves[3].start()
    saves[4].start()
    size = rows // 4

    def first_step(r):
        first_rows(
            tokens, context, merge_half, up_part, vectors, units, first,
            (normed_one, inverse_one, low, active, slope), r, size,
        )

    in_turn(4, first_step, run, plan["first"])
    saves[6].start()
    saves[7].start()
    run(plan["before_second"])
    saves[5].start()

    def second_step(r):
        second_rows(
            active, down_all, vectors, first, (normed_two, inverse_two, leaving), r, size, features
        )

    in_turn(4, second_step, run, plan["second"])
    run(plan["close"])
    route.near_move().wait_recv()
    route.finish()
    near_one = picks[2] == 0
    for k, ref in enumerate((route.a, route.b)):
        pick = near_one if k == 0 else jnp.logical_not(near_one)
        moved = jnp.where(pick, near_got[...], far[...])
        ref[...] = jnp.where(picks[3 + k] == 1, moved, jnp.zeros_like(moved))
        saves[8 + k].start()
    for chunk in chunks:
        chunk.finish()
    for swap in swaps:
        swap.wait_send()
    for save in saves:
        save.wait()


def forward_layer(lengths, picks, tokens, attn, merge, up, down, biases, gains, unit, grad_act):
    rows, features = tokens.shape
    shard = attn.shape[0]
    slots = lengths.shape[0]
    hidden = up.shape[1]
    widths = (attn.shape[1] // 2 + SMALL, merge.shape[1] // 2, hidden // 2)
    blocks = [(2, 4, 2, 2, 2 * shard, width) for width in widths] + [(4, 2, 2, 2) + down.shape]
    vmem = pl.BlockSpec(memory_space=pltpu.VMEM)
    anywhere = pl.BlockSpec(memory_space=pl.ANY)
    smem = pl.BlockSpec(memory_space=pltpu.SMEM)

    def shape(*dims, kind=bf16):
        return jax.ShapeDtypeStruct(dims, kind)

    return pl.pallas_call(
        forward_kernel,
        out_shape=[
            shape(rows, 3 * features),
            shape(rows, features),
            shape(slots, features // HD, rows // slots, kind=f32),
            *[shape(*block) for block in blocks],
            shape(8, features, kind=f32),
            shape(8, hidden, kind=f32),
            shape(rows, features),
            shape(rows, 1, kind=f32),
            shape(rows, features),
            shape(rows, hidden),
            shape(rows, hidden),
            shape(rows, features),
            shape(rows, 1, kind=f32),
            shape(rows, features),
            shape(*grad_act.shape),
        ],
        in_specs=[smem, smem] + [vmem] * 8 + [anywhere],
        out_specs=[anywhere, anywhere, vmem] + [anywhere] * 4 + [vmem] * 5
        + [anywhere, anywhere, vmem, vmem, vmem, anywhere],
        scratch_shapes=[pltpu.VMEM(block, bf16) for block in blocks]
        + [
            pltpu.VMEM((rows, 3 * features), bf16),
            pltpu.VMEM((rows, features), bf16),
            pltpu.VMEM((rows, hidden), bf16),
            pltpu.VMEM((rows, hidden), bf16),
            pltpu.VMEM((rows, features), f32),
        ]
        + [pltpu.VMEM((shard, width), f32) for width in widths]
        + [pltpu.VMEM((2 * shard, width), f32) for width in widths]
        + [pltpu.VMEM(grad_act.shape[1:], bf16)] * Route.BUFFERS
        + [
            pltpu.SemaphoreType.DMA((4, Gather.SEMS)),
            pltpu.SemaphoreType.DMA((4, Gather.SEMS)),
            pltpu.SemaphoreType.DMA((3,)),
            pltpu.SemaphoreType.DMA((3,)),
            pltpu.SemaphoreType.DMA((12,)),
            pltpu.SemaphoreType.DMA((Route.SEMS,)),
            pltpu.SemaphoreType.DMA((Route.SEMS,)),
        ],
        compiler_params=pltpu.CompilerParams(
            collective_id=0, has_side_effects=True, vmem_limit_bytes=62 << 20
        ),
        cost_estimate=pl.CostEstimate(
            flops=2 * rows * features * 12 * features, bytes_accessed=100 << 20, transcendentals=0
        ),
    )(lengths, picks, tokens, attn, merge, up, down, biases, gains, unit.reshape(1, -1), grad_act)


def exact(left, right, over_left=1, over_right=0):
    return lax.dot_general(
        left,
        right,
        (((over_left,), (over_right,)), ((), ())),
        precision=precise,
        preferred_element_type=f32,
    )


def rows_sum(values):
    return jnp.sum(values, axis=0, keepdims=True)


def pile(rows):
    width = rows[0].shape[1]
    count = sum(r.shape[0] for r in rows)
    return jnp.concatenate(rows + [jnp.zeros((8 - count, width), f32)], axis=0)


def student_slots(
    leaving, proj, pool, dense, label, student_bias, logit_bias, grad_logits, lengths,
    logits, low_grad, pack,
):
    slots = lengths.shape[0]
    length = leaving.shape[0] // slots
    half = proj.shape[1] // SH
    low = lax.broadcasted_iota(jnp.int32, (1, proj.shape[1]), 1) < half
    scale = 1.0 / math.sqrt(half)
    left, right = [[] for _ in range(5)], [[] for _ in range(5)]
    sums, outs = [], []

    def by_head(row):
        return jnp.concatenate([jnp.where(low, row, 0.0), jnp.where(low, 0.0, row)], axis=0)

    def one_row(two):
        return jnp.where(low, two[0:1], two[1:2])

    for slot in range(slots):
        here = pl.ds(slot * length, length)
        projected = jnp.dot(leaving[here, :], proj[...], preferred_element_type=f32)
        projected = projected + student_bias[0:1, :]
        valid = lax.broadcasted_iota(jnp.int32, (length, 1), 0) < lengths[slot]
        start = projected[0:1]
        query = exact(start, pool[0])
        queries = by_head(query)
        asks = exact(queries, pool[1], 1, 1)
        shares, means = [], []
        for h in range(SH):
            scores = jnp.sum(projected * asks[h : h + 1], axis=1, keepdims=True) * scale
            scores = jnp.where(valid, scores, neg_big)
            powers = jnp.exp(scores - jnp.max(scores, axis=0, keepdims=True))
            shares.append(powers / rows_sum(powers))
            means.append(rows_sum(shares[h] * projected))
        mean_rows = jnp.concatenate(means, axis=0)
        pooled = one_row(exact(mean_rows, pool[2]))
        active = jnp.tanh(exact(pooled, dense[...]) + student_bias[1:2, :])
        outs.append(exact(active, label[...]) + logit_bias[...])
        g_logits = grad_logits[slot : slot + 1, :]
        g_pre = exact(g_logits, label[...], 1, 1) * (1.0 - active * active)
        g_pooled = by_head(exact(g_pre, dense[...], 1, 1))
        g_means = exact(g_pooled, pool[2], 1, 1)
        g_projected = jnp.zeros_like(projected)
        g_asks = []
        for h in range(SH):
            g_share = jnp.sum(projected * g_means[h : h + 1], axis=1, keepdims=True)
            g_score = shares[h] * (g_share - rows_sum(g_share * shares[h])) * scale
            g_projected = g_projected + shares[h] * g_means[h : h + 1] + g_score * asks[h : h + 1]
            g_asks.append(rows_sum(g_score * projected))
        g_ask_rows = jnp.concatenate(g_asks, axis=0)
        g_query = one_row(exact(g_ask_rows, pool[1]))
        first = lax.broadcasted_iota(jnp.int32, (length, 1), 0) == 0
        g_projected = g_projected + jnp.where(first, exact(g_query, pool[0], 1, 1), 0.0)
        low_grad[here, :] = g_projected.astype(bf16)
        sums.append((rows_sum(g_projected), g_pre, g_logits))
        for k, (a, b) in enumerate(
            (
                (start, g_query),
                (g_ask_rows, queries),
                (mean_rows, g_pooled),
                (pooled, g_pre),
                (g_logits, active),
            )
        ):
            left[k].append(a)
            right[k].append(b)
    features, lanes = proj.shape
    pack[0:features, :] = dots(leaving[...], low_grad[...], 0, 0)
    for k in range(5):
        grad = exact(pile(left[k]), pile(right[k]), 0, 0)
        row = features + k * lanes
        size = lanes if k < 4 else 16
        pack[row : row + size, :] = grad[:size]
    row = features + 4 * lanes + 16
    pack[row : row + 8, :] = pile([sum(s[k] for s in sums) for k in range(3)])
    logits[...] = pile(outs)


def norm_back(grad, normed, inverse, gain):
    scaled = grad * gain
    return inverse * (
        scaled
        - jnp.mean(scaled, axis=-1, keepdims=True)
        - normed * jnp.mean(scaled * normed, axis=-1, keepdims=True)
    )


ROWS_PLAN = {
    1: (("turn", 0), ("turn", 1)),
    2: (("turn", 2), ("turn", 3)),
}


def rows_kernel(
    lengths, picks, leaving, proj, pool, dense, label, student_bias, logit_bias, grad_logits,
    merge, up, down, vectors, grad_leaving, normed_one, inverse_one, normed_two, inverse_two,
    slope,
    logits, pack, near, a, b, mine, landed, mid_low, inner_low, res, res_low, grad_context,
    proj_low, sums, unit_sum, *scratch,
):
    step = pl.program_id(0)
    size = grad_leaving.shape[0]
    at = Place()
    buffers, (send, recv) = scratch[:-2], scratch[-2:]
    route = RouteStart(at, (None, None, *buffers, *[None] * 4), send, recv, 7, picks[0])
    length = leaving.shape[0] // lengths.shape[0]

    @pl.when(step == 0)
    def _():
        at.greet()
        near_one = picks[1] == 0
        for k in range(route.PARTS):
            part = pl.ds(k * route.size, route.size)
            two = []
            for slot in range(2):
                rows = pl.ds(slot * length + k * route.size, route.size)
                kept = leaving[rows, :]
                two.append(jnp.where(picks[2 + slot] == 1, kept, jnp.zeros_like(kept)))
            near[part, :] = jnp.where(near_one, two[0], two[1])
            route.far[part, :] = jnp.where(near_one, two[1], two[0])
            route.x_move(k).start()

    for when, events in ROWS_PLAN.items():

        @pl.when(step == when)
        def _():
            for event, k in events:
                getattr(route, event)(k)

    @pl.when(step == 0)
    def _():
        student_slots(
            leaving, proj, pool, dense, label, student_bias, logit_bias, grad_logits, lengths,
            logits, proj_low, pack,
        )
        sums[...] = jnp.zeros_like(sums)
        unit_sum[...] = jnp.zeros_like(unit_sum)

    grad_second = grad_leaving[...].astype(f32) + dots(proj_low[rows_of(step, size), :], proj[...], 1, 1)
    two = normed_two[...].astype(f32)
    grad_mid = norm_back(grad_second, two, inverse_two[...], vectors[7:8, :])
    mid = grad_mid.astype(bf16)
    mid_low[...] = mid
    width = up.shape[2]
    grad_first = grad_mid
    for half in range(2):
        for part in range(2):
            cols = pl.ds(half * width + part * (width // 2), width // 2)
            inside = pl.ds(part * (width // 2), width // 2)
            inner = dots(mid, down[cols, :], 1, 1) * slope[:, cols].astype(f32)
            unit_sum[0:1, cols] += rows_sum(inner)
            inner = inner.astype(bf16)
            inner_low[:, cols] = inner
            grad_first = grad_first + dots(inner, up[half, :, inside], 1, 1)
    one = normed_one[...].astype(f32)
    grad_res = norm_back(grad_first, one, inverse_one[...], vectors[6:7, :])
    res[...] = grad_res
    low = grad_res.astype(bf16)
    res_low[...] = low
    narrow = merge.shape[2]
    grad_context[...] = (
        dots(low[:, :narrow], merge[0], 1, 1) + dots(low[:, narrow:], merge[1], 1, 1)
    ).astype(bf16)
    sums[...] += jnp.concatenate(
        [
            jnp.zeros((2, grad_res.shape[1]), f32),
            rows_sum(grad_res),
            rows_sum(grad_first),
            rows_sum(grad_mid),
            rows_sum(grad_second),
            rows_sum(grad_first * one),
            rows_sum(grad_second * two),
        ],
        axis=0,
    )

    @pl.when(step == pl.num_programs(0) - 1)
    def _():
        for k in range(route.PARTS):
            route.settle(k, a, b, mine, landed)
        route.finish()
        row = pack.shape[0] - 72
        for t in range(6):
            pack[row + 8 * t : row + 8 * t + 8, :] = sums[:, 128 * t : 128 * t + 128]
        pack[row + 48 : row + 72, :] = unit_sum[0:1, :].reshape(24, 128)


def rows_backward(lengths, picks, leaving, student, grad_logits, weights, vectors, grad_leaving, saved):
    proj, pool, dense, label, student_bias, logit_bias = student
    merge, up, down = weights
    normed_one, inverse_one, normed_two, inverse_two, slope = saved
    rows, features = leaving.shape
    hidden = down.shape[0]
    size = rows // 4
    lanes = proj.shape[1]
    label_lanes = jnp.pad(label, ((0, 0), (0, lanes - label.shape[1])))
    logit_lanes = jnp.pad(logit_bias, (0, lanes - label.shape[1])).reshape(1, lanes)
    grad_lanes = jnp.pad(grad_logits, ((0, 0), (0, lanes - label.shape[1])))

    def fixed(array):
        return pl.BlockSpec(array.shape, lambda i, n=array.ndim: (0,) * n, pipeline_mode=pl.Buffered(1))

    def by_rows(array):
        return pl.BlockSpec((size, array.shape[1]), lambda i: (i, 0))

    def shape(*dims, kind=f32):
        return jax.ShapeDtypeStruct(dims, kind)

    whole_in = (leaving, proj, pool, dense, label_lanes, student_bias, logit_lanes, grad_lanes, merge, up, down, vectors)
    row_in = (grad_leaving, normed_one, inverse_one, normed_two, inverse_two, slope)
    whole_out = (
        shape(8, lanes), shape(features + 4 * lanes + 24 + 72, lanes),
        *[shape(rows // 2, features, kind=bf16)] * 5,
    )
    row_out = (
        shape(rows, features, kind=bf16), shape(rows, hidden, kind=bf16), shape(rows, features),
        shape(rows, features, kind=bf16), shape(rows, features, kind=bf16),
    )
    return pl.pallas_call(
        rows_kernel,
        grid=(4,),
        out_shape=whole_out + row_out,
        in_specs=[pl.BlockSpec(memory_space=pltpu.SMEM)] * 2
        + [fixed(a) for a in whole_in]
        + [by_rows(a) for a in row_in],
        out_specs=[fixed(a) for a in whole_out] + [by_rows(a) for a in row_out],
        scratch_shapes=[
            pltpu.VMEM((rows, lanes), bf16),
            pltpu.VMEM((8, features), f32),
            pltpu.VMEM((8, hidden), f32),
            *[pltpu.VMEM((rows // 2, features), bf16)] * 4,
            pltpu.SemaphoreType.DMA((Route.SEMS,)),
            pltpu.SemaphoreType.DMA((Route.SEMS,)),
        ],
        compiler_params=pltpu.CompilerParams(
            dimension_semantics=("arbitrary",), collective_id=1, has_side_effects=True,
            vmem_limit_bytes=60 << 20,
        ),
        cost_estimate=pl.CostEstimate(
            flops=2 * rows * features * (2 * hidden + features),
            bytes_accessed=40 << 20,
            transcendentals=0,
        ),
    )(lengths, picks, *whole_in, *row_in)


def attend_back_pair(mixed, grad_context, totals, sums, slot, pair, length, used, features):
    here = rows_of(slot, length)
    base = pl.multiple_of(pair * 128, 128)
    spots = [pl.ds(pl.multiple_of(base + k * features, 128), 128) for k in range(3)]
    two_q, two_k, two_v = (mixed[here, spot] for spot in spots)
    two_g = grad_context[here, pl.ds(base, 128)]
    low = lax.broadcasted_iota(jnp.int32, two_k.shape, 1) < HD
    valid = lax.broadcasted_iota(jnp.int32, (length, 1), 0) < used
    none = jnp.zeros_like(two_k)
    scale = jnp.asarray(HD ** (-0.5), bf16)
    two_q = two_q * scale
    small_k = two_k * scale
    outs = [[], [], []]
    for head in range(2):
        side = low if head == 0 else ~low
        scores = dots(jnp.where(side, two_k, none), two_q, 1, 1)
        probs = jnp.where(valid, jnp.exp(scores - totals[slot, pl.ds(2 * pair + head, 1), :]), 0.0)
        grad_probs = dots(jnp.where(side, two_v, none), two_g, 1, 1)
        shared = jnp.sum(grad_probs * probs, axis=0, keepdims=True)
        grad_scores = (probs * (grad_probs - shared)).astype(bf16)
        outs[0].append(dots(grad_scores, small_k, 0, 0))
        outs[1].append(jnp.dot(grad_scores, two_q, preferred_element_type=f32))
        outs[2].append(jnp.dot(probs.astype(bf16), two_g, preferred_element_type=f32))
    for k in range(3):
        grad = jnp.where(low, outs[k][0], outs[k][1])
        mixed[here, spots[k]] = grad.astype(bf16)
        if k != 1:
            sums[k // 2 : k // 2 + 1, pl.ds(base, 128)] += rows_sum(grad)


CLOSE_PLAN = {
    "up": {
        0: ("r.step", "s.step.0",),
        2: ("d.join.3",),
        7: ("d.join.2",),
    },
    "merge": (),
    "attend": {
        1: ("s.step.1", "d.halve.3", "u.join.3", "r.hand.0", "u.join.2",),
        2: ("m.join.3",),
        3: ("m.join.2",),
        4: ("d.join.1",),
        5: ("d.join.0",),
        6: ("d.halve.2", "u.join.1",),
        8: ("r.hand.2", "d.leave.3", "s.step.2", "d.halve.1", "u.halve.3", "u.halve.2", "r.join",),
        9: ("r.hand.1",),
        10: ("u.join.0",),
        11: ("d.leave.2",),
    },
    "attn": {
        0: ("m.halve.3", "u.leave.3",),
        1: ("m.halve.2",),
        3: (
            "b.step.0", "a.give.1", "m.join.1", "r.take.1", "a.give.3", "a.give.0", "u.halve.1",
            "a.give.2",
        ),
        4: ("m.join.0", "u.leave.2", "u.halve.0",),
        5: ("r.take.0",),
    },
    "before_inputs": (
        "a.join.3", "s.step.3", "r.take.2", "b.step.1", "a.join.2", "m.halve.1", "a.halve.3",
        "m.leave.3", "u.leave.1", "b.step.2", "a.join.1", "m.halve.0",
    ),
    "inputs": {
        0: ("a.halve.2", "r.hand.3", "a.join.0", "d.leave.1",),
        1: (
            "a.leave.3", "b.step.3", "a.halve.1", "u.leave.0", "m.leave.2", "d.halve.0",
            "a.leave.2", "m.leave.1",
        ),
        2: ("a.leave.1", "a.halve.0", "r.take.3",),
        3: ("s.step.4", "b.step.4", "m.leave.0", "d.leave.0",),
    },
    "close": ("a.leave.0",),
}


def close_kernel(
    lengths, picks, totals, pack, mixed_in, grad_context_in, tokens_in, attn_in, res_in,
    active_in, inner_in, mid_in, low_in, context_in, res_low_in, near, a, b, mine_in, landed_in,
    grad_inputs, attn_out, merge_out, up_out, down_out, small_out, late_out, arrived,
    *scratch,
):
    at = Place()
    (
        mixed, attn, tiles, mid, low, context, res_low, bias_sums,
        small_low, small_got, small_sum, late_low, late_got, near_got, a_got, b_got, mine, landed,
        attn_total, merge_total, up_total,
        local, tile_sems, small_send, small_recv, swap_send, swap_recv, route_send, route_recv,
        send, recv,
    ) = scratch[-31:]
    chunks = []
    for k in range(4):
        grad, from_core, from_second, from_first, from_line = scratch[5 * k : 5 * k + 5]
        block, line = (tall_block if k == 3 else wide_block)(grad)
        chunks.append(
            Scatter(
                at, block, line, from_core, from_second, from_first, from_line,
                send.at[k], recv.at[k], mixed=k != 3,
            )
        )
    grads = [scratch[5 * k] for k in range(4)]
    on_attn, on_merge, on_up, on_down = chunks
    features = mid.shape[1]
    slots = lengths.shape[0]
    length = mixed.shape[0] // slots
    tile_lanes = tiles.shape[2]
    steps = inner_in.shape[1] // tile_lanes

    def load(k, src, dst):
        copy = pltpu.make_async_copy(src, dst, local.at[k])
        copy.start()
        return copy

    def tile(src, t):
        return pltpu.make_async_copy(
            src.at[:, lanes_of(t, tile_lanes)], tiles.at[lax.rem(t, 2)], tile_sems.at[lax.rem(t, 2)]
        )

    mid_load = load(0, mid_in, mid)
    tile(active_in, 0).start()
    low_load = load(1, low_in, low)
    context_load = load(2, context_in, context)
    res_low_load = load(3, res_low_in, res_low)
    mixed_load = load(4, mixed_in, mixed)
    res_load = load(5, res_in, grad_inputs)
    attn_load = load(6, attn_in, attn)
    landed_load = load(9, landed_in, landed)
    mine_load = load(12, mine_in, mine)
    at.greet(far=True, routes=True)
    route = RouteEnd(
        at, near, near_got, a, b, mine, a_got, b_got, route_send, route_recv, picks[0]
    )
    small = Butterfly(
        at, small_sum, small_low, small_got, small_send.at[0], small_recv.at[0], True
    )
    late = Butterfly(at, late_out, late_low, late_got, small_send.at[1], small_recv.at[1], False)
    actors = {
        "a": on_attn, "m": on_merge, "u": on_up, "d": on_down, "r": route, "s": small, "b": late
    }
    plan = CLOSE_PLAN

    def run(events):
        for event in events:
            who, what, *rest = event.split(".")
            getattr(actors[who], what)(*(int(j) for j in rest))

    small_rows = small_low.shape[1]
    for half in range(2):
        part = pack[half * small_rows : (half + 1) * small_rows, :].astype(bf16)
        here = at.c == half

        @pl.when(here)
        def _():
            small_sum[...] = part.astype(f32)

        @pl.when(jnp.logical_not(here))
        def _():
            small_low[0] = part

    mine_load.wait()
    for part in range(Route.PARTS):
        route.cross(part)
    small.begin()

    mid_load.wait()

    def down_tile(t, carry):
        tile(active_in, t).wait()

        @pl.when(t + 1 < steps)
        def _():
            tile(active_in, t + 1).start()

        part = dots(tiles[lax.rem(t, 2)], mid[...], 0, 0).astype(bf16)
        grads[3][lax.div(t, 2), lax.rem(t, 2)] = part.reshape(2, 2, part.shape[0] // 4, features)

        @pl.when(lax.rem(t, 2) == 1)
        def _():
            on_down.across(lax.div(t, 2)).start()

        return carry

    lax.fori_loop(0, steps, down_tile, 0)
    tokens_load = load(7, tokens_in, mid)
    low_load.wait()
    half_steps = steps // 2

    def up_source(t):
        half = (1 - at.c) * (1 - lax.div(t, half_steps)) + at.c * lax.div(t, half_steps)
        return half, half * half_steps + lax.rem(t, half_steps)

    def up_fetch(t):
        return pltpu.make_async_copy(
            inner_in.at[:, lanes_of(up_source(t)[1], tile_lanes)],
            tiles.at[lax.rem(t, 2)],
            tile_sems.at[lax.rem(t, 2)],
        )

    up_fetch(0).start()

    def up_tile(t):
        up_fetch(t).wait()

        @pl.when(t + 1 < steps)
        def _():
            up_fetch(t + 1).start()

        part = dots(low[...], tiles[lax.rem(t, 2)], 0, 0).astype(bf16)
        half = up_source(t)[0]
        grads[2][half, :, :, :, :, lanes_of(lax.rem(t, half_steps), tile_lanes)] = part.reshape(
            4, 2, 2, -1, tile_lanes
        )

        @pl.when(t == half_steps - 1)
        def _():
            for j in (3, 2, 1, 0):
                on_up.give(j)

    in_turn(steps, up_tile, run, plan["up"])
    context_load.wait()
    res_low_load.wait()
    narrow = res_low.shape[1] // 2
    for half in range(2):
        part = dots(context[...], res_low[:, half * narrow : (half + 1) * narrow], 0, 0)
        grads[1][half] = part.astype(bf16).reshape(4, 2, 2, -1, narrow)
    for j in (3, 2, 1, 0):
        on_merge.give(j)
    context_again = load(8, grad_context_in, low)
    bias_sums[...] = jnp.zeros_like(bias_sums)
    mixed_load.wait()
    context_again.wait()
    run(plan["merge"])

    def pair_step(i):
        slot, pair = lax.div(i, 6), lax.rem(i, 6)
        used = jnp.where(slot == 0, lengths[0], lengths[1])
        attend_back_pair(mixed, low, totals, bias_sums, slot, pair, length, used, features)

    in_turn(6 * slots, pair_step, run, plan["attend"])
    tokens_load.wait()
    wide = mixed.shape[1] // 2
    third = wide // 3

    late_low[0] = jnp.concatenate(
        [bias_sums[0:2, 128 * t : 128 * t + 128] for t in range(6)] + [jnp.zeros((4, 128), f32)],
        axis=0,
    )
    late_out[...] = late_low[0]
    late.begin()

    def attn_part(p):
        half = (1 - at.c) * (1 - lax.div(p, 3)) + at.c * lax.div(p, 3)
        cols = lanes_of(half * 3 + lax.rem(p, 3), third)
        part = dots(mid[...], mixed[:, cols], 0, 0).astype(bf16)
        grads[0][half, :, :, :, :, lanes_of(lax.rem(p, 3), third)] = part.reshape(
            4, 2, 2, -1, third
        )

    in_turn(6, attn_part, run, plan["attn"])
    run(plan["before_inputs"])
    attn_load.wait()
    res_load.wait()

    def inputs_part(r):
        here = rows_of(r, length // 2)
        total = grad_inputs[here, :]
        for half in range(2):
            weight = attn[half, :, :, :, :, :wide].reshape(features, wide)
            total = total + dots(mixed[here, half * wide : (half + 1) * wide], weight, 1, 1)
        grad_inputs[here, :] = total

    in_turn(2 * slots, inputs_part, run, plan["inputs"])
    landed_load.wait()
    near_lands = picks[4] == 0
    arrived_saves = []
    for k in range(2):
        rows = pl.ds(k * length // 2, length // 2)

        other = jnp.where(route.stays(), landed[rows, :], a_got[rows, :])
        one = near_got[rows, :]
        near_got[rows, :] = jnp.where(near_lands, one, other)
        landed[rows, :] = jnp.where(near_lands, other, one)
    for k, ref in enumerate((near_got, landed)):
        arrived_saves.append(pltpu.make_async_copy(ref, arrived.at[k], local.at[10 + k]))
        arrived_saves[k].start()
    finish_scatter(at, on_down, None, down_out, None, None, True)
    finish_scatter(at, on_up, up_total, up_out, swap_send.at[2], swap_recv.at[2], False)
    finish_scatter(at, on_merge, merge_total, merge_out, swap_send.at[1], swap_recv.at[1], False)
    own = pl.ds(pl.multiple_of(at.c * small_rows, 8), small_rows)
    small_out[own, :] = small_sum[...]
    last = remote(small_sum, small_out.at[own], swap_send.at[3], swap_recv.at[3], at.sibling())
    last.start()
    run(plan["close"])
    finish_scatter(at, on_attn, attn_total, attn_out, swap_send.at[0], swap_recv.at[0], False)
    last.wait()
    small.finish()
    late.finish()
    route.finish()
    for save in arrived_saves:
        save.wait()
    for chunk in chunks:
        chunk.finish()


def close_backward(
    lengths, picks, totals, pack, mixed, grad_context, tokens, attn, res, active, inner, mid, low,
    context, res_low, near, a, b, mine, landed, shards,
):
    rows, features = tokens.shape
    hidden = active.shape[1]
    vmem = pl.BlockSpec(memory_space=pltpu.VMEM)
    anywhere = pl.BlockSpec(memory_space=pl.ANY)
    scratch = []
    for k, (shard_rows, columns) in enumerate(shards):
        if k < 3:
            tall, width = 2 * shard_rows, columns // 2
            scratch.append(pltpu.VMEM((2, 4, 2, 2, tall, width), bf16))
        else:
            tall, width = shard_rows, columns
            scratch.append(pltpu.VMEM((4, 2, 2, 2, tall, width), bf16))
        scratch += [
            pltpu.VMEM((4, 2, 2, tall, width), bf16),
            pltpu.VMEM((4, 2, tall, width), bf16),
            pltpu.VMEM((4, tall, width), bf16),
            pltpu.VMEM((4, 2, tall, width), bf16),
        ]
    small_rows = pack.shape[0] // 2
    wide = [(2 * r, c // 2) for r, c in shards[:3]]
    scratch += [
        pltpu.VMEM(mixed.shape, bf16),
        pltpu.VMEM(attn.shape, bf16),
        pltpu.VMEM((2, rows, hidden // 8), bf16),
        pltpu.VMEM((rows, features), bf16),
        pltpu.VMEM((rows, features), bf16),
        pltpu.VMEM((rows, features), bf16),
        pltpu.VMEM((rows, features), bf16),
        pltpu.VMEM((8, features), f32),
        pltpu.VMEM((5, small_rows, 128), bf16),
        pltpu.VMEM((5, small_rows, 128), bf16),
        pltpu.VMEM((small_rows, 128), f32),
        pltpu.VMEM((5, 16, 128), f32),
        pltpu.VMEM((5, 16, 128), f32),
        *[pltpu.VMEM(near.shape, bf16)] * 5,
        *[pltpu.VMEM(w, f32) for w in wide],
        pltpu.SemaphoreType.DMA((13,)),
        pltpu.SemaphoreType.DMA((2,)),
        pltpu.SemaphoreType.DMA((2, 5)),
        pltpu.SemaphoreType.DMA((2, 5)),
        pltpu.SemaphoreType.DMA((4,)),
        pltpu.SemaphoreType.DMA((4,)),
        pltpu.SemaphoreType.DMA((Route.SEMS,)),
        pltpu.SemaphoreType.DMA((Route.SEMS,)),
        pltpu.SemaphoreType.DMA((4, Scatter.SEMS)),
        pltpu.SemaphoreType.DMA((4, Scatter.SEMS)),
    ]
    return pl.pallas_call(
        close_kernel,
        out_shape=[jax.ShapeDtypeStruct((rows, features), f32)]
        + [jax.ShapeDtypeStruct(shape, f32) for shape in shards]
        + [
            jax.ShapeDtypeStruct(pack.shape, f32),
            jax.ShapeDtypeStruct((16, 128), f32),
            jax.ShapeDtypeStruct((2,) + near.shape, bf16),
        ],
        in_specs=[pl.BlockSpec(memory_space=pltpu.SMEM)] * 2 + [vmem, vmem] + [anywhere] * 16,
        out_specs=[vmem] * 7 + [anywhere],
        scratch_shapes=scratch,
        compiler_params=pltpu.CompilerParams(
            collective_id=2, has_side_effects=True, vmem_limit_bytes=62 << 20
        ),
        cost_estimate=pl.CostEstimate(
            flops=2 * rows * features * 12 * features, bytes_accessed=60 << 20, transcendentals=0
        ),
    )(
        lengths, picks, totals, pack, mixed, grad_context, tokens, attn, res, active, inner, mid, low,
        context, res_low, near, a, b, mine, landed,
    )


def passed_along(block, axis, distance):
    devices = range(lax.axis_size(axis))
    route = [((i - distance) % len(devices), i) for i in devices]
    return lax.ppermute(block, axis, route)


def product(pattern, left, right):
    return jnp.einsum(pattern, left, right, preferred_element_type=jnp.float32)


def gelu_erf(values):
    return 0.5 * values * (1.0 + jax.scipy.special.erf(values * 0.7071067811865476))


def gelu_slope(values):
    return (
        0.5 * (1.0 + jax.scipy.special.erf(values * 0.7071067811865476))
        + values * jnp.exp(-0.5 * values * values) * 0.3989422804014327
    )


def norm_forward(hidden, norm_gain, norm_shift):
    centred = hidden - jnp.mean(hidden, axis=-1, keepdims=True)
    inverse = lax.rsqrt(jnp.mean(centred * centred, axis=-1, keepdims=True) + eps_norm)
    normed = centred * inverse
    return (normed * norm_gain + norm_shift, normed, inverse)


def norm_backward(grad_out, normed, inverse, norm_gain):
    scaled = grad_out * norm_gain
    return inverse * (
        scaled
        - jnp.mean(scaled, axis=-1, keepdims=True)
        - normed * jnp.mean(scaled * normed, axis=-1, keepdims=True)
    )


def student_head(
    hidden, valid_keys, pool_weight, dense_weight, label_weight, dense_bias, logit_bias
):
    groups, length, features = hidden.shape
    head_size = features // SH
    queries = jnp.einsum("bd,de->be", hidden[:, 0], pool_weight[0], precision=precise).reshape(
        groups, SH, head_size
    )
    key_rows = jnp.einsum("bld,de->ble", hidden, pool_weight[1], precision=precise).reshape(
        groups, length, SH, head_size
    )
    value_rows = jnp.einsum("bld,de->ble", hidden, pool_weight[2], precision=precise).reshape(
        groups, length, SH, head_size
    )
    scores = jnp.einsum("bhe,blhe->bhl", queries, key_rows, precision=precise) / math.sqrt(
        head_size
    )
    scores = jnp.where(valid_keys[:, None, :], scores, neg_big)
    shares = jax.nn.softmax(scores, axis=-1)
    pooled = jnp.einsum("bhl,blhe->bhe", shares, value_rows, precision=precise).reshape(
        groups, features
    )
    dense_out = jnp.tanh(jnp.dot(pooled, dense_weight, precision=precise) + dense_bias)
    return jnp.dot(dense_out, label_weight, precision=precise) + logit_bias


def layer_forward(tokens, valid_keys, weights, student):
    attn_weight, merge_weight, up_weight, down_weight, biases, norm_gains, unit_bias = weights
    proj_weight, pool_weight, dense_weight, label_weight, student_biases, logit_bias = student
    groups, length, features = tokens.shape
    mixed_proj = product("bld,de->ble", tokens, attn_weight)
    queries = (
        (mixed_proj[..., :features] + biases[0])
        .astype(jnp.bfloat16)
        .reshape(groups, length, -1, HD)
    )
    key_rows = (
        mixed_proj[..., features : 2 * features]
        .astype(jnp.bfloat16)
        .reshape(groups, length, -1, HD)
    )
    value_rows = (
        (mixed_proj[..., 2 * features :] + biases[1])
        .astype(jnp.bfloat16)
        .reshape(groups, length, -1, HD)
    )
    scores = product("bqhe,bkhe->bhqk", queries, key_rows) * HD ** (-0.5)
    scores = jnp.where(valid_keys[:, None, None, :], scores, neg_big)
    row_top = jnp.max(scores, axis=-1, keepdims=True)
    exponent = jnp.exp(scores - row_top)
    row_total = jnp.sum(exponent, axis=-1, keepdims=True)
    attn_probs = (exponent / row_total).astype(jnp.bfloat16)
    log_total = row_top + jnp.log(row_total)
    context = (
        product("bhqk,bkhe->bqhe", attn_probs, value_rows)
        .astype(jnp.bfloat16)
        .reshape(groups, length, features)
    )
    attended = product("bld,de->ble", context, merge_weight) + biases[2]
    first_norm, normed_one, inverse_one = norm_forward(
        tokens.astype(jnp.float32) + attended, norm_gains[0], biases[3]
    )
    first_low = first_norm.astype(jnp.bfloat16)
    inner_pre = product("bld,df->blf", first_low, up_weight) + unit_bias
    active = gelu_erf(inner_pre).astype(jnp.bfloat16)
    branch_out = product("blf,fd->bld", active, down_weight) + biases[4]
    second, normed_two, inverse_two = norm_forward(
        first_norm + branch_out, norm_gains[1], biases[5]
    )
    leaving = second.astype(jnp.bfloat16)
    projected = product("bld,de->ble", leaving, proj_weight) + student_biases[0]

    def classify(hidden, attn_part, dense_part, label_part, dense_bias, class_bias):
        return student_head(
            hidden, valid_keys, attn_part, dense_part, label_part, dense_bias, class_bias
        )

    logits, pull_back = jax.vjp(
        classify, projected, pool_weight, dense_weight, label_weight, student_biases[1], logit_bias
    )
    saved_state = (
        tokens,
        valid_keys,
        queries,
        key_rows,
        value_rows,
        log_total,
        context,
        normed_one,
        inverse_one,
        first_low,
        inner_pre,
        active,
        normed_two,
        inverse_two,
        leaving,
        pull_back,
    )
    return (leaving, logits, saved_state)


def layer_backward(saved_state, grad_leaving, grad_logits, weights, proj_weight):
    (
        tokens,
        valid_keys,
        queries,
        key_rows,
        value_rows,
        log_total,
        context,
        normed_one,
        inverse_one,
        first_low,
        inner_pre,
        active,
        normed_two,
        inverse_two,
        leaving,
        pull_back,
    ) = saved_state
    attn_weight, merge_weight, up_weight, down_weight, biases, norm_gains, unit_bias = weights
    groups, length, features = tokens.shape
    grad_proj, grad_pool, grad_dense, grad_label, grad_dense_bias, grad_logit_bias = pull_back(
        grad_logits
    )
    proj_low = grad_proj.astype(jnp.bfloat16)
    grad_proj_weight = product("bld,ble->de", leaving, proj_low)
    grad_second = grad_leaving + product("ble,de->bld", proj_low, proj_weight)
    grad_mid = norm_backward(grad_second, normed_two, inverse_two, norm_gains[1])
    down_low = grad_mid.astype(jnp.bfloat16)
    grad_down = product("blf,bld->fd", active, down_low)
    grad_inner = product("bld,fd->blf", down_low, down_weight) * gelu_slope(inner_pre)
    inner_low = grad_inner.astype(jnp.bfloat16)
    grad_up = product("bld,blf->df", first_low, inner_low)
    grad_first = grad_mid + product("blf,df->bld", inner_low, up_weight)
    grad_res = norm_backward(grad_first, normed_one, inverse_one, norm_gains[0])
    res_low = grad_res.astype(jnp.bfloat16)
    grad_merge = product("blc,bld->cd", context, res_low)
    grad_context = (
        product("bld,cd->blc", res_low, merge_weight)
        .astype(jnp.bfloat16)
        .reshape(groups, length, -1, HD)
    )
    scores = product("bqhe,bkhe->bhqk", queries, key_rows) * HD ** (-0.5)
    scores = jnp.where(valid_keys[:, None, None, :], scores, neg_big)
    attn_probs = jnp.exp(scores - log_total)
    grad_values = product("bhqk,bqhe->bkhe", attn_probs.astype(jnp.bfloat16), grad_context)
    grad_probs = product("bqhe,bkhe->bhqk", grad_context, value_rows)
    grad_scores = (
        attn_probs * (grad_probs - jnp.sum(grad_probs * attn_probs, axis=-1, keepdims=True))
    ).astype(jnp.bfloat16)
    grad_queries = product("bhqk,bkhe->bqhe", grad_scores, key_rows) * HD ** (-0.5)
    grad_keys = product("bhqk,bqhe->bkhe", grad_scores, queries) * HD ** (-0.5)
    grad_queries = grad_queries.reshape(groups, length, features)
    grad_values = grad_values.reshape(groups, length, features)
    grad_mixed = jnp.concatenate(
        [grad_queries, grad_keys.reshape(groups, length, features), grad_values], axis=-1
    )
    mixed_low = grad_mixed.astype(jnp.bfloat16)
    grad_attn = product("bld,ble->de", tokens, mixed_low)
    grad_tokens = grad_res + product("ble,de->bld", mixed_low, attn_weight)
    grad_biases = jnp.stack(
        [
            jnp.sum(grad_queries, axis=(0, 1)),
            jnp.sum(grad_values, axis=(0, 1)),
            jnp.sum(grad_res, axis=(0, 1)),
            jnp.sum(grad_first, axis=(0, 1)),
            jnp.sum(grad_mid, axis=(0, 1)),
            jnp.sum(grad_second, axis=(0, 1)),
        ]
    )
    grad_gains = jnp.stack(
        [
            jnp.sum(grad_first * normed_one, axis=(0, 1)),
            jnp.sum(grad_second * normed_two, axis=(0, 1)),
        ]
    )
    grad_unit = jnp.sum(grad_inner, axis=(0, 1))
    grad_student_biases = jnp.stack([jnp.sum(grad_proj, axis=(0, 1)), grad_dense_bias])
    layer_terms = (grad_attn, grad_merge, grad_up, grad_down, grad_biases, grad_gains, grad_unit)
    student_terms = (
        grad_proj_weight,
        grad_pool,
        grad_dense,
        grad_label,
        grad_student_biases,
        grad_logit_bias,
    )
    return (grad_tokens, layer_terms, student_terms)


BOTH = ("batch", "zero")


def swapped(pair, straight):
    return jnp.where(straight, pair[0], pair[1]), jnp.where(straight, pair[1], pair[0])


def shifted(block, distance):
    return passed_along(block, "batch", distance)


def by_steps(far, other, steps, sign):
    for step in steps:
        moved = shifted(far, sign * step)
        far = jnp.where(other // step % 2 == 1, moved, far)
    return far


def routing(routes, slot_count):
    batch_count, zero_count = lax.axis_size("batch"), lax.axis_size("zero")
    offsets = routes // (slot_count * zero_count) - lax.axis_index("batch")
    offsets = (offsets + batch_count) % batch_count
    one_back = offsets[0] == batch_count - 1
    lands_first = routes[0] % slot_count == 0
    return one_back, lands_first, jnp.where(one_back, offsets[1], offsets[0])


def on_device_linked(
    inputs, lengths, exits, routes, attn_weight, merge_weight, up_weight, down_weight,
    layer_biases, norm_gains, unit_bias, proj_weight, pool_weight, dense_weight,
    label_weight, student_biases, logit_bias, grad_act, grad_logits,
):
    slot_count, length, features = inputs.shape
    rows = slot_count * length
    sent = exits > LAYER
    one_back, lands_first, other = routing(routes, slot_count)
    near_slot = jnp.where(one_back, 0, 1)
    near_lands = jnp.where(one_back == lands_first, 0, 1)
    flags = [sent[k].astype(jnp.int32) for k in range(slot_count)]
    tokens = inputs.reshape(rows, features)
    (
        mixed, context, totals, attn_all, merge_all, up_all, down_all, vectors, units,
        normed_one, inverse_one, first_low, active, slope, normed_two, inverse_two, leaving,
        grad_leaving,
    ) = forward_layer(
        lengths,
        jnp.stack([near_lands, 8 - other, near_slot, *flags]),
        tokens,
        attn_weight, merge_weight, up_weight, down_weight, layer_biases, norm_gains, unit_bias,
        grad_act,
    )
    grad_leaving = grad_leaving.reshape(rows, features)
    route = jnp.stack([other, near_slot, *flags, near_lands])
    (
        logits, pack, *moving, mid_low, inner_low, res, res_low, grad_context
    ) = rows_backward(
        lengths,
        route,
        leaving,
        (proj_weight, pool_weight, dense_weight, label_weight, student_biases, logit_bias),
        grad_logits,
        (
            merge_all.reshape(2, features, -1),
            up_all.reshape(2, features, -1),
            down_all.reshape(-1, features),
        ),
        vectors,
        grad_leaving,
        (normed_one, inverse_one, normed_two, inverse_two, slope),
    )
    shards = [w.shape for w in (attn_weight, merge_weight, up_weight, down_weight)]
    (
        grad_tokens, attn_grad, merge_grad, up_grad, down_grad, small, late, arrived
    ) = close_backward(
        lengths, route, totals, pack, mixed, grad_context, tokens, attn_all, res, active, inner_low,
        mid_low, first_low, context, res_low, *moving, shards,
    )
    lanes = proj_weight.shape[1]
    classes = label_weight.shape[1]
    row = features + 4 * lanes
    tail = row + 24
    mine = lax.axis_index("batch") * lax.axis_size("zero") + lax.axis_index("zero")
    vector_grads = small[tail : tail + 48].reshape(6, 8, 128).transpose(1, 0, 2).reshape(8, features)
    shard = features // (lax.axis_size("batch") * lax.axis_size("zero"))
    early = late[:12].reshape(6, 2, 128).transpose(1, 0, 2).reshape(2, features)
    vector_grads = jnp.concatenate([early, vector_grads[2:]])
    vector_grads = lax.dynamic_slice_in_dim(vector_grads, mine * shard, shard, 1)
    unit_grads = small[tail + 48 :].reshape(-1)
    return (
        arrived,
        logits[:slot_count, :classes],
        grad_tokens.reshape(inputs.shape),
        attn_grad,
        merge_grad,
        up_grad,
        down_grad,
        vector_grads[:6],
        vector_grads[6:],
        lax.dynamic_slice_in_dim(unit_grads, mine * unit_bias.shape[0], unit_bias.shape[0]),
        small[:features],
        small[features : features + 3 * lanes].reshape(3, lanes, lanes),
        small[features + 3 * lanes : row],
        small[row : row + classes].T,
        jnp.stack([small[row + 16], small[row + 17]]),
        small[row + 18, :classes],
    )


def whole_gather(attn, merge, up, down, biases, gains, unit):
    return (
        lax.all_gather(attn, BOTH, axis=0, tiled=True),
        lax.all_gather(merge, BOTH, axis=0, tiled=True),
        lax.all_gather(up, BOTH, axis=0, tiled=True),
        lax.all_gather(down, BOTH, axis=0, tiled=True),
        lax.all_gather(biases, BOTH, axis=1, tiled=True).astype(f32),
        lax.all_gather(gains, BOTH, axis=1, tiled=True).astype(f32),
        lax.all_gather(unit, BOTH, axis=0, tiled=True).astype(f32),
    )


def on_device(
    inputs, lengths, exits, routes, attn_weight, merge_weight, up_weight, down_weight,
    layer_biases, norm_gains, unit_bias, proj_weight, pool_weight, dense_weight,
    label_weight, student_biases, logit_bias, grad_act, grad_logits,
):
    slot_count, length, features = inputs.shape
    section_count = (lax.axis_size("batch") - 1).bit_length()
    steps = [1 << level for level in range(section_count)]
    student = (proj_weight, pool_weight, dense_weight, label_weight, student_biases, logit_bias)
    sent = exits > LAYER
    one_back, lands_first, other = routing(routes, slot_count)
    near, far = swapped(swapped(grad_act, lands_first), one_back)
    near, far = shifted(near, 1), by_steps(far, other, steps, -1)
    grad_leaving = jnp.stack(swapped((near, far), one_back)).astype(f32)
    grad_leaving = jnp.where(sent[:, None, None], grad_leaving, 0.0)
    weights = whole_gather(
        attn_weight, merge_weight, up_weight, down_weight, layer_biases, norm_gains, unit_bias
    )
    valid_all = jnp.arange(length)[None, :] < lengths[:, None]
    leaving, logits, saved_state = layer_forward(inputs, valid_all, weights, student)
    pieces = jnp.where(sent[:, None, None], leaving, jnp.zeros_like(leaving))
    near, far = swapped(pieces, one_back)
    near, far = shifted(near, -1), by_steps(far, other, steps, 1)
    arrived = jnp.stack(swapped(swapped((near, far), one_back), lands_first))
    grad_tokens, layer_sum, student_sum = layer_backward(
        saved_state, grad_leaving, grad_logits, weights, proj_weight
    )
    layer_grads = [
        lax.psum_scatter(term, BOTH, scatter_dimension=int(k in (4, 5)), tiled=True)
        for k, term in enumerate(layer_sum)
    ]
    student_grads = lax.psum(student_sum, BOTH)
    return (arrived, logits, grad_tokens, *layer_grads, *student_grads)


def solution(mesh):
    in_specs = (
        P(("batch", "zero"), None, None),
        P(("batch", "zero")),
        P(("batch", "zero")),
        P(("batch", "zero")),
        P(("batch", "zero"), None),
        P(("batch", "zero"), None),
        P(("batch", "zero"), None),
        P(("batch", "zero"), None),
        P(None, ("batch", "zero")),
        P(None, ("batch", "zero")),
        P(("batch", "zero")),
        P(),
        P(),
        P(),
        P(),
        P(),
        P(),
        P(("batch", "zero"), None, None),
        P(("batch", "zero"), None),
    )
    out_specs = (
        P(("batch", "zero"), None, None),
        P(("batch", "zero"), None),
        P(("batch", "zero"), None, None),
        P(("batch", "zero"), None),
        P(("batch", "zero"), None),
        P(("batch", "zero"), None),
        P(("batch", "zero"), None),
        P(None, ("batch", "zero")),
        P(None, ("batch", "zero")),
        P(("batch", "zero")),
        P(),
        P(),
        P(),
        P(),
        P(),
        P(),
    )
    linked = (mesh.shape["batch"], mesh.shape["zero"]) == (8, 4)
    return jax.shard_map(
        on_device_linked if linked else on_device, mesh=mesh, in_specs=in_specs, out_specs=out_specs, check_vma=False
    )
```

```python
import functools
import math

import jax
import jax.numpy as jnp
from jax import lax
from jax.experimental import pallas as pl
from jax.experimental.pallas import tpu as pltpu
from jax.sharding import PartitionSpec as P

HD = 64
SH = 2
LAYER = 4

precise = lax.Precision.HIGHEST
eps_norm = 1e-12
neg_big = -1e30


MESH = pl.DeviceIdType.MESH
f32 = jnp.float32
bf16 = jnp.bfloat16
SMALL = 128


class Place:
    def __init__(self):
        batch, zero = lax.axis_index("batch"), lax.axis_index("zero")
        self.z, self.x = lax.div(batch, 2), lax.rem(batch, 2)
        self.y, self.c = lax.div(zero, 2), lax.rem(zero, 2)

    def device(self, z=None, x=None, y=None, c=None):
        z = self.z if z is None else z
        x = self.x if x is None else x
        y = self.y if y is None else y
        c = self.c if c is None else c
        return (z * 2 + x, y * 2 + c)

    def sibling(self):
        return self.device(c=1 - self.c)

    def greet(self, far=False, routes=False):
        barrier = pltpu.get_barrier_semaphore()

        def call(device):
            pl.semaphore_signal(barrier, inc=1, device_id=device, device_id_type=MESH)

        call(self.sibling())
        call(self.device(x=1 - self.x))
        call(self.device(y=1 - self.y))

        @pl.when(self.z > 0)
        def _():
            call(self.device(z=self.z - 1))

        @pl.when(self.z < 3)
        def _():
            call(self.device(z=self.z + 1))

        if far:
            call(self.device(z=lax.rem(self.z + 2, 4)))
        if routes:
            call(self.ring(1))
            call(self.ring(7))
        inner = lax.rem(lax.div(self.z + 1, 2), 2)
        pl.semaphore_wait(barrier, 4 + inner + (1 if far else 0) + (2 if routes else 0))

    def ring(self, step):
        batch = lax.rem(2 * self.z + self.x + step, 8)
        return (batch, 2 * self.y + self.c)

    def order(self, j):
        low = lax.div(3 - self.z, 2)
        near = self.z * low + (3 - self.z) * (1 - low)
        if j < 2:
            turned = near * (1 - j) + (1 - near) * j
        else:
            turned = j
        return turned * low + (3 - turned) * (1 - low)

    def first_way(self, zb, mixed=True):
        odd = lax.rem(zb, 2) if mixed else 0
        return (
            self.x * odd + (1 - self.x) * (1 - odd),
            self.y * (1 - odd) + (1 - self.y) * odd,
        )

    def second_way(self, zb, mixed=True):
        odd = lax.rem(zb, 2) if mixed else 0
        return (
            self.x * (1 - odd) + (1 - self.x) * odd,
            self.y * odd + (1 - self.y) * (1 - odd),
        )


class Picks:
    def __init__(self, at, routes, exits):
        batch = 2 * at.z + at.x
        offsets = [lax.rem(lax.div(routes[k], 8) - batch + 8, 8) for k in range(2)]
        self.near_first = offsets[0] == 7
        self.shift = jnp.where(self.near_first, offsets[1], offsets[0])
        straight = lax.rem(routes[0], 2) == 0
        self.near_lands_first = self.near_first == straight
        self.sent = [exits[k] > LAYER for k in range(2)]


def remote(src, dst, send_sem, recv_sem, device):
    return pltpu.make_async_remote_copy(
        src_ref=src,
        dst_ref=dst,
        send_sem=send_sem,
        recv_sem=recv_sem,
        device_id=device,
        device_id_type=MESH,
    )


class Gather:
    SEMS = 24

    def __init__(self, at, block, line, send, recv, mixed=True):
        self.mixed = mixed
        self.at, self.block, self.line, self.send, self.recv = at, block, line, send, recv

    def move(self, view, k, device, recv_k=None):
        recv_k = k if recv_k is None else recv_k
        return remote(view, view, self.send.at[k], self.recv.at[recv_k], device)

    def hop(self, zb, step):
        at = self.at
        return self.move(
            self.block(zb, at.x, at.y, at.c),
            zb if step > 0 else zb + 20,
            at.device(z=at.z + step),
            recv_k=zb,
        )

    def first(self, zb, coming=False):
        at = self.at
        x, y = at.first_way(zb, self.mixed)
        view = self.block(zb, x, y, at.c) if coming else self.block(zb, at.x, at.y, at.c)
        return self.move(view, zb + 4, at.device(x=x, y=y))

    def second(self, zb, coming=False):
        at = self.at
        x, y = at.second_way(zb, self.mixed)
        view = self.block(zb, x, y, at.c) if coming else self.block(zb, at.x, at.y, at.c)
        return self.move(view, zb + 8, at.device(x=x, y=y))

    def corner(self, zb, coming=False):
        at = self.at
        x, y = at.second_way(zb, self.mixed)
        if coming:
            view = self.block(zb, 1 - at.x, 1 - at.y, at.c)
        else:
            view = self.block(zb, *at.first_way(zb, self.mixed), at.c)
        return self.move(view, zb + 12, at.device(x=x, y=y))

    def across(self, zb, coming=False):
        at = self.at
        return self.move(self.line(zb, 1 - at.c if coming else at.c), zb + 16, at.sibling())

    def arrive(self, j):
        at = self.at
        zb = at.order(j)
        if j > 0:
            self.hop(zb, 1).wait_recv()

        @pl.when(jnp.logical_and(zb <= at.z, at.z < 3))
        def _():
            self.hop(zb, 1).start()

        @pl.when(jnp.logical_and(zb >= at.z, at.z > 0))
        def _():
            self.hop(zb, -1).start()

        self.first(zb).start()
        self.second(zb).start()

    def turn(self, j):
        zb = self.at.order(j)
        self.first(zb, coming=True).wait_recv()
        self.corner(zb).start()

    def share(self, j):
        zb = self.at.order(j)
        self.second(zb, coming=True).wait_recv()
        self.corner(zb, coming=True).wait_recv()
        self.across(zb).start()

    def settle(self, j):
        self.across(self.at.order(j), coming=True).wait_recv()

    def finish(self):
        at = self.at
        for j in range(4):
            zb = at.order(j)

            @pl.when(jnp.logical_and(zb <= at.z, at.z < 3))
            def _():
                self.hop(zb, 1).wait_send()

            @pl.when(jnp.logical_and(zb >= at.z, at.z > 0))
            def _():
                self.hop(zb, -1).wait_send()

            self.first(zb).wait_send()
            self.second(zb).wait_send()
            self.corner(zb).wait_send()
            self.across(zb).wait_send()


def add_into(total, term):
    total[...] = (total[...].astype(f32) + term[...].astype(f32)).astype(bf16)


class Scatter:
    SEMS = 24

    def __init__(
        self, at, block, line, from_core, from_second, from_first, from_line, send, recv, mixed=True
    ):
        self.mixed = mixed
        self.at, self.block, self.line = at, block, line
        self.from_core, self.from_second = from_core, from_second
        self.from_first, self.from_line = from_first, from_line
        self.send, self.recv = send, recv

    def move(self, src, dst, k, device):
        return remote(src, dst, self.send.at[k], self.recv.at[k], device)

    def across(self, zb):
        at = self.at
        return self.move(self.line(zb, 1 - at.c), self.from_core.at[zb], zb, at.sibling())

    def second(self, zb):
        at = self.at
        x, y = at.second_way(zb, self.mixed)
        return self.move(
            self.block(zb, x, y, at.c), self.from_second.at[zb, 0], zb + 4, at.device(x=x, y=y)
        )

    def corner(self, zb):
        at = self.at
        x, y = at.second_way(zb, self.mixed)
        return self.move(
            self.block(zb, 1 - at.x, 1 - at.y, at.c),
            self.from_second.at[zb, 1],
            zb + 8,
            at.device(x=x, y=y),
        )

    def first(self, zb):
        at = self.at
        x, y = at.first_way(zb, self.mixed)
        return self.move(
            self.block(zb, x, y, at.c), self.from_first.at[zb], zb + 12, at.device(x=x, y=y)
        )

    def hop(self, zb, step):
        at = self.at
        side = 0 if step > 0 else 1
        return self.move(
            self.block(zb, at.x, at.y, at.c),
            self.from_line.at[zb, side],
            zb + 16 + 4 * side,
            at.device(z=at.z + step),
        )

    def give(self, j):
        self.across(self.at.order(j)).start()

    def join(self, j):
        at = self.at
        zb = at.order(j)
        self.across(zb).wait_recv()

        def one(k, carry):
            x, y = lax.div(k, 2), lax.rem(k, 2)
            add_into(self.block(zb, x, y, at.c), self.from_core.at[zb, x, y])
            return carry

        lax.fori_loop(0, 4, one, 0)
        self.second(zb).start()
        self.corner(zb).start()

    def halve(self, j):
        at = self.at
        zb = at.order(j)
        self.second(zb).wait_recv()
        self.corner(zb).wait_recv()
        x, y = at.first_way(zb, self.mixed)
        add_into(self.block(zb, x, y, at.c), self.from_second.at[zb, 1])
        self.first(zb).start()
        add_into(self.block(zb, at.x, at.y, at.c), self.from_second.at[zb, 0])

    def leave(self, j):
        at = self.at
        zb = at.order(j)
        mine = self.block(zb, at.x, at.y, at.c)
        self.first(zb).wait_recv()
        add_into(mine, self.from_first.at[zb])

        @pl.when(jnp.logical_and(zb >= at.z, at.z > 0))
        def _():
            self.hop(zb, 1).wait_recv()
            add_into(mine, self.from_line.at[zb, 0])

        @pl.when(jnp.logical_and(zb <= at.z, at.z < 3))
        def _():
            self.hop(zb, -1).wait_recv()
            add_into(mine, self.from_line.at[zb, 1])

        @pl.when(zb > at.z)
        def _():
            self.hop(zb, 1).start()

        @pl.when(zb < at.z)
        def _():
            self.hop(zb, -1).start()

    def finish(self):
        at = self.at
        for j in range(4):
            zb = at.order(j)
            self.across(zb).wait_send()
            self.second(zb).wait_send()
            self.corner(zb).wait_send()
            self.first(zb).wait_send()

            @pl.when(zb > at.z)
            def _():
                self.hop(zb, 1).wait_send()

            @pl.when(zb < at.z)
            def _():
                self.hop(zb, -1).wait_send()


class Route:
    PARTS = 4
    BUFFERS = 10
    SEMS = 7 * PARTS + 1

    def __init__(self, at, buffers, send, recv, near_step, shift):
        self.at, self.send, self.recv, self.near_step = at, send, recv, near_step
        (
            self.near, self.near_got, self.far, self.other, self.mine, self.end,
            self.a, self.b, self.a_got, self.b_got,
        ) = buffers
        self.size = self.far.shape[0] // self.PARTS
        low = lax.div(3 - at.z, 2)
        self.outer = lax.rem(lax.div(at.z + 1, 2), 2) == 0
        inward = 2 * low - 1
        self.inward = at.device(z=at.z + inward)
        side = lax.rem(lax.div(at.z + 1, 2), 2)
        self.outward = at.device(z=at.z + inward * (1 - 2 * side))
        self.odd = lax.rem(shift, 2) == 1
        up = lax.rem(lax.div(shift + lax.rem(shift + at.x, 2), 2), 4)
        self.up = up * low + lax.rem(4 - up, 4) * (1 - low)

    def part(self, ref, k):
        return ref.at[pl.ds(k * self.size, self.size), :]

    def move(self, src, dst, k, sem, device):
        sem = sem * self.PARTS + k + 1
        return remote(
            self.part(src, k), self.part(dst, k), self.send.at[sem], self.recv.at[sem], device
        )

    def near_move(self):
        return remote(
            self.near, self.near_got, self.send.at[0], self.recv.at[0], self.at.ring(self.near_step)
        )

    def x_move(self, k):
        return self.move(self.far, self.other, k, 0, self.at.device(x=1 - self.at.x))

    def in_move(self, k):
        return self.move(self.mine, self.end, k, 1, self.inward)

    def a_move(self, k):
        return self.move(self.a, self.a_got, k, 2, self.inward)

    def b_move(self, k):
        return self.move(self.b, self.b_got, k, 3, self.inward)

    def out_move(self, k):
        return self.move(self.other, self.end, k, 4, self.outward)

    def start(self):
        for k in range(self.PARTS):
            self.x_move(k).start()

    def step(self):
        self.near_move().start()

    def turn(self, k):
        self.x_move(k).wait_recv()
        mine, other = self.part(self.mine, k), self.part(self.other, k)
        mine[...] = jnp.where(self.odd, other[...], self.part(self.far, k)[...])

        @pl.when(self.outer)
        def _():
            self.in_move(k).start()

    def cross(self, k):
        @pl.when(jnp.logical_not(self.outer))
        def _():
            self.in_move(k).wait_recv()
            mine, end = self.part(self.mine, k)[...], self.part(self.end, k)[...]
            self.part(self.b, k)[...] = jnp.where(self.up == 2, mine, end)
            self.b_move(k).start()
            self.part(self.a, k)[...] = jnp.where(self.up == 1, mine, end)
            self.a_move(k).start()

    def hand(self, k):
        @pl.when(jnp.logical_not(self.outer))
        def _():
            self.b_move(k).wait_recv()
            self.part(self.other, k)[...] = jnp.where(
                self.up == 3, self.part(self.mine, k)[...], self.part(self.b_got, k)[...]
            )
            self.out_move(k).start()

    def land(self, k):
        self.x_move(k).wait_send()
        far, mine, end = self.part(self.far, k), self.part(self.mine, k), self.part(self.end, k)

        @pl.when(self.outer)
        def _():
            self.out_move(k).wait_recv()
            far[...] = jnp.where(self.up == 0, mine[...], end[...])

        @pl.when(jnp.logical_not(self.outer))
        def _():
            self.a_move(k).wait_recv()
            moved = jnp.where(self.up == 1, end[...], self.part(self.a_got, k)[...])
            far[...] = jnp.where(self.up == 0, mine[...], moved)

    def finish(self):
        self.near_move().wait_send()
        for k in range(self.PARTS):

            @pl.when(self.outer)
            def _():
                self.in_move(k).wait_send()

            @pl.when(jnp.logical_not(self.outer))
            def _():
                self.a_move(k).wait_send()
                self.b_move(k).wait_send()
                self.out_move(k).wait_send()


class RouteStart(Route):
    def settle(self, k, a_out, b_out, mine_out, landed):
        rows = pl.ds(k * self.size, self.size)
        mine = self.part(self.mine, k)
        mine_out[rows, :] = mine[...]

        @pl.when(self.outer)
        def _():
            landed[rows, :] = mine[...]

        @pl.when(jnp.logical_not(self.outer))
        def _():
            self.in_move(k).wait_recv()
            end = self.part(self.end, k)
            a_out[rows, :] = jnp.where(self.up == 1, mine[...], end[...])
            b_out[rows, :] = jnp.where(self.up == 2, mine[...], end[...])
            landed[rows, :] = jnp.where(self.up == 0, mine[...], end[...])

    def finish(self):
        for k in range(self.PARTS):
            self.x_move(k).wait_send()

            @pl.when(self.outer)
            def _():
                self.in_move(k).wait_send()


class RouteEnd(Route):
    def __init__(self, at, near, near_got, a, b, mine, a_got, b_got, send, recv, shift):
        super().__init__(
            at, (near, near_got, a, b_got, mine, a_got, a, b, a_got, b_got), send, recv, 7, shift
        )

    def cross(self, k):
        @pl.when(jnp.logical_not(self.outer))
        def _():
            self.b_move(k).start()
            self.a_move(k).start()

    def hand(self, k):
        @pl.when(jnp.logical_not(self.outer))
        def _():
            self.b_move(k).wait_recv()
            onward = self.part(self.b_got, k)
            onward[...] = jnp.where(self.up == 3, self.part(self.mine, k)[...], onward[...])
            self.out_move(k).start()

    def take(self, k):
        @pl.when(self.outer)
        def _():
            self.out_move(k).wait_recv()

        @pl.when(jnp.logical_not(self.outer))
        def _():
            self.a_move(k).wait_recv()

    def join(self):
        self.near_move().wait_recv()

    def stays(self):
        return jnp.logical_or(self.up == 0, jnp.logical_and(self.up == 1, jnp.logical_not(self.outer)))

    def finish(self):
        self.near_move().wait_send()
        for k in range(self.PARTS):

            @pl.when(jnp.logical_not(self.outer))
            def _():
                self.a_move(k).wait_send()
                self.b_move(k).wait_send()
                self.out_move(k).wait_send()


class Butterfly:
    def __init__(self, at, total, low, got, send, recv, halves):
        self.at, self.total, self.low, self.got = at, total, low, got
        self.send, self.recv, self.halves = send, recv, halves
        self.partners = (
            at.sibling(),
            at.device(y=1 - at.y),
            at.device(x=1 - at.x),
            at.device(z=at.z + 1 - 2 * lax.rem(at.z, 2)),
            at.device(z=lax.rem(at.z + 2, 4)),
        )

    def move(self, k):
        return remote(
            self.low.at[k], self.got.at[k], self.send.at[k], self.recv.at[k], self.partners[k]
        )

    def begin(self):
        self.move(0).start()

    def step(self, k):
        self.move(k).wait_recv()
        total = self.total[...] + self.got[k].astype(f32)
        if k < 4:
            kept = total.astype(self.low.dtype)
            self.low[k + 1] = kept
            total = kept.astype(f32)
        self.total[...] = total
        if k < 4:
            self.move(k + 1).start()

    def finish(self):
        for k in range(5):
            self.move(k).wait_send()


def in_turn(count, body, run, plan):
    def one(i, carry):
        for when, events in plan.items():

            @pl.when(i == when)
            def _():
                run(events)

        body(i)
        return carry

    lax.fori_loop(0, count, one, 0)


def wide_block(ref):
    return (lambda z, x, y, c: ref.at[c, z, x, y]), (lambda z, c: ref.at[c, z])


def tall_block(ref):
    return (lambda z, x, y, c: ref.at[z, x, y, c]), (lambda z, c: ref.at[z, :, :, c])


def take_half(ref, c):
    width = ref.shape[1] // 2
    return ref[:, pl.ds(pl.multiple_of(c * width, 128), width)].astype(f32)


def finish_scatter(at, chunk, total, out, swap_send, swap_recv, tall):
    mine = chunk.block(at.z, at.x, at.y, at.c)
    if tall:
        out[...] = mine[...].astype(f32)
        return
    total[...] = mine[...].astype(f32)
    rows, width = out.shape[0], out.shape[1] // 2
    here = pl.ds(pl.multiple_of(at.c * width, 128), width)
    there = pl.ds(pl.multiple_of((1 - at.c) * width, 128), width)
    swap = remote(
        total.at[pl.ds(pl.multiple_of((1 - at.c) * rows, 8), rows)],
        out.at[:, here],
        swap_send,
        swap_recv,
        at.sibling(),
    )
    swap.start()
    out[:, here] = total[pl.ds(pl.multiple_of(at.c * rows, 8), rows), :]
    remote(
        total.at[pl.ds(pl.multiple_of((1 - at.c) * rows, 8), rows)],
        out.at[:, there],
        swap_send,
        swap_recv,
        at.sibling(),
    ).wait_recv()
    swap.wait_send()


def dots(left, right, over_left, over_right):
    return lax.dot_general(
        left, right, (((over_left,), (over_right,)), ((), ())), preferred_element_type=f32
    )


def rows_of(i, size):
    return pl.ds(pl.multiple_of(i * size, size), size)


def lanes_of(i, size=128):
    return pl.ds(pl.multiple_of(i * size, size), size)


def unpack_small(attn_all, vectors, units, shard):
    halves, width = attn_all.shape[-2:]
    lanes = pl.ds(width - SMALL, SMALL)
    lane = lax.broadcasted_iota(jnp.int32, (8, SMALL), 1)
    for ref, rows, size in ((vectors, 0, shard), (units, 8, 4 * shard)):
        tiles = [jnp.zeros((8, SMALL), f32) for _ in range(ref.shape[1] // SMALL)]
        for n in range(32):
            chip, core = n // 2, n % 2
            piece = attn_all[0, chip // 4, chip // 2 % 2, chip % 2, :, lanes].astype(f32)
            piece = piece[core * shard + rows : core * shard + rows + 8]
            tile, shift = n * size // SMALL, n * size % SMALL
            if shift:
                piece = pltpu.roll(piece, shift, 1)
            tiles[tile] = tiles[tile] + jnp.where(lane >= shift, piece, 0.0)
            if shift + size > SMALL:
                tiles[tile + 1] = tiles[tile + 1] + jnp.where(lane < shift, piece, 0.0)
        for t, tile in enumerate(tiles):
            ref[:, t * SMALL : (t + 1) * SMALL] = tile[: ref.shape[0]]


def project_half(tokens, weights, vectors, mixed, slot, length, half):
    features = tokens.shape[1]
    width = 3 * features // 2
    here = pl.ds(slot * length, length)
    for part in range(2):
        size = features if (part == half) else width - features
        start = 0 if part == 0 else width - size
        out = jnp.dot(tokens[here, :], weights(half, start, size), preferred_element_type=f32)
        if part == half:
            out = out + vectors[half : half + 1, :]
        mixed[here, half * width + start : half * width + start + size] = out.astype(bf16)


def attend_pair(mixed, context, totals, slot, pair, length, used):
    features = context.shape[1]
    here = pl.ds(slot * length, length) if isinstance(slot, int) else rows_of(slot, length)
    base = pl.multiple_of(pair * 128, 128)
    two_q = mixed[here, pl.ds(base, 128)]
    two_k = mixed[here, pl.ds(pl.multiple_of(base + features, 128), 128)]
    two_v = mixed[here, pl.ds(pl.multiple_of(base + 2 * features, 128), 128)]
    low = lax.broadcasted_iota(jnp.int32, two_k.shape, 1) < HD
    valid = lax.broadcasted_iota(jnp.int32, (length, 1), 0) < used
    none = jnp.zeros_like(two_k)
    two_q = two_q * jnp.asarray(HD ** (-0.5), bf16)
    outs = []
    for head in range(2):
        keys = jnp.where(low if head == 0 else ~low, two_k, none)
        scores = jnp.where(valid, dots(keys, two_q, 1, 1), neg_big)
        top = jnp.max(scores, axis=0, keepdims=True)
        powers = jnp.exp(scores - top)
        total = jnp.sum(powers, axis=0, keepdims=True)
        shares = (powers * (1.0 / total)).astype(bf16)
        outs.append(dots(shares, two_v, 0, 0))
        totals[slot, pl.ds(2 * pair + head, 1), :] = top + jnp.log(total)
    context[here, pl.ds(base, 128)] = jnp.where(low, outs[0], outs[1]).astype(bf16)


def norm_rows(hidden, gain, shift):
    centred = hidden - jnp.mean(hidden, axis=-1, keepdims=True)
    inverse = lax.rsqrt(jnp.mean(centred * centred, axis=-1, keepdims=True) + eps_norm)
    normed = centred * inverse
    return normed * gain + shift, normed, inverse


def gelu_both(v):
    size = jnp.abs(v) * 0.7071067811865476
    t = 1.0 / (1.0 + 0.3275911 * size)
    bell = jnp.exp(-0.5 * v * v)
    poly = t * (
        0.254829592
        + t * (-0.284496736 + t * (1.421413741 + t * (-1.453152027 + t * 1.061405429)))
    )
    tail = 0.5 * poly * bell
    share = jnp.where(v < 0.0, tail, 1.0 - tail)
    return v * share, share + v * bell * 0.3989422804014327


def first_rows(tokens, context, merge, up, vectors, units, first, outs, r, size):
    normed_out, inverse_out, low_out, active_out, slope_out = outs
    here = rows_of(r, size)
    attended = jnp.concatenate(
        [jnp.dot(context[here, :], merge(h), preferred_element_type=f32) for h in range(2)], axis=1
    )
    hidden = tokens[here, :].astype(f32) + (attended + vectors[2:3, :])
    full, normed, inverse = norm_rows(hidden, vectors[6:7, :], vectors[3:4, :])
    first[here, :] = full
    low = full.astype(bf16)
    normed_out[here, :] = normed.astype(bf16)
    inverse_out[here, :] = inverse
    low_out[here, :] = low
    width = units.shape[1] // 2
    step = width // 2
    for part in range(4):
        cols = pl.ds(part * step, step)
        inner = jnp.dot(low, up(part // 2, part % 2 * step, step), preferred_element_type=f32)
        active, slope = gelu_both(inner + units[0:1, cols])
        active_out[here, cols] = active.astype(bf16)
        slope_out[here, cols] = slope.astype(bf16)


def second_rows(active, down, vectors, first, outs, r, size, features):
    normed_out, inverse_out, leaving_out = outs
    here = rows_of(r, size)
    branch = jnp.dot(
        active[here, :], down[...].reshape(-1, features), preferred_element_type=f32
    )
    hidden = first[here, :] + (branch + vectors[4:5, :])
    full, normed, inverse = norm_rows(hidden, vectors[7:8, :], vectors[5:6, :])
    normed_out[here, :] = normed.astype(bf16)
    inverse_out[here, :] = inverse
    leaving_out[here, :] = full.astype(bf16)


FORWARD_PLAN = {
    "open": ("m.begin", "a.begin", "d.arrive.0", "u.begin",),
    "gather": (
        "a.arrive.1", "m.turn.0", "m.arrive.1", "a.arrive.2", "a.turn.0", "a.turn.1",
        "a.arrive.3", "u.arrive.1", "a.turn.2", "a.turn.3", "m.turn.1", "u.arrive.2", "u.turn.1",
        "a.share.1", "a.share.0", "m.arrive.2", "a.share.2", "r.start", "u.arrive.3",
        "d.arrive.1", "a.settle.2", "a.share.3", "a.settle.3", "a.settle.0", "a.settle.1",
    ),
    "project": (
        (),
        ("r.turn.0", "m.arrive.3",),
        (),
        ("u.turn.2", "u.turn.0",),
    ),
    "attend": {
        0: ("d.arrive.2",),
        1: ("u.share.1", "m.share.1", "m.turn.2", "m.share.0",),
        3: ("r.turn.2", "r.cross.0", "r.turn.1", "m.settle.1", "d.arrive.3", "u.share.0",),
        4: ("r.step",),
        5: ("u.share.2", "u.settle.1",),
        6: ("r.cross.2", "u.turn.3",),
        7: ("u.settle.2",),
        8: ("m.share.2", "m.turn.3", "m.settle.0",),
        9: ("m.settle.2", "d.turn.1",),
        10: ("u.share.3", "d.turn.2", "m.share.3", "r.turn.3", "u.settle.0",),
        11: ("d.turn.3",),
    },
    "before_first": ("m.settle.3", "u.settle.3",),
    "first": {
        0: ("d.share.1",),
        1: ("d.turn.0", "r.cross.1", "r.hand.0",),
        2: ("d.share.2", "r.hand.2", "r.cross.3",),
        3: ("d.settle.2", "d.share.3", "r.hand.1", "d.share.0",),
    },
    "before_second": ("d.settle.1", "d.settle.3", "d.settle.0",),
    "second": {
        1: ("r.hand.3",),
        2: ("r.land.0", "r.land.2",),
    },
    "close": ("r.land.3", "r.land.1",),
}


def forward_kernel(
    lengths, exits, routes, tokens, attn, merge, up, down, biases, gains, unit, grad_act,
    mixed_out, context_out, totals, attn_out, merge_out, up_out, down_out, vectors, units,
    normed_one, inverse_one, low, active_out, slope_out, normed_two, inverse_two, leaving,
    grad_leaving,
    attn_all, merge_all, up_all, down_all, mixed, context, active, slope, first,
    attn_mine, merge_mine, up_mine, attn_pair, merge_pair, up_pair, *scratch,
):
    at = Place()
    route_buffers = scratch[: Route.BUFFERS]
    send, recv, swap_send, swap_recv, local, route_send, route_recv = scratch[Route.BUFFERS :]
    shard = attn.shape[0]
    own = pl.ds(pl.multiple_of(at.c * shard, 8), shard)
    lanes = attn.shape[1] // 2
    slots = lengths.shape[0]
    rows, features = tokens.shape
    length = rows // slots
    sources = (attn, merge, up)
    mine = (attn_mine, merge_mine, up_mine)
    pairs = (attn_pair, merge_pair, up_pair)
    gathered = (attn_all, merge_all, up_all)
    picks = Picks(at, routes, exits)
    route = Route(at, route_buffers, route_send, route_recv, 1, 8 - picks.shift)
    near, near_got, far = route.near, route.near_got, route.far
    here = [
        pltpu.make_async_copy(grad_act.at[k], ref, local.at[k])
        for k, ref in enumerate((route.a, route.b))
    ]
    for copy in here:
        copy.start()
    for k in range(3):
        width = sources[k].shape[1] // 2
        mine[k][:, :width] = take_half(sources[k], 1 - at.c)
        pairs[k][own, :width] = take_half(sources[k], at.c)
    attn_mine[:, lanes:] = jnp.zeros((shard, SMALL), f32)
    attn_mine[0:8, lanes : lanes + shard] = jnp.concatenate(
        [biases[...].astype(f32), gains[...].astype(f32)], axis=0
    )
    attn_mine[8:9, lanes : lanes + unit.shape[1]] = unit[...].astype(f32)
    attn_pair[own, lanes:] = attn_mine[:, lanes:]
    down_all[at.z, at.x, at.y, at.c] = down[...]
    at.greet(routes=True)
    swaps = []
    for k in range(3):
        swaps.append(
            remote(mine[k], pairs[k].at[own], swap_send.at[k], swap_recv.at[k], at.sibling())
        )
        swaps[-1].start()
    chunks = [
        Gather(at, *wide_block(gathered[k]), send.at[k], recv.at[k], mixed=k == 0)
        for k in range(3)
    ]
    chunks.append(Gather(at, *tall_block(down_all), send.at[3], recv.at[3], mixed=False))
    on_attn, on_merge, on_up, on_down = chunks

    actors = {"a": on_attn, "m": on_merge, "u": on_up, "d": on_down, "r": route}
    wide = {"a": 0, "m": 1, "u": 2}

    def run(events):
        for event in events:
            who, what, *rest = event.split(".")
            if what == "begin":
                k = wide[who]
                swaps[k].wait_recv()
                gathered[k][at.c, at.z, at.x, at.y] = pairs[k][...].astype(bf16)
                chunks[k].arrive(0)
            else:
                getattr(actors[who], what)(*(int(j) for j in rest))

    plan = FORWARD_PLAN
    run(plan["open"])
    for copy in here:
        copy.wait()
    near[...] = jnp.where(picks.near_lands_first, route.a[...], route.b[...])
    far[...] = jnp.where(picks.near_lands_first, route.b[...], route.a[...])
    run(plan["gather"])
    unpack_small(attn_all, vectors, units, shard)

    def columns(half, start, size):
        return attn_all[half, :, :, :, :, start : start + size].reshape(features, size)

    def up_part(half, start, width):
        return up_all[half, :, :, :, :, start : start + width].reshape(features, width)

    def merge_half(half):
        return merge_all[half].reshape(features, merge_all.shape[-1])

    for slot in range(slots):
        for half in range(2):
            project_half(tokens, columns, vectors, mixed, slot, length, half)
            run(plan["project"][2 * slot + half])
    saves = [
        pltpu.make_async_copy(src, dst, local.at[k + 2])
        for k, (src, dst) in enumerate(
            (
                (attn_all, attn_out),
                (mixed, mixed_out),
                (context, context_out),
                (merge_all, merge_out),
                (up_all, up_out),
                (down_all, down_out),
                (active, active_out),
                (slope, slope_out),
                (route.a, grad_leaving.at[0]),
                (route.b, grad_leaving.at[1]),
            )
        )
    ]
    saves[0].start()
    saves[1].start()

    def pair_step(i):
        slot, pair = lax.div(i, 6), lax.rem(i, 6)
        used = jnp.where(slot == 0, lengths[0], lengths[1])
        attend_pair(mixed, context, totals, slot, pair, length, used)

    in_turn(6 * slots, pair_step, run, plan["attend"])
    saves[2].start()
    run(plan["before_first"])
    saves[3].start()
    saves[4].start()
    size = rows // 4

    def first_step(r):
        first_rows(
            tokens, context, merge_half, up_part, vectors, units, first,
            (normed_one, inverse_one, low, active, slope), r, size,
        )

    in_turn(4, first_step, run, plan["first"])
    saves[6].start()
    saves[7].start()
    run(plan["before_second"])
    saves[5].start()

    def second_step(r):
        second_rows(
            active, down_all, vectors, first, (normed_two, inverse_two, leaving), r, size, features
        )

    in_turn(4, second_step, run, plan["second"])
    run(plan["close"])
    route.near_move().wait_recv()
    route.finish()
    for k, ref in enumerate((route.a, route.b)):
        pick = picks.near_first if k == 0 else jnp.logical_not(picks.near_first)
        moved = jnp.where(pick, near_got[...], far[...])
        ref[...] = jnp.where(picks.sent[k], moved, jnp.zeros_like(moved))
        saves[8 + k].start()
    for chunk in chunks:
        chunk.finish()
    for swap in swaps:
        swap.wait_send()
    for save in saves:
        save.wait()


def forward_layer(lengths, exits, routes, tokens, attn, merge, up, down, biases, gains, unit, grad_act):
    rows, features = tokens.shape
    shard = attn.shape[0]
    slots = lengths.shape[0]
    hidden = up.shape[1]
    widths = (attn.shape[1] // 2 + SMALL, merge.shape[1] // 2, hidden // 2)
    blocks = [(2, 4, 2, 2, 2 * shard, width) for width in widths] + [(4, 2, 2, 2) + down.shape]
    vmem = pl.BlockSpec(memory_space=pltpu.VMEM)
    anywhere = pl.BlockSpec(memory_space=pl.ANY)
    smem = pl.BlockSpec(memory_space=pltpu.SMEM)

    def shape(*dims, kind=bf16):
        return jax.ShapeDtypeStruct(dims, kind)

    return pl.pallas_call(
        forward_kernel,
        out_shape=[
            shape(rows, 3 * features),
            shape(rows, features),
            shape(slots, features // HD, rows // slots, kind=f32),
            *[shape(*block) for block in blocks],
            shape(8, features, kind=f32),
            shape(8, hidden, kind=f32),
            shape(rows, features),
            shape(rows, 1, kind=f32),
            shape(rows, features),
            shape(rows, hidden),
            shape(rows, hidden),
            shape(rows, features),
            shape(rows, 1, kind=f32),
            shape(rows, features),
            shape(*grad_act.shape),
        ],
        in_specs=[smem] * 3 + [vmem] * 8 + [anywhere],
        out_specs=[anywhere, anywhere, vmem] + [anywhere] * 4 + [vmem] * 5
        + [anywhere, anywhere, vmem, vmem, vmem, anywhere],
        scratch_shapes=[pltpu.VMEM(block, bf16) for block in blocks]
        + [
            pltpu.VMEM((rows, 3 * features), bf16),
            pltpu.VMEM((rows, features), bf16),
            pltpu.VMEM((rows, hidden), bf16),
            pltpu.VMEM((rows, hidden), bf16),
            pltpu.VMEM((rows, features), f32),
        ]
        + [pltpu.VMEM((shard, width), f32) for width in widths]
        + [pltpu.VMEM((2 * shard, width), f32) for width in widths]
        + [pltpu.VMEM(grad_act.shape[1:], bf16)] * Route.BUFFERS
        + [
            pltpu.SemaphoreType.DMA((4, Gather.SEMS)),
            pltpu.SemaphoreType.DMA((4, Gather.SEMS)),
            pltpu.SemaphoreType.DMA((3,)),
            pltpu.SemaphoreType.DMA((3,)),
            pltpu.SemaphoreType.DMA((12,)),
            pltpu.SemaphoreType.DMA((Route.SEMS,)),
            pltpu.SemaphoreType.DMA((Route.SEMS,)),
        ],
        compiler_params=pltpu.CompilerParams(
            collective_id=0, has_side_effects=True, vmem_limit_bytes=62 << 20
        ),
        cost_estimate=pl.CostEstimate(
            flops=2 * rows * features * 12 * features, bytes_accessed=100 << 20, transcendentals=0
        ),
    )(lengths, exits, routes, tokens, attn, merge, up, down, biases, gains, unit.reshape(1, -1), grad_act)


def exact(left, right, over_left=1, over_right=0):
    return lax.dot_general(
        left,
        right,
        (((over_left,), (over_right,)), ((), ())),
        precision=precise,
        preferred_element_type=f32,
    )


def rows_sum(values):
    return jnp.sum(values, axis=0, keepdims=True)


def pile(rows):
    width = rows[0].shape[1]
    count = sum(r.shape[0] for r in rows)
    return jnp.concatenate(rows + [jnp.zeros((8 - count, width), f32)], axis=0)


def student_slots(
    leaving, proj, pool, dense, label, student_bias, logit_bias, grad_logits, lengths,
    logits, low_grad, pack,
):
    slots = lengths.shape[0]
    length = leaving.shape[0] // slots
    half = proj.shape[1] // SH
    low = lax.broadcasted_iota(jnp.int32, (1, proj.shape[1]), 1) < half
    scale = 1.0 / math.sqrt(half)
    left, right = [[] for _ in range(5)], [[] for _ in range(5)]
    sums, outs = [], []

    def by_head(row):
        return jnp.concatenate([jnp.where(low, row, 0.0), jnp.where(low, 0.0, row)], axis=0)

    def one_row(two):
        return jnp.where(low, two[0:1], two[1:2])

    for slot in range(slots):
        here = pl.ds(slot * length, length)
        projected = jnp.dot(leaving[here, :], proj[...], preferred_element_type=f32)
        projected = projected + student_bias[0:1, :]
        valid = lax.broadcasted_iota(jnp.int32, (length, 1), 0) < lengths[slot]
        start = projected[0:1]
        query = exact(start, pool[0])
        queries = by_head(query)
        asks = exact(queries, pool[1], 1, 1)
        shares, means = [], []
        for h in range(SH):
            scores = jnp.sum(projected * asks[h : h + 1], axis=1, keepdims=True) * scale
            scores = jnp.where(valid, scores, neg_big)
            powers = jnp.exp(scores - jnp.max(scores, axis=0, keepdims=True))
            shares.append(powers / rows_sum(powers))
            means.append(rows_sum(shares[h] * projected))
        mean_rows = jnp.concatenate(means, axis=0)
        pooled = one_row(exact(mean_rows, pool[2]))
        active = jnp.tanh(exact(pooled, dense[...]) + student_bias[1:2, :])
        outs.append(exact(active, label[...], 1, 1) + logit_bias[...])
        g_logits = grad_logits[slot : slot + 1, :]
        g_pre = exact(g_logits, label[...]) * (1.0 - active * active)
        g_pooled = by_head(exact(g_pre, dense[...], 1, 1))
        g_means = exact(g_pooled, pool[2], 1, 1)
        g_projected = jnp.zeros_like(projected)
        g_asks = []
        for h in range(SH):
            g_share = jnp.sum(projected * g_means[h : h + 1], axis=1, keepdims=True)
            g_score = shares[h] * (g_share - rows_sum(g_share * shares[h])) * scale
            g_projected = g_projected + shares[h] * g_means[h : h + 1] + g_score * asks[h : h + 1]
            g_asks.append(rows_sum(g_score * projected))
        g_ask_rows = jnp.concatenate(g_asks, axis=0)
        g_query = one_row(exact(g_ask_rows, pool[1]))
        first = lax.broadcasted_iota(jnp.int32, (length, 1), 0) == 0
        g_projected = g_projected + jnp.where(first, exact(g_query, pool[0], 1, 1), 0.0)
        low_grad[here, :] = g_projected.astype(bf16)
        sums.append((rows_sum(g_projected), g_pre, g_logits))
        for k, (a, b) in enumerate(
            (
                (start, g_query),
                (g_ask_rows, queries),
                (mean_rows, g_pooled),
                (pooled, g_pre),
                (g_logits, active),
            )
        ):
            left[k].append(a)
            right[k].append(b)
    features, lanes = proj.shape
    pack[0:features, :] = dots(leaving[...], low_grad[...], 0, 0)
    for k in range(5):
        grad = exact(pile(left[k]), pile(right[k]), 0, 0)
        row = features + k * lanes
        size = lanes if k < 4 else 16
        pack[row : row + size, :] = grad[:size]
    row = features + 4 * lanes + 16
    pack[row : row + 8, :] = pile([sum(s[k] for s in sums) for k in range(3)])
    logits[...] = pile(outs)


def norm_back(grad, normed, inverse, gain):
    scaled = grad * gain
    return inverse * (
        scaled
        - jnp.mean(scaled, axis=-1, keepdims=True)
        - normed * jnp.mean(scaled * normed, axis=-1, keepdims=True)
    )


ROWS_PLAN = {
    1: (("turn", 0), ("turn", 1)),
    2: (("turn", 2), ("turn", 3)),
}


def rows_kernel(
    lengths, exits, routes, leaving, proj, pool, dense, label_in, student_bias, logit_bias_in,
    grad_logits_in, merge, up, down, vectors, grad_leaving, normed_one, inverse_one, normed_two, inverse_two,
    slope,
    logits, pack, near, a, b, mine, landed, mid_low, inner_low, res, res_low, grad_context,
    proj_low, sums, unit_sum, label, logit_bias, grad_logits, *scratch,
):
    step = pl.program_id(0)
    size = grad_leaving.shape[0]
    at = Place()
    buffers, (send, recv) = scratch[:-2], scratch[-2:]
    picks = Picks(at, routes, exits)
    route = RouteStart(at, (None, None, *buffers, *[None] * 4), send, recv, 7, picks.shift)
    length = leaving.shape[0] // lengths.shape[0]

    @pl.when(step == 0)
    def _():
        at.greet()
        for k in range(route.PARTS):
            part = pl.ds(k * route.size, route.size)
            two = []
            for slot in range(2):
                rows = pl.ds(slot * length + k * route.size, route.size)
                kept = leaving[rows, :]
                two.append(jnp.where(picks.sent[slot], kept, jnp.zeros_like(kept)))
            near[part, :] = jnp.where(picks.near_first, two[0], two[1])
            route.far[part, :] = jnp.where(picks.near_first, two[1], two[0])
            route.x_move(k).start()

    for when, events in ROWS_PLAN.items():

        @pl.when(step == when)
        def _():
            for event, k in events:
                getattr(route, event)(k)

    @pl.when(step == 0)
    def _():
        classes = label_in.shape[0]
        label[...] = jnp.zeros_like(label)
        label[:classes, :] = label_in[...]
        for wide, narrow in ((logit_bias, logit_bias_in), (grad_logits, grad_logits_in)):
            wide[...] = jnp.zeros_like(wide)
            wide[:, :classes] = narrow[...]
        student_slots(
            leaving, proj, pool, dense, label, student_bias, logit_bias, grad_logits, lengths,
            logits, proj_low, pack,
        )
        sums[...] = jnp.zeros_like(sums)
        unit_sum[...] = jnp.zeros_like(unit_sum)

    grad_second = grad_leaving[...].astype(f32) + dots(proj_low[rows_of(step, size), :], proj[...], 1, 1)
    two = normed_two[...].astype(f32)
    grad_mid = norm_back(grad_second, two, inverse_two[...], vectors[7:8, :])
    mid = grad_mid.astype(bf16)
    mid_low[...] = mid
    width = up.shape[2]
    grad_first = grad_mid
    for half in range(2):
        for part in range(2):
            cols = pl.ds(half * width + part * (width // 2), width // 2)
            inside = pl.ds(part * (width // 2), width // 2)
            inner = dots(mid, down[cols, :], 1, 1) * slope[:, cols].astype(f32)
            unit_sum[0:1, cols] += rows_sum(inner)
            inner = inner.astype(bf16)
            inner_low[:, cols] = inner
            grad_first = grad_first + dots(inner, up[half, :, inside], 1, 1)
    one = normed_one[...].astype(f32)
    grad_res = norm_back(grad_first, one, inverse_one[...], vectors[6:7, :])
    res[...] = grad_res
    low = grad_res.astype(bf16)
    res_low[...] = low
    narrow = merge.shape[2]
    grad_context[...] = (
        dots(low[:, :narrow], merge[0], 1, 1) + dots(low[:, narrow:], merge[1], 1, 1)
    ).astype(bf16)
    sums[...] += jnp.concatenate(
        [
            jnp.zeros((2, grad_res.shape[1]), f32),
            rows_sum(grad_res),
            rows_sum(grad_first),
            rows_sum(grad_mid),
            rows_sum(grad_second),
            rows_sum(grad_first * one),
            rows_sum(grad_second * two),
        ],
        axis=0,
    )

    @pl.when(step == pl.num_programs(0) - 1)
    def _():
        for k in range(route.PARTS):
            route.settle(k, a, b, mine, landed)
        route.finish()
        row = pack.shape[0] - 72
        for t in range(6):
            pack[row + 8 * t : row + 8 * t + 8, :] = sums[:, 128 * t : 128 * t + 128]
        pack[row + 48 : row + 72, :] = unit_sum[0:1, :].reshape(24, 128)


def rows_backward(lengths, exits, routes, leaving, student, grad_logits, weights, vectors, grad_leaving, saved):
    proj, pool, dense, label, student_bias, logit_bias = student
    merge, up, down = weights
    normed_one, inverse_one, normed_two, inverse_two, slope = saved
    rows, features = leaving.shape
    hidden = down.shape[0]
    size = rows // 4
    lanes = proj.shape[1]
    def fixed(array):
        return pl.BlockSpec(array.shape, lambda i, n=array.ndim: (0,) * n, pipeline_mode=pl.Buffered(1))

    def by_rows(array):
        return pl.BlockSpec((size, array.shape[1]), lambda i: (i, 0))

    def shape(*dims, kind=f32):
        return jax.ShapeDtypeStruct(dims, kind)

    whole_in = (
        leaving, proj, pool, dense, label.T, student_bias, logit_bias.reshape(1, -1), grad_logits,
        merge, up, down, vectors,
    )
    row_in = (grad_leaving, normed_one, inverse_one, normed_two, inverse_two, slope)
    whole_out = (
        shape(8, lanes), shape(features + 4 * lanes + 24 + 72, lanes),
        *[shape(rows // 2, features, kind=bf16)] * 5,
    )
    row_out = (
        shape(rows, features, kind=bf16), shape(rows, hidden, kind=bf16), shape(rows, features),
        shape(rows, features, kind=bf16), shape(rows, features, kind=bf16),
    )
    return pl.pallas_call(
        rows_kernel,
        grid=(4,),
        out_shape=whole_out + row_out,
        in_specs=[pl.BlockSpec(memory_space=pltpu.SMEM)] * 3
        + [fixed(a) for a in whole_in]
        + [by_rows(a) for a in row_in],
        out_specs=[fixed(a) for a in whole_out] + [by_rows(a) for a in row_out],
        scratch_shapes=[
            pltpu.VMEM((rows, lanes), bf16),
            pltpu.VMEM((8, features), f32),
            pltpu.VMEM((8, hidden), f32),
            pltpu.VMEM((lanes, lanes), f32),
            pltpu.VMEM((1, lanes), f32),
            pltpu.VMEM((2, lanes), f32),
            *[pltpu.VMEM((rows // 2, features), bf16)] * 4,
            pltpu.SemaphoreType.DMA((Route.SEMS,)),
            pltpu.SemaphoreType.DMA((Route.SEMS,)),
        ],
        compiler_params=pltpu.CompilerParams(
            dimension_semantics=("arbitrary",), collective_id=1, has_side_effects=True,
            vmem_limit_bytes=60 << 20,
        ),
        cost_estimate=pl.CostEstimate(
            flops=2 * rows * features * (2 * hidden + features),
            bytes_accessed=40 << 20,
            transcendentals=0,
        ),
    )(lengths, exits, routes, *whole_in, *row_in)


def attend_back_pair(mixed, grad_context, totals, sums, slot, pair, length, used, features):
    here = rows_of(slot, length)
    base = pl.multiple_of(pair * 128, 128)
    spots = [pl.ds(pl.multiple_of(base + k * features, 128), 128) for k in range(3)]
    two_q, two_k, two_v = (mixed[here, spot] for spot in spots)
    two_g = grad_context[here, pl.ds(base, 128)]
    low = lax.broadcasted_iota(jnp.int32, two_k.shape, 1) < HD
    valid = lax.broadcasted_iota(jnp.int32, (length, 1), 0) < used
    none = jnp.zeros_like(two_k)
    scale = jnp.asarray(HD ** (-0.5), bf16)
    two_q = two_q * scale
    small_k = two_k * scale
    outs = [[], [], []]
    for head in range(2):
        side = low if head == 0 else ~low
        scores = dots(jnp.where(side, two_k, none), two_q, 1, 1)
        probs = jnp.where(valid, jnp.exp(scores - totals[slot, pl.ds(2 * pair + head, 1), :]), 0.0)
        grad_probs = dots(jnp.where(side, two_v, none), two_g, 1, 1)
        shared = jnp.sum(grad_probs * probs, axis=0, keepdims=True)
        grad_scores = (probs * (grad_probs - shared)).astype(bf16)
        outs[0].append(dots(grad_scores, small_k, 0, 0))
        outs[1].append(jnp.dot(grad_scores, two_q, preferred_element_type=f32))
        outs[2].append(jnp.dot(probs.astype(bf16), two_g, preferred_element_type=f32))
    for k in range(3):
        grad = jnp.where(low, outs[k][0], outs[k][1])
        mixed[here, spots[k]] = grad.astype(bf16)
        if k != 1:
            sums[k // 2 : k // 2 + 1, pl.ds(base, 128)] += rows_sum(grad)


CLOSE_PLAN = {
    "up": {
        0: ("r.step", "s.step.0",),
        2: ("d.join.3",),
        7: ("d.join.2",),
    },
    "merge": (),
    "attend": {
        1: ("s.step.1", "d.halve.3", "u.join.3", "r.hand.0", "u.join.2",),
        2: ("m.join.3",),
        3: ("m.join.2",),
        4: ("d.join.1",),
        5: ("d.join.0",),
        6: ("d.halve.2", "u.join.1",),
        8: ("r.hand.2", "d.leave.3", "s.step.2", "d.halve.1", "u.halve.3", "u.halve.2", "r.join",),
        9: ("r.hand.1",),
        10: ("u.join.0",),
        11: ("d.leave.2",),
    },
    "attn": {
        0: ("m.halve.3", "u.leave.3",),
        1: ("m.halve.2",),
        3: (
            "b.step.0", "a.give.1", "m.join.1", "r.take.1", "a.give.3", "a.give.0", "u.halve.1",
            "a.give.2",
        ),
        4: ("m.join.0", "u.leave.2", "u.halve.0",),
        5: ("r.take.0",),
    },
    "before_inputs": (
        "a.join.3", "s.step.3", "r.take.2", "b.step.1", "a.join.2", "m.halve.1", "a.halve.3",
        "m.leave.3", "u.leave.1", "b.step.2", "a.join.1", "m.halve.0",
    ),
    "inputs": {
        0: ("a.halve.2", "r.hand.3", "a.join.0", "d.leave.1",),
        1: (
            "a.leave.3", "b.step.3", "a.halve.1", "u.leave.0", "m.leave.2", "d.halve.0",
            "a.leave.2", "m.leave.1",
        ),
        2: ("a.leave.1", "a.halve.0", "r.take.3",),
        3: ("s.step.4", "b.step.4", "m.leave.0", "d.leave.0",),
    },
    "close": ("a.leave.0",),
}


def close_kernel(
    lengths, exits, routes, totals, pack, mixed_in, grad_context_in, tokens_in, attn_in, res_in,
    active_in, inner_in, mid_in, low_in, context_in, res_low_in, near, a, b, mine_in, landed_in,
    grad_inputs, attn_out, merge_out, up_out, down_out, small_out, late_out, arrived,
    *scratch,
):
    at = Place()
    (
        mixed, attn, tiles, mid, low, context, res_low, bias_sums,
        small_low, small_got, small_sum, late_low, late_got, near_got, a_got, b_got, mine, landed,
        attn_total, merge_total, up_total,
        local, tile_sems, small_send, small_recv, swap_send, swap_recv, route_send, route_recv,
        send, recv,
    ) = scratch[-31:]
    chunks = []
    for k in range(4):
        grad, from_core, from_second, from_first, from_line = scratch[5 * k : 5 * k + 5]
        block, line = (tall_block if k == 3 else wide_block)(grad)
        chunks.append(
            Scatter(
                at, block, line, from_core, from_second, from_first, from_line,
                send.at[k], recv.at[k], mixed=k != 3,
            )
        )
    grads = [scratch[5 * k] for k in range(4)]
    on_attn, on_merge, on_up, on_down = chunks
    features = mid.shape[1]
    slots = lengths.shape[0]
    length = mixed.shape[0] // slots
    tile_lanes = tiles.shape[2]
    steps = inner_in.shape[1] // tile_lanes

    def load(k, src, dst):
        copy = pltpu.make_async_copy(src, dst, local.at[k])
        copy.start()
        return copy

    def tile(src, t):
        return pltpu.make_async_copy(
            src.at[:, lanes_of(t, tile_lanes)], tiles.at[lax.rem(t, 2)], tile_sems.at[lax.rem(t, 2)]
        )

    mid_load = load(0, mid_in, mid)
    tile(active_in, 0).start()
    low_load = load(1, low_in, low)
    context_load = load(2, context_in, context)
    res_low_load = load(3, res_low_in, res_low)
    mixed_load = load(4, mixed_in, mixed)
    res_load = load(5, res_in, grad_inputs)
    attn_load = load(6, attn_in, attn)
    landed_load = load(9, landed_in, landed)
    mine_load = load(12, mine_in, mine)
    at.greet(far=True, routes=True)
    picks = Picks(at, routes, exits)
    route = RouteEnd(
        at, near, near_got, a, b, mine, a_got, b_got, route_send, route_recv, picks.shift
    )
    small = Butterfly(
        at, small_sum, small_low, small_got, small_send.at[0], small_recv.at[0], True
    )
    late = Butterfly(at, late_out, late_low, late_got, small_send.at[1], small_recv.at[1], False)
    actors = {
        "a": on_attn, "m": on_merge, "u": on_up, "d": on_down, "r": route, "s": small, "b": late
    }
    plan = CLOSE_PLAN

    def run(events):
        for event in events:
            who, what, *rest = event.split(".")
            getattr(actors[who], what)(*(int(j) for j in rest))

    small_rows = small_low.shape[1]
    for half in range(2):
        part = pack[half * small_rows : (half + 1) * small_rows, :].astype(bf16)
        here = at.c == half

        @pl.when(here)
        def _():
            small_sum[...] = part.astype(f32)

        @pl.when(jnp.logical_not(here))
        def _():
            small_low[0] = part

    mine_load.wait()
    for part in range(Route.PARTS):
        route.cross(part)
    small.begin()

    mid_load.wait()

    def down_tile(t, carry):
        tile(active_in, t).wait()

        @pl.when(t + 1 < steps)
        def _():
            tile(active_in, t + 1).start()

        part = dots(tiles[lax.rem(t, 2)], mid[...], 0, 0).astype(bf16)
        grads[3][lax.div(t, 2), lax.rem(t, 2)] = part.reshape(2, 2, part.shape[0] // 4, features)

        @pl.when(lax.rem(t, 2) == 1)
        def _():
            on_down.across(lax.div(t, 2)).start()

        return carry

    lax.fori_loop(0, steps, down_tile, 0)
    tokens_load = load(7, tokens_in, mid)
    low_load.wait()
    half_steps = steps // 2

    def up_source(t):
        half = (1 - at.c) * (1 - lax.div(t, half_steps)) + at.c * lax.div(t, half_steps)
        return half, half * half_steps + lax.rem(t, half_steps)

    def up_fetch(t):
        return pltpu.make_async_copy(
            inner_in.at[:, lanes_of(up_source(t)[1], tile_lanes)],
            tiles.at[lax.rem(t, 2)],
            tile_sems.at[lax.rem(t, 2)],
        )

    up_fetch(0).start()

    def up_tile(t):
        up_fetch(t).wait()

        @pl.when(t + 1 < steps)
        def _():
            up_fetch(t + 1).start()

        part = dots(low[...], tiles[lax.rem(t, 2)], 0, 0).astype(bf16)
        half = up_source(t)[0]
        grads[2][half, :, :, :, :, lanes_of(lax.rem(t, half_steps), tile_lanes)] = part.reshape(
            4, 2, 2, -1, tile_lanes
        )

        @pl.when(t == half_steps - 1)
        def _():
            for j in (3, 2, 1, 0):
                on_up.give(j)

    in_turn(steps, up_tile, run, plan["up"])
    context_load.wait()
    res_low_load.wait()
    narrow = res_low.shape[1] // 2
    for half in range(2):
        part = dots(context[...], res_low[:, half * narrow : (half + 1) * narrow], 0, 0)
        grads[1][half] = part.astype(bf16).reshape(4, 2, 2, -1, narrow)
    for j in (3, 2, 1, 0):
        on_merge.give(j)
    context_again = load(8, grad_context_in, low)
    bias_sums[...] = jnp.zeros_like(bias_sums)
    mixed_load.wait()
    context_again.wait()
    run(plan["merge"])

    def pair_step(i):
        slot, pair = lax.div(i, 6), lax.rem(i, 6)
        used = jnp.where(slot == 0, lengths[0], lengths[1])
        attend_back_pair(mixed, low, totals, bias_sums, slot, pair, length, used, features)

    in_turn(6 * slots, pair_step, run, plan["attend"])
    tokens_load.wait()
    wide = mixed.shape[1] // 2
    third = wide // 3

    late_low[0] = jnp.concatenate(
        [bias_sums[0:2, 128 * t : 128 * t + 128] for t in range(6)] + [jnp.zeros((4, 128), f32)],
        axis=0,
    )
    late_out[...] = late_low[0]
    late.begin()

    def attn_part(p):
        half = (1 - at.c) * (1 - lax.div(p, 3)) + at.c * lax.div(p, 3)
        cols = lanes_of(half * 3 + lax.rem(p, 3), third)
        part = dots(mid[...], mixed[:, cols], 0, 0).astype(bf16)
        grads[0][half, :, :, :, :, lanes_of(lax.rem(p, 3), third)] = part.reshape(
            4, 2, 2, -1, third
        )

    in_turn(6, attn_part, run, plan["attn"])
    run(plan["before_inputs"])
    attn_load.wait()
    res_load.wait()

    def inputs_part(r):
        here = rows_of(r, length // 2)
        total = grad_inputs[here, :]
        for half in range(2):
            weight = attn[half, :, :, :, :, :wide].reshape(features, wide)
            total = total + dots(mixed[here, half * wide : (half + 1) * wide], weight, 1, 1)
        grad_inputs[here, :] = total

    in_turn(2 * slots, inputs_part, run, plan["inputs"])
    landed_load.wait()
    arrived_saves = []
    for k in range(2):
        rows = pl.ds(k * length // 2, length // 2)

        other = jnp.where(route.stays(), landed[rows, :], a_got[rows, :])
        one = near_got[rows, :]
        near_got[rows, :] = jnp.where(picks.near_lands_first, one, other)
        landed[rows, :] = jnp.where(picks.near_lands_first, other, one)
    for k, ref in enumerate((near_got, landed)):
        arrived_saves.append(pltpu.make_async_copy(ref, arrived.at[k], local.at[10 + k]))
        arrived_saves[k].start()
    finish_scatter(at, on_down, None, down_out, None, None, True)
    finish_scatter(at, on_up, up_total, up_out, swap_send.at[2], swap_recv.at[2], False)
    finish_scatter(at, on_merge, merge_total, merge_out, swap_send.at[1], swap_recv.at[1], False)
    own = pl.ds(pl.multiple_of(at.c * small_rows, 8), small_rows)
    small_out[own, :] = small_sum[...]
    last = remote(small_sum, small_out.at[own], swap_send.at[3], swap_recv.at[3], at.sibling())
    last.start()
    run(plan["close"])
    finish_scatter(at, on_attn, attn_total, attn_out, swap_send.at[0], swap_recv.at[0], False)
    last.wait()
    small.finish()
    late.finish()
    route.finish()
    for save in arrived_saves:
        save.wait()
    for chunk in chunks:
        chunk.finish()


def close_backward(
    lengths, exits, routes, totals, pack, mixed, grad_context, tokens, attn, res, active, inner,
    mid, low, context, res_low, near, a, b, mine, landed, shards,
):
    rows, features = tokens.shape
    hidden = active.shape[1]
    vmem = pl.BlockSpec(memory_space=pltpu.VMEM)
    anywhere = pl.BlockSpec(memory_space=pl.ANY)
    scratch = []
    for k, (shard_rows, columns) in enumerate(shards):
        if k < 3:
            tall, width = 2 * shard_rows, columns // 2
            scratch.append(pltpu.VMEM((2, 4, 2, 2, tall, width), bf16))
        else:
            tall, width = shard_rows, columns
            scratch.append(pltpu.VMEM((4, 2, 2, 2, tall, width), bf16))
        scratch += [
            pltpu.VMEM((4, 2, 2, tall, width), bf16),
            pltpu.VMEM((4, 2, tall, width), bf16),
            pltpu.VMEM((4, tall, width), bf16),
            pltpu.VMEM((4, 2, tall, width), bf16),
        ]
    small_rows = pack.shape[0] // 2
    wide = [(2 * r, c // 2) for r, c in shards[:3]]
    scratch += [
        pltpu.VMEM(mixed.shape, bf16),
        pltpu.VMEM(attn.shape, bf16),
        pltpu.VMEM((2, rows, hidden // 8), bf16),
        pltpu.VMEM((rows, features), bf16),
        pltpu.VMEM((rows, features), bf16),
        pltpu.VMEM((rows, features), bf16),
        pltpu.VMEM((rows, features), bf16),
        pltpu.VMEM((8, features), f32),
        pltpu.VMEM((5, small_rows, 128), bf16),
        pltpu.VMEM((5, small_rows, 128), bf16),
        pltpu.VMEM((small_rows, 128), f32),
        pltpu.VMEM((5, 16, 128), f32),
        pltpu.VMEM((5, 16, 128), f32),
        *[pltpu.VMEM(near.shape, bf16)] * 5,
        *[pltpu.VMEM(w, f32) for w in wide],
        pltpu.SemaphoreType.DMA((13,)),
        pltpu.SemaphoreType.DMA((2,)),
        pltpu.SemaphoreType.DMA((2, 5)),
        pltpu.SemaphoreType.DMA((2, 5)),
        pltpu.SemaphoreType.DMA((4,)),
        pltpu.SemaphoreType.DMA((4,)),
        pltpu.SemaphoreType.DMA((Route.SEMS,)),
        pltpu.SemaphoreType.DMA((Route.SEMS,)),
        pltpu.SemaphoreType.DMA((4, Scatter.SEMS)),
        pltpu.SemaphoreType.DMA((4, Scatter.SEMS)),
    ]
    return pl.pallas_call(
        close_kernel,
        out_shape=[jax.ShapeDtypeStruct((rows, features), f32)]
        + [jax.ShapeDtypeStruct(shape, f32) for shape in shards]
        + [
            jax.ShapeDtypeStruct(pack.shape, f32),
            jax.ShapeDtypeStruct((16, 128), f32),
            jax.ShapeDtypeStruct((2,) + near.shape, bf16),
        ],
        in_specs=[pl.BlockSpec(memory_space=pltpu.SMEM)] * 3 + [vmem, vmem] + [anywhere] * 16,
        out_specs=[vmem] * 7 + [anywhere],
        scratch_shapes=scratch,
        compiler_params=pltpu.CompilerParams(
            collective_id=2, has_side_effects=True, vmem_limit_bytes=62 << 20
        ),
        cost_estimate=pl.CostEstimate(
            flops=2 * rows * features * 12 * features, bytes_accessed=60 << 20, transcendentals=0
        ),
    )(
        lengths, exits, routes, totals, pack, mixed, grad_context, tokens, attn, res, active, inner,
        mid, low, context, res_low, near, a, b, mine, landed,
    )


def hand_kernel(
    small, late, logits_in, attn_in, merge_in, up_in, down_in, grad_inputs_in, arrived_in,
    arrived, logits, grad_inputs, attn, merge, up, down, bias_grad, gain_grad, unit_grad,
    proj_grad, pool_grad, dense_grad, label_grad, student_grad, logit_grad,
    grad_held, arrived_held, sems,
):
    moves = []
    for k, (src, held, dst) in enumerate(
        ((grad_inputs_in, grad_held, grad_inputs), (arrived_in, arrived_held, arrived))
    ):
        for part in range(4):
            rows = pl.ds(part * (held.shape[0] // 4), held.shape[0] // 4)
            sem = sems.at[4 * k + part]
            moves.append(
                (
                    pltpu.make_async_copy(src.at[rows, :], held.at[rows, :], sem),
                    pltpu.make_async_copy(held.at[rows, :], dst.at[rows, :], sem),
                )
            )
    for fetch, _ in moves:
        fetch.start()
    for src, dst in ((attn_in, attn), (merge_in, merge), (up_in, up), (down_in, down)):
        dst[...] = src[...]
    for fetch, save in moves:
        fetch.wait()
        save.start()
    mine = 4 * lax.axis_index("batch") + lax.axis_index("zero")
    features, lanes = proj_grad.shape
    classes = label_grad.shape[0]
    shard, wide = bias_grad.shape[1], unit_grad.shape[1]
    logits[...] = logits_in[: logits.shape[0], :classes]
    proj_grad[...] = small[:features, :]
    for k in range(3):
        pool_grad[k] = small[features + k * lanes : features + (k + 1) * lanes, :]
    row = features + 3 * lanes
    dense_grad[...] = small[row : row + lanes, :]
    row += lanes
    label_grad[...] = small[row : row + classes, :]
    student_grad[...] = small[row + 16 : row + 18, :]
    logit_grad[...] = small[row + 18 : row + 19, :classes]
    row += 24
    tiles = features // 128
    vectors = jnp.concatenate(
        [
            jnp.concatenate(
                [late[2 * t : 2 * t + 2, :], small[row + 8 * t + 2 : row + 8 * t + 8, :]], axis=0
            )
            for t in range(tiles)
        ],
        axis=1,
    )

    def window(size, start, width):
        place = lax.broadcasted_iota(jnp.int32, (size, 128), 0)
        lane = lax.broadcasted_iota(jnp.int32, (size, 128), 1)
        inside = jnp.logical_and(place == start + lane, lane < width)
        return jnp.where(inside, 1.0, 0.0)

    part = exact(vectors, window(features, mine * shard, shard))
    bias_grad[...] = part[:6, :shard]
    gain_grad[...] = part[6:8, :shard]
    row += 8 * tiles
    units = jnp.concatenate([small[row + t : row + t + 1, :] for t in range(24)], axis=1)
    units = jnp.concatenate([units, jnp.zeros((7, units.shape[1]), f32)], axis=0)
    part = exact(units, window(units.shape[1], mine * wide, wide))
    unit_grad[...] = part[0:1, :wide]
    for _, save in moves:
        save.wait()


def hand_over(small, late, logits, shards, grad_inputs, arrived, slots, classes, shard):
    vmem = pl.BlockSpec(memory_space=pltpu.VMEM)
    anywhere = pl.BlockSpec(memory_space=pl.ANY)
    lanes = small.shape[1]
    features = grad_inputs.shape[1]

    def shape(*dims, kind=f32):
        return jax.ShapeDtypeStruct(dims, kind)

    return pl.pallas_call(
        hand_kernel,
        out_shape=[
            shape(*arrived.shape, kind=bf16),
            shape(slots, classes),
            shape(*grad_inputs.shape),
            *[shape(*s.shape) for s in shards],
            shape(6, shard),
            shape(2, shard),
            shape(1, 4 * shard),
            shape(features, lanes),
            shape(3, lanes, lanes),
            shape(lanes, lanes),
            shape(classes, lanes),
            shape(2, lanes),
            shape(1, classes),
        ],
        in_specs=[vmem] * 7 + [anywhere, anywhere],
        out_specs=[anywhere, vmem, anywhere] + [vmem] * 13,
        scratch_shapes=[
            pltpu.VMEM(grad_inputs.shape, f32),
            pltpu.VMEM(arrived.shape, bf16),
            pltpu.SemaphoreType.DMA((8,)),
        ],
        compiler_params=pltpu.CompilerParams(vmem_limit_bytes=62 << 20),
    )(small, late, logits, *shards, grad_inputs, arrived)


def passed_along(block, axis, distance):
    devices = range(lax.axis_size(axis))
    route = [((i - distance) % len(devices), i) for i in devices]
    return lax.ppermute(block, axis, route)


def product(pattern, left, right):
    return jnp.einsum(pattern, left, right, preferred_element_type=jnp.float32)


def gelu_erf(values):
    return 0.5 * values * (1.0 + jax.scipy.special.erf(values * 0.7071067811865476))


def gelu_slope(values):
    return (
        0.5 * (1.0 + jax.scipy.special.erf(values * 0.7071067811865476))
        + values * jnp.exp(-0.5 * values * values) * 0.3989422804014327
    )


def norm_forward(hidden, norm_gain, norm_shift):
    centred = hidden - jnp.mean(hidden, axis=-1, keepdims=True)
    inverse = lax.rsqrt(jnp.mean(centred * centred, axis=-1, keepdims=True) + eps_norm)
    normed = centred * inverse
    return (normed * norm_gain + norm_shift, normed, inverse)


def norm_backward(grad_out, normed, inverse, norm_gain):
    scaled = grad_out * norm_gain
    return inverse * (
        scaled
        - jnp.mean(scaled, axis=-1, keepdims=True)
        - normed * jnp.mean(scaled * normed, axis=-1, keepdims=True)
    )


def student_head(
    hidden, valid_keys, pool_weight, dense_weight, label_weight, dense_bias, logit_bias
):
    groups, length, features = hidden.shape
    head_size = features // SH
    queries = jnp.einsum("bd,de->be", hidden[:, 0], pool_weight[0], precision=precise).reshape(
        groups, SH, head_size
    )
    key_rows = jnp.einsum("bld,de->ble", hidden, pool_weight[1], precision=precise).reshape(
        groups, length, SH, head_size
    )
    value_rows = jnp.einsum("bld,de->ble", hidden, pool_weight[2], precision=precise).reshape(
        groups, length, SH, head_size
    )
    scores = jnp.einsum("bhe,blhe->bhl", queries, key_rows, precision=precise) / math.sqrt(
        head_size
    )
    scores = jnp.where(valid_keys[:, None, :], scores, neg_big)
    shares = jax.nn.softmax(scores, axis=-1)
    pooled = jnp.einsum("bhl,blhe->bhe", shares, value_rows, precision=precise).reshape(
        groups, features
    )
    dense_out = jnp.tanh(jnp.dot(pooled, dense_weight, precision=precise) + dense_bias)
    return jnp.dot(dense_out, label_weight, precision=precise) + logit_bias


def layer_forward(tokens, valid_keys, weights, student):
    attn_weight, merge_weight, up_weight, down_weight, biases, norm_gains, unit_bias = weights
    proj_weight, pool_weight, dense_weight, label_weight, student_biases, logit_bias = student
    groups, length, features = tokens.shape
    mixed_proj = product("bld,de->ble", tokens, attn_weight)
    queries = (
        (mixed_proj[..., :features] + biases[0])
        .astype(jnp.bfloat16)
        .reshape(groups, length, -1, HD)
    )
    key_rows = (
        mixed_proj[..., features : 2 * features]
        .astype(jnp.bfloat16)
        .reshape(groups, length, -1, HD)
    )
    value_rows = (
        (mixed_proj[..., 2 * features :] + biases[1])
        .astype(jnp.bfloat16)
        .reshape(groups, length, -1, HD)
    )
    scores = product("bqhe,bkhe->bhqk", queries, key_rows) * HD ** (-0.5)
    scores = jnp.where(valid_keys[:, None, None, :], scores, neg_big)
    row_top = jnp.max(scores, axis=-1, keepdims=True)
    exponent = jnp.exp(scores - row_top)
    row_total = jnp.sum(exponent, axis=-1, keepdims=True)
    attn_probs = (exponent / row_total).astype(jnp.bfloat16)
    log_total = row_top + jnp.log(row_total)
    context = (
        product("bhqk,bkhe->bqhe", attn_probs, value_rows)
        .astype(jnp.bfloat16)
        .reshape(groups, length, features)
    )
    attended = product("bld,de->ble", context, merge_weight) + biases[2]
    first_norm, normed_one, inverse_one = norm_forward(
        tokens.astype(jnp.float32) + attended, norm_gains[0], biases[3]
    )
    first_low = first_norm.astype(jnp.bfloat16)
    inner_pre = product("bld,df->blf", first_low, up_weight) + unit_bias
    active = gelu_erf(inner_pre).astype(jnp.bfloat16)
    branch_out = product("blf,fd->bld", active, down_weight) + biases[4]
    second, normed_two, inverse_two = norm_forward(
        first_norm + branch_out, norm_gains[1], biases[5]
    )
    leaving = second.astype(jnp.bfloat16)
    projected = product("bld,de->ble", leaving, proj_weight) + student_biases[0]

    def classify(hidden, attn_part, dense_part, label_part, dense_bias, class_bias):
        return student_head(
            hidden, valid_keys, attn_part, dense_part, label_part, dense_bias, class_bias
        )

    logits, pull_back = jax.vjp(
        classify, projected, pool_weight, dense_weight, label_weight, student_biases[1], logit_bias
    )
    saved_state = (
        tokens,
        valid_keys,
        queries,
        key_rows,
        value_rows,
        log_total,
        context,
        normed_one,
        inverse_one,
        first_low,
        inner_pre,
        active,
        normed_two,
        inverse_two,
        leaving,
        pull_back,
    )
    return (leaving, logits, saved_state)


def layer_backward(saved_state, grad_leaving, grad_logits, weights, proj_weight):
    (
        tokens,
        valid_keys,
        queries,
        key_rows,
        value_rows,
        log_total,
        context,
        normed_one,
        inverse_one,
        first_low,
        inner_pre,
        active,
        normed_two,
        inverse_two,
        leaving,
        pull_back,
    ) = saved_state
    attn_weight, merge_weight, up_weight, down_weight, biases, norm_gains, unit_bias = weights
    groups, length, features = tokens.shape
    grad_proj, grad_pool, grad_dense, grad_label, grad_dense_bias, grad_logit_bias = pull_back(
        grad_logits
    )
    proj_low = grad_proj.astype(jnp.bfloat16)
    grad_proj_weight = product("bld,ble->de", leaving, proj_low)
    grad_second = grad_leaving + product("ble,de->bld", proj_low, proj_weight)
    grad_mid = norm_backward(grad_second, normed_two, inverse_two, norm_gains[1])
    down_low = grad_mid.astype(jnp.bfloat16)
    grad_down = product("blf,bld->fd", active, down_low)
    grad_inner = product("bld,fd->blf", down_low, down_weight) * gelu_slope(inner_pre)
    inner_low = grad_inner.astype(jnp.bfloat16)
    grad_up = product("bld,blf->df", first_low, inner_low)
    grad_first = grad_mid + product("blf,df->bld", inner_low, up_weight)
    grad_res = norm_backward(grad_first, normed_one, inverse_one, norm_gains[0])
    res_low = grad_res.astype(jnp.bfloat16)
    grad_merge = product("blc,bld->cd", context, res_low)
    grad_context = (
        product("bld,cd->blc", res_low, merge_weight)
        .astype(jnp.bfloat16)
        .reshape(groups, length, -1, HD)
    )
    scores = product("bqhe,bkhe->bhqk", queries, key_rows) * HD ** (-0.5)
    scores = jnp.where(valid_keys[:, None, None, :], scores, neg_big)
    attn_probs = jnp.exp(scores - log_total)
    grad_values = product("bhqk,bqhe->bkhe", attn_probs.astype(jnp.bfloat16), grad_context)
    grad_probs = product("bqhe,bkhe->bhqk", grad_context, value_rows)
    grad_scores = (
        attn_probs * (grad_probs - jnp.sum(grad_probs * attn_probs, axis=-1, keepdims=True))
    ).astype(jnp.bfloat16)
    grad_queries = product("bhqk,bkhe->bqhe", grad_scores, key_rows) * HD ** (-0.5)
    grad_keys = product("bhqk,bqhe->bkhe", grad_scores, queries) * HD ** (-0.5)
    grad_queries = grad_queries.reshape(groups, length, features)
    grad_values = grad_values.reshape(groups, length, features)
    grad_mixed = jnp.concatenate(
        [grad_queries, grad_keys.reshape(groups, length, features), grad_values], axis=-1
    )
    mixed_low = grad_mixed.astype(jnp.bfloat16)
    grad_attn = product("bld,ble->de", tokens, mixed_low)
    grad_tokens = grad_res + product("ble,de->bld", mixed_low, attn_weight)
    grad_biases = jnp.stack(
        [
            jnp.sum(grad_queries, axis=(0, 1)),
            jnp.sum(grad_values, axis=(0, 1)),
            jnp.sum(grad_res, axis=(0, 1)),
            jnp.sum(grad_first, axis=(0, 1)),
            jnp.sum(grad_mid, axis=(0, 1)),
            jnp.sum(grad_second, axis=(0, 1)),
        ]
    )
    grad_gains = jnp.stack(
        [
            jnp.sum(grad_first * normed_one, axis=(0, 1)),
            jnp.sum(grad_second * normed_two, axis=(0, 1)),
        ]
    )
    grad_unit = jnp.sum(grad_inner, axis=(0, 1))
    grad_student_biases = jnp.stack([jnp.sum(grad_proj, axis=(0, 1)), grad_dense_bias])
    layer_terms = (grad_attn, grad_merge, grad_up, grad_down, grad_biases, grad_gains, grad_unit)
    student_terms = (
        grad_proj_weight,
        grad_pool,
        grad_dense,
        grad_label,
        grad_student_biases,
        grad_logit_bias,
    )
    return (grad_tokens, layer_terms, student_terms)


BOTH = ("batch", "zero")


def swapped(pair, straight):
    return jnp.where(straight, pair[0], pair[1]), jnp.where(straight, pair[1], pair[0])


def shifted(block, distance):
    return passed_along(block, "batch", distance)


def by_steps(far, other, steps, sign):
    for step in steps:
        moved = shifted(far, sign * step)
        far = jnp.where(other // step % 2 == 1, moved, far)
    return far


def routing(routes, slot_count):
    batch_count, zero_count = lax.axis_size("batch"), lax.axis_size("zero")
    offsets = routes // (slot_count * zero_count) - lax.axis_index("batch")
    offsets = (offsets + batch_count) % batch_count
    one_back = offsets[0] == batch_count - 1
    lands_first = routes[0] % slot_count == 0
    return one_back, lands_first, jnp.where(one_back, offsets[1], offsets[0])


def on_device_linked(
    inputs, lengths, exits, routes, attn_weight, merge_weight, up_weight, down_weight,
    layer_biases, norm_gains, unit_bias, proj_weight, pool_weight, dense_weight,
    label_weight, student_biases, logit_bias, grad_act, grad_logits,
):
    slot_count, length, features = inputs.shape
    rows = slot_count * length
    tokens = inputs.reshape(rows, features)
    (
        mixed, context, totals, attn_all, merge_all, up_all, down_all, vectors, units,
        normed_one, inverse_one, first_low, active, slope, normed_two, inverse_two, leaving,
        grad_leaving,
    ) = forward_layer(
        lengths,
        exits,
        routes,
        tokens,
        attn_weight, merge_weight, up_weight, down_weight, layer_biases, norm_gains, unit_bias,
        grad_act,
    )
    grad_leaving = grad_leaving.reshape(rows, features)
    (
        logits, pack, *moving, mid_low, inner_low, res, res_low, grad_context
    ) = rows_backward(
        lengths,
        exits,
        routes,
        leaving,
        (proj_weight, pool_weight, dense_weight, label_weight, student_biases, logit_bias),
        grad_logits,
        (
            merge_all.reshape(2, features, -1),
            up_all.reshape(2, features, -1),
            down_all.reshape(-1, features),
        ),
        vectors,
        grad_leaving,
        (normed_one, inverse_one, normed_two, inverse_two, slope),
    )
    shards = [w.shape for w in (attn_weight, merge_weight, up_weight, down_weight)]
    (
        grad_tokens, attn_grad, merge_grad, up_grad, down_grad, small, late, arrived
    ) = close_backward(
        lengths, exits, routes, totals, pack, mixed, grad_context, tokens, attn_all, res, active, inner_low,
        mid_low, first_low, context, res_low, *moving, shards,
    )
    (
        arrived, logits, grad_tokens, attn_grad, merge_grad, up_grad, down_grad, bias_grad,
        gain_grad, unit_grad, proj_grad, pool_grad, dense_grad, label_grad, student_grad,
        logit_grad,
    ) = hand_over(
        small, late, logits, (attn_grad, merge_grad, up_grad, down_grad), grad_tokens,
        arrived.reshape(rows, features), slot_count, label_weight.shape[1], layer_biases.shape[1],
    )
    return (
        arrived.reshape(inputs.shape), logits, grad_tokens.reshape(inputs.shape), attn_grad, merge_grad, up_grad,
        down_grad, bias_grad, gain_grad, unit_grad.reshape(-1), proj_grad, pool_grad, dense_grad,
        label_grad.T, student_grad, logit_grad.reshape(-1),
    )


def whole_gather(attn, merge, up, down, biases, gains, unit):
    return (
        lax.all_gather(attn, BOTH, axis=0, tiled=True),
        lax.all_gather(merge, BOTH, axis=0, tiled=True),
        lax.all_gather(up, BOTH, axis=0, tiled=True),
        lax.all_gather(down, BOTH, axis=0, tiled=True),
        lax.all_gather(biases, BOTH, axis=1, tiled=True).astype(f32),
        lax.all_gather(gains, BOTH, axis=1, tiled=True).astype(f32),
        lax.all_gather(unit, BOTH, axis=0, tiled=True).astype(f32),
    )


def on_device(
    inputs, lengths, exits, routes, attn_weight, merge_weight, up_weight, down_weight,
    layer_biases, norm_gains, unit_bias, proj_weight, pool_weight, dense_weight,
    label_weight, student_biases, logit_bias, grad_act, grad_logits,
):
    slot_count, length, features = inputs.shape
    section_count = (lax.axis_size("batch") - 1).bit_length()
    steps = [1 << level for level in range(section_count)]
    student = (proj_weight, pool_weight, dense_weight, label_weight, student_biases, logit_bias)
    sent = exits > LAYER
    one_back, lands_first, other = routing(routes, slot_count)
    near, far = swapped(swapped(grad_act, lands_first), one_back)
    near, far = shifted(near, 1), by_steps(far, other, steps, -1)
    grad_leaving = jnp.stack(swapped((near, far), one_back)).astype(f32)
    grad_leaving = jnp.where(sent[:, None, None], grad_leaving, 0.0)
    weights = whole_gather(
        attn_weight, merge_weight, up_weight, down_weight, layer_biases, norm_gains, unit_bias
    )
    valid_all = jnp.arange(length)[None, :] < lengths[:, None]
    leaving, logits, saved_state = layer_forward(inputs, valid_all, weights, student)
    pieces = jnp.where(sent[:, None, None], leaving, jnp.zeros_like(leaving))
    near, far = swapped(pieces, one_back)
    near, far = shifted(near, -1), by_steps(far, other, steps, 1)
    arrived = jnp.stack(swapped(swapped((near, far), one_back), lands_first))
    grad_tokens, layer_sum, student_sum = layer_backward(
        saved_state, grad_leaving, grad_logits, weights, proj_weight
    )
    layer_grads = [
        lax.psum_scatter(term, BOTH, scatter_dimension=int(k in (4, 5)), tiled=True)
        for k, term in enumerate(layer_sum)
    ]
    student_grads = lax.psum(student_sum, BOTH)
    return (arrived, logits, grad_tokens, *layer_grads, *student_grads)


def solution(mesh):
    in_specs = (
        P(("batch", "zero"), None, None),
        P(("batch", "zero")),
        P(("batch", "zero")),
        P(("batch", "zero")),
        P(("batch", "zero"), None),
        P(("batch", "zero"), None),
        P(("batch", "zero"), None),
        P(("batch", "zero"), None),
        P(None, ("batch", "zero")),
        P(None, ("batch", "zero")),
        P(("batch", "zero")),
        P(),
        P(),
        P(),
        P(),
        P(),
        P(),
        P(("batch", "zero"), None, None),
        P(("batch", "zero"), None),
    )
    out_specs = (
        P(("batch", "zero"), None, None),
        P(("batch", "zero"), None),
        P(("batch", "zero"), None, None),
        P(("batch", "zero"), None),
        P(("batch", "zero"), None),
        P(("batch", "zero"), None),
        P(("batch", "zero"), None),
        P(None, ("batch", "zero")),
        P(None, ("batch", "zero")),
        P(("batch", "zero")),
        P(),
        P(),
        P(),
        P(),
        P(),
        P(),
    )
    linked = (mesh.shape["batch"], mesh.shape["zero"]) == (8, 4)
    return jax.shard_map(
        on_device_linked if linked else on_device, mesh=mesh, in_specs=in_specs, out_specs=out_specs, check_vma=False
    )
```
